32 devices in a mesh: pair: 4 (over y, x), aux: 8 (over z, core).
Axes of the slice: x: 2, y: 2, z: 4, core: 2. Of those that a mesh axis runs over, the one named last changes fastest.
Arguments:
- integrals: bfloat16 [128, 49152], P('pair', 'aux'), may hold values from -6 to 6
- block_mask: int32 [2, 768], P(None, 'aux'), may hold values 0 or 1
- block_atom: int32 [2], replicated, may hold values from 0 to 15
- green_occ: bfloat16 [2, 16, 64, 64], replicated, may hold values from -0.75 to 0.75
- green_virt: bfloat16 [2, 16, 64, 64], replicated, may hold values from -0.75 to 0.75
- time_weights: float32 [2], replicated, may hold values from 0.3 to 3
Outputs:
- polarizability: float32 [2, 768, 768], P(None, 'aux', 'pair')
- energy: float32 [], replicated
The draws below stay inside these ranges and needn't reach their ends.
All inputs are finite; a program needn't handle non-finite values. No bound on the sum of `block_mask` on one device may be relied on, other than what follows from the above.
Results may differ from the reference program's by a relative error of at most 0.004.
Values may be sent and summed in bfloat16 or wider, within the bound.
No kernel may reach another device: no remote copies, remote signals or barrier semaphores. Data moves between devices by JAX's collectives and lax.ppermute only.
A program may use at most 192 MiB of HBM per device.

```python
import math
import jax
import jax.numpy as jnp

BLK = 64
NT = 2
NATOM = 16
NROWS = 128
NAUX = 768
NBLK = 2


def touch_ends(entries, rng, least, largest):
    spot = [jax.random.randint(jax.random.fold_in(rng, axis), (), 0, length) for axis, length in enumerate(entries.shape)]
    widest = entries.shape.index(max(entries.shape))
    next_to = spot[:widest] + [(spot[widest] + 1) % entries.shape[widest]] + spot[widest + 1:]
    return entries.at[tuple(spot)].set(least).at[tuple(next_to)].set(largest)


def shard_levels(own_key, dims, pieces, least, top_value):
    def one(position, blocks):
        draws = jax.random.uniform(jax.random.fold_in(jax.random.fold_in(own_key, 6), position), (blocks,), jnp.float32, least / len(pieces), top_value / len(pieces))
        return jnp.repeat(jnp.exp(draws), dims[position] // blocks).reshape((-1,) + (1,) * (len(dims) - position - 1))

    level = one(*pieces[0])
    for cut in pieces[1:]:
        level = level * one(*cut)
    return level


def centred(rng, dims, spread, limit, shards=(), dtype=jnp.bfloat16):
    gain = shard_levels(rng, dims, shards, -0.22, 0.18) if shards else 1.0
    drawn = jax.random.normal(rng, dims, jnp.float32) * spread * gain
    return jnp.minimum(jnp.maximum(drawn, -limit), limit).astype(dtype)


def setup_inputs(seed: int = 0) -> dict:
    keys = jax.random.split(jax.random.key(seed), 7)
    integrals = centred(keys[0], (NROWS, NAUX * BLK), 1.0, 6.0, ((0, 4), (1, 8)))
    block_mask = touch_ends((jax.random.randint(keys[1], (NBLK, NAUX), 0, 4) < 3).astype(jnp.int32), jax.random.fold_in(keys[1], 1), 0, 1)
    block_atom = jax.random.randint(keys[2], (NBLK,), 0, NATOM).astype(jnp.int32)
    green_occ = centred(keys[3], (NT, NATOM, BLK, BLK), BLK ** -0.5, 0.75)
    green_virt = centred(keys[4], (NT, NATOM, BLK, BLK), BLK ** -0.5, 0.75)
    time_weights = jnp.clip(jnp.exp(jax.random.uniform(keys[5], (NT,), jnp.float32, math.log(0.3), math.log(3.0))), 0.3, 3.0)
    return dict(integrals=integrals, block_mask=block_mask, block_atom=block_atom, green_occ=green_occ, green_virt=green_virt, time_weights=time_weights)


def reference(integrals, block_mask, block_atom, green_occ, green_virt, time_weights):
    three = integrals.reshape(NROWS, NAUX, BLK)
    row_mask = jnp.repeat(block_mask, BLK, axis=0)
    masked = jnp.where(row_mask[:, :, None] > 0, three, jnp.zeros_like(three)).astype(jnp.float32)
    row_atom = jnp.repeat(block_atom, BLK).astype(jnp.int32)
    occ_rows = green_occ[:, row_atom].astype(jnp.float32)
    virt_rows = green_virt[:, row_atom].astype(jnp.float32)
    scale = 1.0 / jnp.sqrt(jnp.float32(NROWS * BLK))
    tiles = []
    total = jnp.float32(0.0)
    for step in range(NT):
        occ_half = jnp.einsum('rpn,rnl->rpl', masked, occ_rows[step]).astype(jnp.bfloat16).astype(jnp.float32)
        virt_half = jnp.einsum('rpn,rnl->rpl', masked, virt_rows[step]).astype(jnp.bfloat16).astype(jnp.float32)
        chi = jnp.einsum('rpl,rql->pq', occ_half, virt_half) * scale
        tiles.append(chi)
        total = total + time_weights[step] * jnp.sum(chi * chi)
    energy = -total / jnp.float32(NAUX * NAUX)
    return (jnp.stack(tiles), energy)
```

```python
import functools
import jax
import jax.numpy as jnp
from jax import lax
from jax.experimental import pallas as pl
from jax.experimental.pallas import tpu as pltpu
from jax.sharding import PartitionSpec as P

BLK = 64
VMEM = pl.BlockSpec(memory_space=pltpu.VMEM)
SMEM = pl.BlockSpec(memory_space=pltpu.SMEM)
PARAMS = pltpu.CompilerParams(vmem_limit_bytes=40 * 1024 * 1024)
NT_DIMS = (((1,), (1,)), ((), ()))


def arrange_kernel(rows, aux, x_ref, mask_ref, y_ref, wide):
    groups = rows // 8
    block = lax.axis_index("pair") * rows // BLK
    low = lax.broadcasted_iota(jnp.int32, (8, 128), 1) < BLK
    for i in range(aux // 2):
        tile = x_ref[:, i * 128:(i + 1) * 128].astype(jnp.float32)
        keep0 = mask_ref[block, 2 * i] > 0
        keep1 = mask_ref[block, 2 * i + 1] > 0
        for g in range(0, groups, 2):
            first = tile[8 * g:8 * g + 8]
            second = tile[8 * g + 8:8 * g + 16]
            even = jnp.where(low, first, pltpu.roll(second, BLK, 1))
            odd = jnp.where(low, pltpu.roll(first, BLK, 1), second)
            even = jnp.where(keep0, even, 0.0)
            odd = jnp.where(keep1, odd, 0.0)
            half = g // 2
            wide[half, pl.ds(2 * i, 8, stride=aux), :] = even
            wide[half, pl.ds(2 * i + 1, 8, stride=aux), :] = odd
    for s in range(8):
        for half in range(groups // 2):
            y_ref[s, :, half * 128:(half + 1) * 128] = wide[half, s * aux:(s + 1) * aux, :].astype(y_ref.dtype)


def arrange(integrals, block_mask):
    rows, width = integrals.shape
    aux = width // BLK
    return pl.pallas_call(
        functools.partial(arrange_kernel, rows, aux),
        out_shape=jax.ShapeDtypeStruct((8, aux, rows // 8 * BLK), jnp.bfloat16),
        in_specs=[VMEM, SMEM],
        out_specs=VMEM,
        scratch_shapes=[pltpu.VMEM((rows // 16, 8 * aux, 128), jnp.float32)],
        compiler_params=PARAMS,
        name="arrange",
    )(integrals, block_mask)


def transform_kernel(nt, atom_ref, y_ref, occ_ref, virt_ref, z_ref):
    steps, aux, wide = y_ref.shape
    copies = wide // BLK
    same = (
        lax.broadcasted_iota(jnp.int32, (wide, wide), 0) // BLK
        == lax.broadcasted_iota(jnp.int32, (wide, wide), 1) // BLK
    )
    y = y_ref[...].reshape(steps * aux, wide)
    for t in range(nt):
        occ = jnp.concatenate([occ_ref[t, 0]] * copies, axis=0)
        virt = jnp.concatenate([virt_ref[t, 0]] * copies, axis=0)
        both = lax.dot_general(occ, virt, NT_DIMS, preferred_element_type=jnp.float32)
        both = jnp.where(same, both, 0.0)
        high = both.astype(jnp.bfloat16)
        rest = (both - high.astype(jnp.float32)).astype(jnp.bfloat16)
        z = jnp.dot(y, high, preferred_element_type=jnp.float32)
        z += jnp.dot(y, rest, preferred_element_type=jnp.float32)
        z = z.astype(jnp.bfloat16)
        for s in range(steps):
            z_ref[s, t * aux:(t + 1) * aux, :] = z[s * aux:(s + 1) * aux]


def transform(atom, y, green_occ, green_virt):
    nt = green_occ.shape[0]
    steps, aux, wide = y.shape
    green = pl.BlockSpec((nt, 1, BLK, BLK), lambda i, atom: (0, atom[0], 0, 0))
    return pl.pallas_call(
        functools.partial(transform_kernel, nt),
        out_shape=jax.ShapeDtypeStruct((steps, nt * aux, wide), jnp.bfloat16),
        grid_spec=pltpu.PrefetchScalarGridSpec(
            num_scalar_prefetch=1,
            grid=(1,),
            in_specs=[pl.BlockSpec((steps, aux, wide), lambda i, atom: (0, 0, 0)), green, green],
            out_specs=pl.BlockSpec((steps, nt * aux, wide), lambda i, atom: (0, 0, 0)),
        ),
        compiler_params=PARAMS,
        name="transform",
    )(atom, y, green_occ, green_virt)


def products(z_ref, first_ref, second_ref):
    total = None
    for s in range(z_ref.shape[0]):
        partner = jnp.concatenate([first_ref[s], second_ref[s]], axis=0)
        term = lax.dot_general(z_ref[s], partner, NT_DIMS, preferred_element_type=jnp.float32)
        total = term if total is None else total + term
    return total


def chunk_kernel(z_ref, mine_ref, other_ref, out_ref):
    odd = lax.rem(lax.axis_index("aux"), 2)

    @pl.when(odd == 0)
    def _():
        out_ref[...] = products(z_ref, mine_ref, other_ref)

    @pl.when(odd == 1)
    def _():
        out_ref[...] = products(z_ref, other_ref, mine_ref)


def chunk(z, mine, other):
    return pl.pallas_call(
        chunk_kernel,
        out_shape=jax.ShapeDtypeStruct((z.shape[1], 2 * mine.shape[1]), jnp.float32),
        in_specs=[VMEM] * 3,
        out_specs=VMEM,
        compiler_params=PARAMS,
        name="chunk",
    )(z, mine, other)


def finish_kernel(scale, count, nt, weight_ref, *refs):
    parts, (chi_ref, sum_ref) = refs[:count], refs[count:]
    aux = chi_ref.shape[1]
    total = parts[0][...]
    for part in parts[1:]:
        total += part[...].astype(jnp.float32)
    total *= scale
    local = jnp.zeros((1, 1), jnp.float32)
    for t in range(nt):
        chi = total[t * aux:(t + 1) * aux]
        chi_ref[t] = chi
        local += weight_ref[t] * jnp.sum(chi * chi, keepdims=True)
    sum_ref[...] = jnp.broadcast_to(local, sum_ref.shape)


def finish(scale, time_weights, parts, replicas):
    nt = time_weights.shape[0]
    height, width = parts[0].shape
    return pl.pallas_call(
        functools.partial(finish_kernel, scale, len(parts), nt),
        out_shape=(
            jax.ShapeDtypeStruct((nt, height // nt, width), jnp.float32),
            jax.ShapeDtypeStruct((replicas, 128), jnp.float32),
        ),
        in_specs=[SMEM] + [VMEM] * len(parts),
        out_specs=(VMEM, VMEM),
        compiler_params=PARAMS,
        name="finish",
    )(time_weights, *parts)


def per_device(integrals, block_mask, block_atom, green_occ, green_virt, time_weights):
    rows = integrals.shape[0]
    aux_here = integrals.shape[1] // BLK
    pairs, auxes = lax.axis_size("pair"), lax.axis_size("aux")
    pair, aux = lax.axis_index("pair"), lax.axis_index("aux")
    chips = auxes // 2
    aux_total = aux_here * auxes
    columns = aux_total // pairs
    nt = green_occ.shape[0]

    sibling = [(i, i ^ 1) for i in range(auxes)]
    onward = [(i, (i + 2) % auxes) for i in range(auxes)]
    y = arrange(integrals, block_mask)
    atom = lax.dynamic_slice(block_atom, (pair * rows // BLK,), (1,))
    z = transform(atom, y, green_occ, green_virt)
    mine = y
    chunks = []
    for step in range(chips):
        other = lax.ppermute(mine, "aux", sibling)
        following = lax.ppermute(mine, "aux", onward) if step < chips - 1 else None
        chunks.append(chunk(z, mine, other))
        mine = following
    stacked = jnp.stack(chunks)
    order = (aux // 2 - jnp.arange(chips)) % chips
    whole = stacked[order]
    whole = whole.transpose(1, 0, 2).reshape(nt * aux_here, aux_total)
    parts = [lax.dynamic_slice(whole, (0, pair * columns), (nt * aux_here, columns))]
    for j in range(1, pairs):
        towards = [(i, (i + j) % pairs) for i in range(pairs)]
        target = (pair + j) % pairs
        piece = lax.dynamic_slice(whole, (0, target * columns), (nt * aux_here, columns))
        parts.append(lax.ppermute(piece.astype(jnp.bfloat16), "pair", towards))
    scale = float((rows * pairs * BLK) ** -0.5)
    chi, sums = finish(scale, time_weights, parts, pairs * auxes)
    everyone = lax.all_to_all(sums, ("pair", "aux"), 0, 0, tiled=True)
    energy = -jnp.sum(everyone[:, 0]) / jnp.float32(aux_total * aux_total)
    return chi, energy


def solution(mesh):
    placed = (P("pair", "aux"), P(None, "aux"), P(), P(), P(), P())
    return jax.shard_map(
        per_device,
        mesh=mesh,
        in_specs=placed,
        out_specs=(P(None, "aux", "pair"), P()),
        check_vma=False,
    )
```

```python
import functools
import jax
import jax.numpy as jnp
from jax import lax
from jax.experimental import pallas as pl
from jax.experimental.pallas import tpu as pltpu
from jax.sharding import PartitionSpec as P

BLK = 64
VMEM = pl.BlockSpec(memory_space=pltpu.VMEM)
SMEM = pl.BlockSpec(memory_space=pltpu.SMEM)
ANY = pl.BlockSpec(memory_space=pl.ANY)
NT_DIMS = (((1,), (1,)), ((), ()))


def call(kernel, name, flops, **settings):
    return pl.pallas_call(
        kernel,
        name=name,
        compiler_params=pltpu.CompilerParams(vmem_limit_bytes=40 * 1024 * 1024),
        cost_estimate=pl.CostEstimate(flops=flops, bytes_accessed=1 << 20, transcendentals=0),
        **settings,
    )


def chip_of():
    return lax.axis_index("aux") // 2


def early(chips, chip):
    return (chip < chips // 2).astype(jnp.int32)


def arrange_kernel(rows, aux, chips, second, x_ref, mask_ref, y_ref, x, wide, arrived):
    half = early(chips, chip_of())
    half = 1 - half if second else half
    start = pl.multiple_of(half * (rows // 2), rows // 2)
    copy = pltpu.make_async_copy(x_ref.at[pl.ds(start, rows // 2)], x, arrived)
    copy.start()
    block = lax.axis_index("pair") * rows // BLK
    low = lax.broadcasted_iota(jnp.int32, (8, 128), 1) < BLK
    copy.wait()
    for i in range(aux // 2):
        tile = x[:, i * 128:(i + 1) * 128].astype(jnp.float32)
        first, last = tile[:8], tile[8:]
        even = jnp.where(low, first, pltpu.roll(last, BLK, 1))
        odd = jnp.where(low, pltpu.roll(first, BLK, 1), last)
        even = jnp.where(mask_ref[block, 2 * i] > 0, even, 0.0)
        odd = jnp.where(mask_ref[block, 2 * i + 1] > 0, odd, 0.0)
        wide[pl.ds(2 * i, 8, stride=aux), :] = even
        wide[pl.ds(2 * i + 1, 8, stride=aux), :] = odd
    for s in range(8):
        lane = s % 2 * 128
        y_ref[s // 2, :, lane:lane + 128] = wide[s * aux:(s + 1) * aux, :].astype(y_ref.dtype)


def arrange(integrals, block_mask, chips, second):
    rows, width = integrals.shape
    aux = width // BLK
    return call(
        functools.partial(arrange_kernel, rows, aux, chips, second),
        "arrange",
        1 << 28,
        out_shape=jax.ShapeDtypeStruct((4, aux, 256), jnp.bfloat16),
        in_specs=[ANY, SMEM],
        out_specs=VMEM,
        scratch_shapes=[
            pltpu.VMEM((rows // 2, width), jnp.bfloat16),
            pltpu.VMEM((8 * aux, 128), jnp.float32),
            pltpu.SemaphoreType.DMA,
        ],
    )(integrals, block_mask)


def transform_kernel(nt, rows, atom_ref, occ_hbm, virt_hbm, y1, y2, o1, o2, z_ref, w_ref, occ_ref, virt_ref, arrived):
    steps, aux, wide = y1.shape
    copies = wide // BLK
    atom = atom_ref[lax.axis_index("pair") * rows // BLK]
    fetch = [
        pltpu.make_async_copy(occ_hbm.at[:, atom], occ_ref, arrived.at[0]),
        pltpu.make_async_copy(virt_hbm.at[:, atom], virt_ref, arrived.at[1]),
    ]
    for copy in fetch:
        copy.start()
    for copy in fetch:
        copy.wait()
    core = lax.rem(lax.axis_index("aux"), 2)
    same = (
        lax.broadcasted_iota(jnp.int32, (wide, wide), 0) // BLK
        == lax.broadcasted_iota(jnp.int32, (wide, wide), 1) // BLK
    )

    def diagonal(block):
        tall = jnp.concatenate([block.astype(jnp.float32)] * copies, axis=0)
        full = jnp.concatenate([tall] * copies, axis=1)
        return jnp.where(same, full, 0.0).astype(jnp.bfloat16)

    def through(y, first, second):
        half = jnp.dot(y, first, preferred_element_type=jnp.float32).astype(jnp.bfloat16)
        return lax.dot_general(half, second, NT_DIMS, preferred_element_type=jnp.float32).astype(jnp.bfloat16)

    for t in range(nt):
        occ, virt = diagonal(occ_ref[t]), diagonal(virt_ref[t])
        for half, (mine, other) in enumerate(((y1, o1), (y2, o2))):
            mine = mine[...].reshape(steps * aux, wide)
            other = other[...].reshape(steps * aux, wide)
            z = through(mine, occ, virt).reshape(steps, aux, wide)
            z_ref[half, :, t * aux:(t + 1) * aux, :] = z
            own = through(mine, virt, occ).reshape(steps, aux, wide)
            w_ref[half, t, :, pl.ds(pl.multiple_of(core * aux, aux), aux), :] = own
            sib = through(other, virt, occ).reshape(steps, aux, wide)
            w_ref[half, t, :, pl.ds(pl.multiple_of((1 - core) * aux, aux), aux), :] = sib


def transform(atom, green_occ, green_virt, rows, mine, other):
    nt = green_occ.shape[0]
    steps, aux, wide = mine[0].shape
    return call(
        functools.partial(transform_kernel, nt, rows),
        "transform",
        3 << 30,
        out_shape=(
            jax.ShapeDtypeStruct((2, steps, nt * aux, wide), jnp.bfloat16),
            jax.ShapeDtypeStruct((2, nt, steps, 2 * aux, wide), jnp.bfloat16),
        ),
        in_specs=[SMEM, ANY, ANY] + [VMEM] * 4,
        out_specs=(VMEM, VMEM),
        scratch_shapes=[
            pltpu.VMEM((nt, BLK, BLK), jnp.bfloat16),
            pltpu.VMEM((nt, BLK, BLK), jnp.bfloat16),
            pltpu.SemaphoreType.DMA((2,)),
        ],
    )(atom, green_occ, green_virt, *mine, *other)


def matching(chips, step, piece):
    chip = chip_of()
    source = lax.rem(chip + chips - step, chips)
    swap = early(chips, chip) != early(chips, source)
    return jnp.where(swap, 1 - piece, piece)


def near_kernel(chips, step, count, z_ref, *refs):
    mine, other, out_ref = refs[:count], refs[count:2 * count], refs[2 * count]
    halves = [matching(chips, step, piece) for piece in range(count)]

    def products(low, high):
        total = jnp.zeros(out_ref.shape, jnp.float32)
        for half, first, second in zip(halves, low, high):
            for j in range(z_ref.shape[1]):
                partner = jnp.concatenate([first[j], second[j]], axis=0)
                total += lax.dot_general(z_ref[half, j], partner, NT_DIMS, preferred_element_type=jnp.float32)
        out_ref[...] = total

    core = lax.rem(lax.axis_index("aux"), 2)
    pl.when(core == 0)(lambda: products(mine, other))
    pl.when(core == 1)(lambda: products(other, mine))


def near(z, chips, step, mine, other):
    size = z.shape[2]
    return call(
        functools.partial(near_kernel, chips, step, len(mine)),
        "near",
        1 << 30,
        out_shape=jax.ShapeDtypeStruct((size, 2 * mine[0].shape[1]), jnp.float32),
        in_specs=[VMEM] * (1 + 2 * len(mine)),
        out_specs=VMEM,
    )(z, *mine, *other)


def far_kernel(chips, step, count, w_ref, *refs):
    mine, out_ref = refs[:count], refs[count]
    nt, steps = w_ref.shape[1:3]
    aux = mine[0].shape[1]
    halves = [matching(chips, step, piece) for piece in range(count)]
    for t in range(nt):
        total = jnp.zeros((aux, out_ref.shape[1]), jnp.float32)
        for half, piece in zip(halves, mine):
            for j in range(steps):
                total += lax.dot_general(piece[j], w_ref[half, t, j], NT_DIMS, preferred_element_type=jnp.float32)
        out_ref[t * aux:(t + 1) * aux, :] = total.astype(out_ref.dtype)


def far(w, chips, step, mine):
    aux = mine[0].shape[1]
    return call(
        functools.partial(far_kernel, chips, step, len(mine)),
        "far",
        1 << 30,
        out_shape=jax.ShapeDtypeStruct((w.shape[1] * aux, w.shape[3]), jnp.bfloat16),
        in_specs=[VMEM] * (1 + len(mine)),
        out_specs=VMEM,
    )(w, *mine)


def pack_kernel(chips, *refs):
    backs, aheads, out_ref = refs[:chips // 2 + 1], refs[chips // 2 + 1:chips + 1], refs[chips + 1]
    chip = chip_of()
    for step in range(chips // 2):
        out_ref[lax.rem(chip + chips - step, chips)] = backs[step][...].astype(out_ref.dtype)
    for step in range(1, chips // 2):
        out_ref[lax.rem(chip + step, chips)] = aheads[step - 1][...]
    opposite = backs[-1][...] + aheads[-1][...].astype(jnp.float32)
    out_ref[lax.rem(chip + chips // 2, chips)] = opposite.astype(out_ref.dtype)


def pack(chips, backs, aheads):
    return call(
        functools.partial(pack_kernel, chips),
        "pack",
        1 << 28,
        out_shape=jax.ShapeDtypeStruct((chips,) + backs[0].shape, jnp.bfloat16),
        in_specs=[VMEM] * (chips + 1),
        out_specs=VMEM,
    )(*backs, *aheads)


def finish_kernel(scale, nt, weight_ref, part_ref, chi_ref, sum_ref):
    aux = chi_ref.shape[1]
    total = part_ref[0].astype(jnp.float32)
    for p in range(1, part_ref.shape[0]):
        total += part_ref[p].astype(jnp.float32)
    total *= scale
    local = jnp.zeros((1, 1), jnp.float32)
    for t in range(nt):
        chi = total[t * aux:(t + 1) * aux]
        chi_ref[t] = chi
        local += weight_ref[t] * jnp.sum(chi * chi, keepdims=True)
    sum_ref[...] = jnp.broadcast_to(local, sum_ref.shape)


def finish(scale, time_weights, parts, copies):
    nt = time_weights.shape[0]
    _, height, width = parts.shape
    return call(
        functools.partial(finish_kernel, scale, nt),
        "finish",
        1 << 28,
        out_shape=(
            jax.ShapeDtypeStruct((nt, height // nt, width), jnp.float32),
            jax.ShapeDtypeStruct((copies, 128), jnp.float32),
        ),
        in_specs=[SMEM, VMEM],
        out_specs=(VMEM, VMEM),
    )(time_weights, parts)


def per_device(integrals, block_mask, block_atom, green_occ, green_virt, time_weights):
    rows = integrals.shape[0]
    aux_here = integrals.shape[1] // BLK
    pairs, auxes = lax.axis_size("pair"), lax.axis_size("aux")
    chips = auxes // 2
    aux_total = aux_here * auxes
    columns = aux_total // pairs
    nt = green_occ.shape[0]

    def along(shift):
        return [(i, (i + 2 * shift) % auxes) for i in range(auxes)]

    def to_sibling(arrays):
        pairing = [(i, i ^ 1) for i in range(auxes)]
        return [lax.ppermute(a, "aux", pairing) for a in arrays]

    own = [arrange(integrals, block_mask, chips, second) for second in (False, True)]
    held = [own]
    for step in range(1, chips // 2 + 1):
        sent = held[-1] if step < chips // 2 else held[-1][:1]
        held.append([lax.ppermute(a, "aux", along(1)) for a in sent])
    others = [to_sibling(pieces) for pieces in held]
    z, w = transform(block_atom, green_occ, green_virt, rows, own, others[0])
    aheads = []
    for step in range(1, chips // 2 + 1):
        share = far(w, chips, step, held[step])
        aheads.append(lax.ppermute(share, "aux", along(-step)))
    backs = [near(z, chips, step, held[step], others[step]) for step in range(chips // 2 + 1)]
    parts = pack(chips, backs, aheads)
    if columns != 2 * aux_here:
        parts = parts.transpose(1, 0, 2).reshape(nt * aux_here, pairs, columns).transpose(1, 0, 2)
    parts = lax.all_to_all(parts, "pair", 0, 0)
    scale = float((rows * pairs * BLK) ** -0.5)
    chi, sums = finish(scale, time_weights, parts, auxes)
    level = jnp.sum(lax.all_to_all(sums, "aux", 0, 0, tiled=True), axis=0, keepdims=True)
    level = lax.all_to_all(jnp.broadcast_to(level, (pairs, 128)), "pair", 0, 0, tiled=True)
    energy = -jnp.sum(level[:, 0]) / jnp.float32(aux_total * aux_total)
    return chi, energy


def solution(mesh):
    placed = (P("pair", "aux"), P(None, "aux"), P(), P(), P(), P())
    return jax.shard_map(
        per_device,
        mesh=mesh,
        in_specs=placed,
        out_specs=(P(None, "aux", "pair"), P()),
        check_vma=False,
    )
```

```python
import functools
import jax
import jax.numpy as jnp
from jax import lax
from jax.experimental import pallas as pl
from jax.experimental.pallas import tpu as pltpu
from jax.sharding import PartitionSpec as P

BLK = 64
VMEM = pl.BlockSpec(memory_space=pltpu.VMEM)
SMEM = pl.BlockSpec(memory_space=pltpu.SMEM)
HBM = pl.BlockSpec(memory_space=pltpu.HBM)
NT_DIMS = (((1,), (1,)), ((), ()))


def call(kernel, name, flops, **settings):
    return pl.pallas_call(
        kernel,
        name=name,
        compiler_params=pltpu.CompilerParams(vmem_limit_bytes=40 * 1024 * 1024),
        cost_estimate=pl.CostEstimate(flops=flops // 16, bytes_accessed=1 << 10, transcendentals=0),
        **settings,
    )


def stay(array):
    return pltpu.with_memory_space_constraint(array, pltpu.HBM)


def chip_of():
    return lax.axis_index("aux") // 2


def early(chips, chip):
    return (chip < chips // 2).astype(jnp.int32)


def arrange_kernel(rows, aux, chips, second, x_hbm, mask_hbm, y_ref, x, mask, wide, arrived):
    half = early(chips, chip_of())
    half = 1 - half if second else half
    start = pl.multiple_of(half * (rows // 2), rows // 2)
    copies = [
        pltpu.make_async_copy(x_hbm.at[pl.ds(start, rows // 2)], x, arrived.at[0]),
        pltpu.make_async_copy(mask_hbm, mask, arrived.at[1]),
    ]
    for copy in copies:
        copy.start()
    block = lax.axis_index("pair") * rows // BLK
    low = lax.broadcasted_iota(jnp.int32, (8, 128), 1) < BLK
    for copy in copies:
        copy.wait()
    for i in range(aux // 2):
        tile = x[:, i * 128:(i + 1) * 128].astype(jnp.float32)
        first, last = tile[:8], tile[8:]
        even = jnp.where(low, first, pltpu.roll(last, BLK, 1))
        odd = jnp.where(low, pltpu.roll(first, BLK, 1), last)
        even = jnp.where(mask[block, 2 * i] > 0, even, 0.0)
        odd = jnp.where(mask[block, 2 * i + 1] > 0, odd, 0.0)
        wide[pl.ds(2 * i, 8, stride=aux), :] = even
        wide[pl.ds(2 * i + 1, 8, stride=aux), :] = odd
    for s in range(8):
        lane = s % 2 * 128
        y_ref[s // 2, :, lane:lane + 128] = wide[s * aux:(s + 1) * aux, :].astype(y_ref.dtype)


def arrange(integrals, block_mask, chips, second):
    rows, width = integrals.shape
    aux = width // BLK
    return call(
        functools.partial(arrange_kernel, rows, aux, chips, second),
        "arrange",
        1 << 28,
        out_shape=jax.ShapeDtypeStruct((4, aux, 256), jnp.bfloat16),
        in_specs=[HBM, HBM],
        out_specs=VMEM,
        scratch_shapes=[
            pltpu.VMEM((rows // 2, width), jnp.bfloat16),
            pltpu.SMEM(block_mask.shape, jnp.int32),
            pltpu.VMEM((8 * aux, 128), jnp.float32),
            pltpu.SemaphoreType.DMA((2,)),
        ],
    )(stay(integrals), stay(block_mask))


def transform_kernel(nt, rows, own, atom_hbm, occ_hbm, virt_hbm, *refs):
    parts, (w_ref, atom_ref, occ_ref, virt_ref, arrived) = refs[:-5], refs[-5:]
    pieces, z_ref = (parts[:2], parts[2]) if own else (parts[1:], None)
    steps, aux, wide = pieces[0].shape
    copies = wide // BLK
    copy = pltpu.make_async_copy(atom_hbm, atom_ref, arrived.at[0])
    copy.start()
    copy.wait()
    atom = atom_ref[lax.axis_index("pair") * rows // BLK]
    fetch = [
        pltpu.make_async_copy(occ_hbm.at[:, atom], occ_ref, arrived.at[0]),
        pltpu.make_async_copy(virt_hbm.at[:, atom], virt_ref, arrived.at[1]),
    ]
    for copy in fetch:
        copy.start()
    for copy in fetch:
        copy.wait()
    core = lax.rem(lax.axis_index("aux"), 2)
    core = core if own else 1 - core
    place = pl.ds(pl.multiple_of(core * aux, aux), aux)
    same = (
        lax.broadcasted_iota(jnp.int32, (wide, wide), 0) // BLK
        == lax.broadcasted_iota(jnp.int32, (wide, wide), 1) // BLK
    )

    def diagonal(block):
        tall = jnp.concatenate([block.astype(jnp.float32)] * copies, axis=0)
        full = jnp.concatenate([tall] * copies, axis=1)
        return jnp.where(same, full, 0.0).astype(jnp.bfloat16)

    def through(y, first, second):
        half = jnp.dot(y, first, preferred_element_type=jnp.float32).astype(jnp.bfloat16)
        full = lax.dot_general(half, second, NT_DIMS, preferred_element_type=jnp.float32)
        return full.astype(jnp.bfloat16).reshape(steps, aux, wide)

    for t in range(nt):
        occ, virt = diagonal(occ_ref[t]), diagonal(virt_ref[t])
        for half in range(2):
            y = pieces[half][...].reshape(steps * aux, wide)
            if own:
                z_ref[half, :, t * aux:(t + 1) * aux, :] = through(y, occ, virt)
            w_ref[half, t, :, place, :] = through(y, virt, occ)


def transform(atom, green_occ, green_virt, rows, pieces, before=None):
    nt = green_occ.shape[0]
    steps, aux, wide = pieces[0].shape
    own = before is None
    w_shape = jax.ShapeDtypeStruct((2, nt, steps, 2 * aux, wide), jnp.bfloat16)
    z_shape = jax.ShapeDtypeStruct((2, steps, nt * aux, wide), jnp.bfloat16)
    operands = (stay(atom), stay(green_occ), stay(green_virt), *(() if own else (before,)), *pieces)
    return call(
        functools.partial(transform_kernel, nt, rows, own),
        "transform",
        2 << 30,
        out_shape=(z_shape, w_shape) if own else w_shape,
        in_specs=[HBM] * 3 + [VMEM] * (len(operands) - 3),
        out_specs=(VMEM, VMEM) if own else VMEM,
        input_output_aliases={} if own else {3: 0},
        scratch_shapes=[
            pltpu.SMEM(atom.shape, jnp.int32),
            pltpu.VMEM((nt, BLK, BLK), jnp.bfloat16),
            pltpu.VMEM((nt, BLK, BLK), jnp.bfloat16),
            pltpu.SemaphoreType.DMA((2,)),
        ],
    )(*operands)


def matching(chips, step, piece):
    chip = chip_of()
    source = lax.rem(chip + chips - step, chips)
    swap = early(chips, chip) != early(chips, source)
    return jnp.where(swap, 1 - piece, piece)


def near_kernel(chips, step, count, z_ref, *refs):
    mine, other, out_ref = refs[:count], refs[count:2 * count], refs[-1]
    halves = [matching(chips, step, piece) for piece in range(count)]

    def products(low, high):
        total = jnp.zeros(out_ref.shape, jnp.float32)
        for half, first, second in zip(halves, low, high):
            for j in range(z_ref.shape[1]):
                partner = jnp.concatenate([first[j], second[j]], axis=0)
                total += lax.dot_general(z_ref[half, j], partner, NT_DIMS, preferred_element_type=jnp.float32)
        out_ref[...] = total

    core = lax.rem(lax.axis_index("aux"), 2)
    pl.when(core == 0)(lambda: products(mine, other))
    pl.when(core == 1)(lambda: products(other, mine))


def near(z, chips, step, mine, other):
    size = z.shape[2]
    return call(
        functools.partial(near_kernel, chips, step, len(mine)),
        "near",
        1 << 30,
        out_shape=jax.ShapeDtypeStruct((size, 2 * mine[0].shape[-2]), jnp.float32),
        in_specs=[VMEM] * (1 + 2 * len(mine)),
        out_specs=VMEM,
    )(z, *mine, *other)


def fold(x):
    high = x.shape[0] // 2
    past = jnp.concatenate([x[:high, 128:], x[high:, 128:]], axis=1)
    return jnp.concatenate([x[:, :128], past], axis=0)


def unfold(x):
    high = x.shape[0] // 3
    past = x[2 * high:]
    past = jnp.concatenate([past[:, :BLK], past[:, BLK:]], axis=0)
    return jnp.concatenate([x[:2 * high], past], axis=1)


def far_kernel(chips, step, count, w_ref, *refs):
    mine, out_ref = refs[:count], refs[count]
    nt, steps = w_ref.shape[1:3]
    aux = mine[0].shape[1]
    halves = [matching(chips, step, piece) for piece in range(count)]
    shares = []
    for t in range(nt):
        total = jnp.zeros((aux, w_ref.shape[3]), jnp.float32)
        for half, piece in zip(halves, mine):
            for j in range(steps):
                total += lax.dot_general(piece[j], w_ref[half, t, j], NT_DIMS, preferred_element_type=jnp.float32)
        shares.append(total)
    out_ref[...] = fold(jnp.concatenate(shares, axis=0)).astype(out_ref.dtype)


def far(w, chips, step, mine):
    aux = mine[0].shape[1]
    return call(
        functools.partial(far_kernel, chips, step, len(mine)),
        "far",
        1 << 30,
        out_shape=jax.ShapeDtypeStruct((w.shape[1] * aux * 3 // 2, 128), jnp.bfloat16),
        in_specs=[VMEM] * (1 + len(mine)),
        out_specs=VMEM,
    )(w, *mine)


def pack_kernel(chips, pairs, *refs):
    backs, aheads = refs[:chips // 2 + 1], refs[chips // 2 + 1:chips + 1]
    outs, shares = refs[chips + 1:-1], refs[-1]
    chip = chip_of()
    for step in range(chips // 2):
        shares[lax.rem(chip + chips - step, chips)] = fold(backs[step][...])
    for step in range(1, chips // 2):
        shares[lax.rem(chip + step, chips)] = aheads[step - 1][...].astype(jnp.float32)
    opposite = fold(backs[-1][...]) + aheads[-1][...].astype(jnp.float32)
    shares[lax.rem(chip + chips // 2, chips)] = opposite
    if pairs is None:
        for q in range(chips):
            outs[0][q] = unfold(shares[q]).astype(jnp.bfloat16)
    else:
        pair = lax.axis_index("pair")
        for j, out_ref in enumerate(outs):
            out_ref[...] = shares[lax.bitwise_xor(pair, j)].astype(out_ref.dtype)


def pack(chips, pairs, backs, aheads):
    height, width = backs[0].shape
    folded = (height * 3 // 2, 128)
    if pairs is None:
        out_shape = (jax.ShapeDtypeStruct((chips, height, width), jnp.bfloat16),)
    else:
        out_shape = (jax.ShapeDtypeStruct(folded, jnp.float32),)
        out_shape += (jax.ShapeDtypeStruct(folded, jnp.bfloat16),) * (pairs - 1)
    return call(
        functools.partial(pack_kernel, chips, pairs),
        "pack",
        1 << 28,
        out_shape=out_shape,
        in_specs=[VMEM] * (chips + 1),
        out_specs=(VMEM,) * len(out_shape),
        scratch_shapes=[pltpu.VMEM((chips,) + folded, jnp.float32)],
    )(*backs, *aheads)


def finish_kernel(scale, nt, folded, weight_ref, *refs):
    parts, (chi_ref, sum_ref) = refs[:-2], refs[-2:]
    aux = chi_ref.shape[1]
    if folded:
        total = parts[0][...]
        for part in parts[1:]:
            total += part[...].astype(jnp.float32)
        total = unfold(total * scale)
    else:
        total = parts[0][0].astype(jnp.float32)
        for p in range(1, parts[0].shape[0]):
            total += parts[0][p].astype(jnp.float32)
        total *= scale
    local = jnp.zeros((1, 1), jnp.float32)
    for t in range(nt):
        chi = total[t * aux:(t + 1) * aux]
        chi_ref[t] = chi
        local += weight_ref[t] * jnp.sum(chi * chi, keepdims=True)
    sum_ref[...] = jnp.broadcast_to(local, sum_ref.shape)


def finish(scale, time_weights, parts, chi_shape, copies):
    return call(
        functools.partial(finish_kernel, scale, chi_shape[0], len(parts) > 1),
        "finish",
        1 << 28,
        out_shape=(
            jax.ShapeDtypeStruct(chi_shape, jnp.float32),
            jax.ShapeDtypeStruct((copies, 128), jnp.float32),
        ),
        in_specs=[SMEM] + [VMEM] * len(parts),
        out_specs=(VMEM, VMEM),
    )(time_weights, *parts)


def per_device(integrals, block_mask, block_atom, green_occ, green_virt, time_weights):
    rows = integrals.shape[0]
    aux_here = integrals.shape[1] // BLK
    pairs, auxes = lax.axis_size("pair"), lax.axis_size("aux")
    chips = auxes // 2
    aux_total = aux_here * auxes
    columns = aux_total // pairs
    nt = green_occ.shape[0]

    def along(shift):
        return [(i, (i + 2 * shift) % auxes) for i in range(auxes)]

    def to_sibling(array):
        return lax.ppermute(array, "aux", [(i, i ^ 1) for i in range(auxes)])

    own = [arrange(integrals, block_mask, chips, second) for second in (False, True)]
    arriving = [lax.ppermute(a, "aux", along(1)) for a in own]
    z, w = transform(block_atom, green_occ, green_virt, rows, own)
    *later, z = lax.optimization_barrier((*own, z))
    arriving[0], z = lax.optimization_barrier((arriving[0], z))
    sibling = [to_sibling(a) for a in later]
    backs, aheads = [], []
    for step in range(1, chips // 2 + 1):
        held, last = arriving, step == chips // 2
        if not last:
            sent = held if step + 1 < chips // 2 else held[:1]
            arriving = [lax.ppermute(a, "aux", along(1)) for a in sent]
        other = [to_sibling(a) for a in held]
        if step == 1:
            w = transform(block_atom, green_occ, green_virt, rows, sibling, w)
        share = far(w, chips, step, held)
        aheads.append(lax.ppermute(share, "aux", along(-step)))
        if step == 1:
            backs.append(near(z, chips, 0, own, sibling))
        back = near(z, chips, step, held, other)
        if not last:
            arriving[0], share, back = lax.optimization_barrier((arriving[0], share, back))
        backs.append(back)
    if columns == 2 * aux_here and pairs & (pairs - 1) == 0:
        mine, *sends = pack(chips, pairs, backs, aheads)
        parts = [mine]
        for j in range(pairs - 1, 0, -1):
            parts.append(lax.ppermute(sends[j - 1], "pair", [(i, i ^ j) for i in range(pairs)]))
    else:
        (shares,) = pack(chips, None, backs, aheads)
        shares = shares.transpose(1, 0, 2).reshape(nt * aux_here, pairs, columns).transpose(1, 0, 2)
        parts = [lax.all_to_all(shares, "pair", 0, 0)]
    scale = float((rows * pairs * BLK) ** -0.5)
    chi, sums = finish(scale, time_weights, parts, (nt, aux_here, columns), pairs * auxes)
    everyone = lax.all_to_all(sums, ("pair", "aux"), 0, 0, tiled=True)
    energy = -jnp.sum(everyone[:, 0]) / jnp.float32(aux_total * aux_total)
    return chi, energy


def solution(mesh):
    placed = (P("pair", "aux"), P(None, "aux"), P(), P(), P(), P())
    return jax.shard_map(
        per_device,
        mesh=mesh,
        in_specs=placed,
        out_specs=(P(None, "aux", "pair"), P()),
        check_vma=False,
    )
```

```python
import functools
import jax
import jax.numpy as jnp
from jax import lax
from jax.experimental import pallas as pl
from jax.experimental.pallas import tpu as pltpu
from jax.sharding import PartitionSpec as P

BLK = 64
VMEM = pl.BlockSpec(memory_space=pltpu.VMEM)
SMEM = pl.BlockSpec(memory_space=pltpu.SMEM)
HBM = pl.BlockSpec(memory_space=pltpu.HBM)
NT_DIMS = (((1,), (1,)), ((), ()))


def call(kernel, name, flops, **settings):
    return pl.pallas_call(
        kernel,
        name=name,
        compiler_params=pltpu.CompilerParams(vmem_limit_bytes=40 * 1024 * 1024),
        cost_estimate=pl.CostEstimate(flops=flops, bytes_accessed=1 << 8, transcendentals=0),
        **settings,
    )


def stay(array):
    return pltpu.with_memory_space_constraint(array, pltpu.HBM)


def chip_of():
    return lax.axis_index("aux") // 2


def early(chips, chip):
    return (chip < chips // 2).astype(jnp.int32)


def arrange_kernel(rows, aux, chips, second, x_hbm, mask_hbm, y_ref, x, mask, wide, arrived):
    half = early(chips, chip_of())
    half = 1 - half if second else half
    start = pl.multiple_of(half * (rows // 2), rows // 2)
    copies = [
        pltpu.make_async_copy(x_hbm.at[pl.ds(start, rows // 2)], x, arrived.at[0]),
        pltpu.make_async_copy(mask_hbm, mask, arrived.at[1]),
    ]
    for copy in copies:
        copy.start()
    block = lax.axis_index("pair") * rows // BLK
    low = lax.broadcasted_iota(jnp.int32, (8, 128), 1) < BLK
    for copy in copies:
        copy.wait()
    for i in range(aux // 2):
        tile = x[:, i * 128:(i + 1) * 128].astype(jnp.float32)
        first, last = tile[:8], tile[8:]
        even = jnp.where(low, first, pltpu.roll(last, BLK, 1))
        odd = jnp.where(low, pltpu.roll(first, BLK, 1), last)
        even = jnp.where(mask[block, 2 * i] > 0, even, 0.0)
        odd = jnp.where(mask[block, 2 * i + 1] > 0, odd, 0.0)
        wide[pl.ds(2 * i, 8, stride=aux), :] = even
        wide[pl.ds(2 * i + 1, 8, stride=aux), :] = odd
    for s in range(8):
        lane = s % 2 * 128
        y_ref[s // 2, :, lane:lane + 128] = wide[s * aux:(s + 1) * aux, :].astype(y_ref.dtype)


def arrange(integrals, block_mask, chips, second):
    rows, width = integrals.shape
    aux = width // BLK
    return call(
        functools.partial(arrange_kernel, rows, aux, chips, second),
        "arrange",
        1 << 28,
        out_shape=jax.ShapeDtypeStruct((4, aux, 256), jnp.bfloat16),
        in_specs=[HBM, HBM],
        out_specs=VMEM,
        scratch_shapes=[
            pltpu.VMEM((rows // 2, width), jnp.bfloat16),
            pltpu.SMEM(block_mask.shape, jnp.int32),
            pltpu.VMEM((8 * aux, 128), jnp.float32),
            pltpu.SemaphoreType.DMA((2,)),
        ],
    )(stay(integrals), stay(block_mask))


def transform_kernel(nt, rows, own, atom_hbm, occ_hbm, virt_hbm, *refs):
    parts, (w_ref, atom_ref, occ_ref, virt_ref, arrived) = refs[:-5], refs[-5:]
    pieces, z_ref = (parts[:2], parts[2]) if own else (parts[1:], None)
    steps, aux, wide = pieces[0].shape
    copies = wide // BLK
    copy = pltpu.make_async_copy(atom_hbm, atom_ref, arrived.at[0])
    copy.start()
    copy.wait()
    atom = atom_ref[lax.axis_index("pair") * rows // BLK]
    fetch = [
        pltpu.make_async_copy(occ_hbm.at[:, atom], occ_ref, arrived.at[0]),
        pltpu.make_async_copy(virt_hbm.at[:, atom], virt_ref, arrived.at[1]),
    ]
    for copy in fetch:
        copy.start()
    for copy in fetch:
        copy.wait()
    core = lax.rem(lax.axis_index("aux"), 2)
    core = core if own else 1 - core
    place = pl.ds(pl.multiple_of(core * aux, aux), aux)
    same = (
        lax.broadcasted_iota(jnp.int32, (wide, wide), 0) // BLK
        == lax.broadcasted_iota(jnp.int32, (wide, wide), 1) // BLK
    )

    def diagonal(block):
        tall = jnp.concatenate([block.astype(jnp.float32)] * copies, axis=0)
        full = jnp.concatenate([tall] * copies, axis=1)
        return jnp.where(same, full, 0.0).astype(jnp.bfloat16)

    def through(y, first, second):
        half = jnp.dot(y, first, preferred_element_type=jnp.float32).astype(jnp.bfloat16)
        full = lax.dot_general(half, second, NT_DIMS, preferred_element_type=jnp.float32)
        return full.astype(jnp.bfloat16).reshape(steps, aux, wide)

    for t in range(nt):
        occ, virt = diagonal(occ_ref[t]), diagonal(virt_ref[t])
        for half in range(2):
            y = pieces[half][...].reshape(steps * aux, wide)
            if own:
                z_ref[half, :, t * aux:(t + 1) * aux, :] = through(y, occ, virt)
            w_ref[half, t, :, place, :] = through(y, virt, occ)


def transform(atom, green_occ, green_virt, rows, pieces, before=None):
    nt = green_occ.shape[0]
    steps, aux, wide = pieces[0].shape
    own = before is None
    w_shape = jax.ShapeDtypeStruct((2, nt, steps, 2 * aux, wide), jnp.bfloat16)
    z_shape = jax.ShapeDtypeStruct((2, steps, nt * aux, wide), jnp.bfloat16)
    operands = (stay(atom), stay(green_occ), stay(green_virt), *(() if own else (before,)), *pieces)
    return call(
        functools.partial(transform_kernel, nt, rows, own),
        "transform",
        2 << 30,
        out_shape=(z_shape, w_shape) if own else w_shape,
        in_specs=[HBM] * 3 + [VMEM] * (len(operands) - 3),
        out_specs=(VMEM, VMEM) if own else VMEM,
        input_output_aliases={} if own else {3: 0},
        scratch_shapes=[
            pltpu.SMEM(atom.shape, jnp.int32),
            pltpu.VMEM((nt, BLK, BLK), jnp.bfloat16),
            pltpu.VMEM((nt, BLK, BLK), jnp.bfloat16),
            pltpu.SemaphoreType.DMA((2,)),
        ],
    )(*operands)


def matching(chips, step, piece):
    chip = chip_of()
    source = lax.rem(chip + chips - step, chips)
    swap = early(chips, chip) != early(chips, source)
    return jnp.where(swap, 1 - piece, piece)


def near_kernel(chips, step, count, z_ref, *refs):
    mine, other, out_ref = refs[:count], refs[count:2 * count], refs[-1]
    halves = [matching(chips, step, piece) for piece in range(count)]

    def products(low, high):
        total = jnp.zeros(out_ref.shape, jnp.float32)
        for half, first, second in zip(halves, low, high):
            for j in range(z_ref.shape[1]):
                partner = jnp.concatenate([first[j], second[j]], axis=0)
                total += lax.dot_general(z_ref[half, j], partner, NT_DIMS, preferred_element_type=jnp.float32)
        out_ref[...] = total

    core = lax.rem(lax.axis_index("aux"), 2)
    pl.when(core == 0)(lambda: products(mine, other))
    pl.when(core == 1)(lambda: products(other, mine))


def near(z, chips, step, mine, other):
    size = z.shape[2]
    return call(
        functools.partial(near_kernel, chips, step, len(mine)),
        "near",
        1 << 30,
        out_shape=jax.ShapeDtypeStruct((size, 2 * mine[0].shape[-2]), jnp.float32),
        in_specs=[VMEM] * (1 + 2 * len(mine)),
        out_specs=VMEM,
    )(z, *mine, *other)


def fold(x):
    high = x.shape[0] // 2
    past = jnp.concatenate([x[:high, 128:], x[high:, 128:]], axis=1)
    return jnp.concatenate([x[:, :128], past], axis=0)


def unfold(x):
    high = x.shape[0] // 3
    past = x[2 * high:]
    past = jnp.concatenate([past[:, :BLK], past[:, BLK:]], axis=0)
    return jnp.concatenate([x[:2 * high], past], axis=1)


def far_kernel(chips, step, count, w_ref, *refs):
    mine, out_ref = refs[:count], refs[count]
    nt, steps = w_ref.shape[1:3]
    aux = mine[0].shape[1]
    halves = [matching(chips, step, piece) for piece in range(count)]
    shares = []
    for t in range(nt):
        total = jnp.zeros((aux, w_ref.shape[3]), jnp.float32)
        for half, piece in zip(halves, mine):
            for j in range(steps):
                total += lax.dot_general(piece[j], w_ref[half, t, j], NT_DIMS, preferred_element_type=jnp.float32)
        shares.append(total)
    out_ref[...] = fold(jnp.concatenate(shares, axis=0)).astype(out_ref.dtype)


def far(w, chips, step, mine):
    aux = mine[0].shape[1]
    return call(
        functools.partial(far_kernel, chips, step, len(mine)),
        "far",
        1 << 30,
        out_shape=jax.ShapeDtypeStruct((w.shape[1] * aux * 3 // 2, 128), jnp.bfloat16),
        in_specs=[VMEM] * (1 + len(mine)),
        out_specs=VMEM,
    )(w, *mine)


def pack_kernel(chips, pairs, *refs):
    backs, aheads = refs[:chips // 2 + 1], refs[chips // 2 + 1:chips + 1]
    outs, shares = refs[chips + 1:-1], refs[-1]
    chip = chip_of()
    for step in range(chips // 2):
        shares[lax.rem(chip + chips - step, chips)] = fold(backs[step][...])
    for step in range(1, chips // 2):
        shares[lax.rem(chip + step, chips)] = aheads[step - 1][...].astype(jnp.float32)
    opposite = fold(backs[-1][...]) + aheads[-1][...].astype(jnp.float32)
    shares[lax.rem(chip + chips // 2, chips)] = opposite
    if pairs is None:
        for q in range(chips):
            outs[0][q] = unfold(shares[q]).astype(jnp.bfloat16)
    else:
        pair = lax.axis_index("pair")
        for j, out_ref in enumerate(outs):
            out_ref[...] = shares[lax.bitwise_xor(pair, j)].astype(out_ref.dtype)


def pack(chips, pairs, backs, aheads):
    height, width = backs[0].shape
    folded = (height * 3 // 2, 128)
    if pairs is None:
        out_shape = (jax.ShapeDtypeStruct((chips, height, width), jnp.bfloat16),)
    else:
        out_shape = (jax.ShapeDtypeStruct(folded, jnp.float32),)
        out_shape += (jax.ShapeDtypeStruct(folded, jnp.bfloat16),) * (pairs - 1)
    return call(
        functools.partial(pack_kernel, chips, pairs),
        "pack",
        1 << 28,
        out_shape=out_shape,
        in_specs=[VMEM] * (chips + 1),
        out_specs=(VMEM,) * len(out_shape),
        scratch_shapes=[pltpu.VMEM((chips,) + folded, jnp.float32)],
    )(*backs, *aheads)


def finish_kernel(scale, nt, folded, weight_ref, *refs):
    parts, (chi_ref, sum_ref) = refs[:-2], refs[-2:]
    aux = chi_ref.shape[1]
    if folded:
        total = parts[0][...]
        for part in parts[1:]:
            total += part[...].astype(jnp.float32)
        total = unfold(total * scale)
    else:
        total = parts[0][0].astype(jnp.float32)
        for p in range(1, parts[0].shape[0]):
            total += parts[0][p].astype(jnp.float32)
        total *= scale
    local = jnp.zeros((1, 1), jnp.float32)
    for t in range(nt):
        chi = total[t * aux:(t + 1) * aux]
        chi_ref[t] = chi
        local += weight_ref[t] * jnp.sum(chi * chi, keepdims=True)
    sum_ref[...] = jnp.broadcast_to(local, sum_ref.shape)


def finish(scale, time_weights, parts, chi_shape, copies):
    return call(
        functools.partial(finish_kernel, scale, chi_shape[0], len(parts) > 1),
        "finish",
        1 << 28,
        out_shape=(
            jax.ShapeDtypeStruct(chi_shape, jnp.float32),
            jax.ShapeDtypeStruct((copies, 128), jnp.float32),
        ),
        in_specs=[SMEM] + [VMEM] * len(parts),
        out_specs=(VMEM, VMEM),
    )(time_weights, *parts)


def per_device(integrals, block_mask, block_atom, green_occ, green_virt, time_weights):
    rows = integrals.shape[0]
    aux_here = integrals.shape[1] // BLK
    pairs, auxes = lax.axis_size("pair"), lax.axis_size("aux")
    chips = auxes // 2
    aux_total = aux_here * auxes
    columns = aux_total // pairs
    nt = green_occ.shape[0]

    def along(shift):
        return [(i, (i + 2 * shift) % auxes) for i in range(auxes)]

    def to_sibling(array):
        return lax.ppermute(array, "aux", [(i, i ^ 1) for i in range(auxes)])

    own = [arrange(integrals, block_mask, chips, second) for second in (False, True)]
    arriving = [lax.ppermute(a, "aux", along(1)) for a in own]
    z, w = transform(block_atom, green_occ, green_virt, rows, own)
    *later, z = lax.optimization_barrier((*own, z))
    arriving[0], z = lax.optimization_barrier((arriving[0], z))
    sibling = [to_sibling(a) for a in later]
    backs, aheads = [], []
    for step in range(1, chips // 2 + 1):
        held, last = arriving, step == chips // 2
        if not last:
            sent = held if step + 1 < chips // 2 else held[:1]
            arriving = [lax.ppermute(a, "aux", along(1)) for a in sent]
        if step == 1:
            w = transform(block_atom, green_occ, green_virt, rows, sibling, w)
        share = far(w, chips, step, held)
        onward = held
        if last:
            *onward, share = lax.optimization_barrier((*held, share))
        other = [to_sibling(a) for a in onward]
        ahead = lax.ppermute(share, "aux", along(-step))
        if step == 1:
            backs.append(near(z, chips, 0, own, sibling))
        back = near(z, chips, step, held, other)
        if not last:
            arriving[0], ahead, back, backs[-1] = lax.optimization_barrier((arriving[0], ahead, back, backs[-1]))
        aheads.append(ahead)
        backs.append(back)
    if columns == 2 * aux_here and pairs & (pairs - 1) == 0:
        mine, *sends = pack(chips, pairs, backs, aheads)
        parts = [mine]
        for j in range(pairs - 1, 0, -1):
            parts.append(lax.ppermute(sends[j - 1], "pair", [(i, i ^ j) for i in range(pairs)]))
    else:
        (shares,) = pack(chips, None, backs, aheads)
        shares = shares.transpose(1, 0, 2).reshape(nt * aux_here, pairs, columns).transpose(1, 0, 2)
        parts = [lax.all_to_all(shares, "pair", 0, 0)]
    scale = float((rows * pairs * BLK) ** -0.5)
    chi, sums = finish(scale, time_weights, parts, (nt, aux_here, columns), pairs * auxes)
    everyone = lax.all_to_all(sums, ("pair", "aux"), 0, 0, tiled=True)
    energy = -jnp.sum(everyone[:, 0]) / jnp.float32(aux_total * aux_total)
    return chi, energy


def solution(mesh):
    placed = (P("pair", "aux"), P(None, "aux"), P(), P(), P(), P())
    return jax.shard_map(
        per_device,
        mesh=mesh,
        in_specs=placed,
        out_specs=(P(None, "aux", "pair"), P()),
        check_vma=False,
    )
```

```python
import functools
import jax
import jax.numpy as jnp
from jax import lax
from jax.experimental import pallas as pl
from jax.experimental.pallas import tpu as pltpu
from jax.sharding import PartitionSpec as P

BLK = 64
VMEM = pl.BlockSpec(memory_space=pltpu.VMEM)
SMEM = pl.BlockSpec(memory_space=pltpu.SMEM)
HBM = pl.BlockSpec(memory_space=pltpu.HBM)
NT_DIMS = (((1,), (1,)), ((), ()))


def call(kernel, name, flops, **settings):
    return pl.pallas_call(
        kernel,
        name=name,
        compiler_params=pltpu.CompilerParams(vmem_limit_bytes=40 * 1024 * 1024),
        cost_estimate=pl.CostEstimate(flops=flops, bytes_accessed=1 << 8, transcendentals=0),
        **settings,
    )


def stay(array):
    return pltpu.with_memory_space_constraint(array, pltpu.HBM)


def chip_of():
    return lax.axis_index("aux") // 2


def early(chips, chip):
    return (chip < chips // 2).astype(jnp.int32)


def arrange_kernel(rows, aux, chips, second, x_hbm, mask_hbm, y_ref, x, mask, wide, arrived):
    half = early(chips, chip_of())
    half = 1 - half if second else half
    start = pl.multiple_of(half * (rows // 2), rows // 2)
    copies = [
        pltpu.make_async_copy(x_hbm.at[pl.ds(start, rows // 2)], x, arrived.at[0]),
        pltpu.make_async_copy(mask_hbm, mask, arrived.at[1]),
    ]
    for copy in copies:
        copy.start()
    block = lax.axis_index("pair") * rows // BLK
    low = lax.broadcasted_iota(jnp.int32, (8, 128), 1) < BLK
    for copy in copies:
        copy.wait()
    for i in range(aux // 2):
        tile = x[:, i * 128:(i + 1) * 128].astype(jnp.float32)
        first, last = tile[:8], tile[8:]
        even = jnp.where(low, first, pltpu.roll(last, BLK, 1))
        odd = jnp.where(low, pltpu.roll(first, BLK, 1), last)
        even = jnp.where(mask[block, 2 * i] > 0, even, 0.0)
        odd = jnp.where(mask[block, 2 * i + 1] > 0, odd, 0.0)
        wide[pl.ds(2 * i, 8, stride=aux), :] = even
        wide[pl.ds(2 * i + 1, 8, stride=aux), :] = odd
    for s in range(8):
        lane = s % 2 * 128
        y_ref[s // 2, :, lane:lane + 128] = wide[s * aux:(s + 1) * aux, :].astype(y_ref.dtype)


def arrange(integrals, block_mask, chips, second):
    rows, width = integrals.shape
    aux = width // BLK
    return call(
        functools.partial(arrange_kernel, rows, aux, chips, second),
        "arrange",
        1 << 28,
        out_shape=jax.ShapeDtypeStruct((4, aux, 256), jnp.bfloat16),
        in_specs=[HBM, HBM],
        out_specs=VMEM,
        scratch_shapes=[
            pltpu.VMEM((rows // 2, width), jnp.bfloat16),
            pltpu.SMEM(block_mask.shape, jnp.int32),
            pltpu.VMEM((8 * aux, 128), jnp.float32),
            pltpu.SemaphoreType.DMA((2,)),
        ],
    )(stay(integrals), stay(block_mask))


def transform_kernel(nt, rows, own, atom_hbm, occ_hbm, virt_hbm, *refs):
    parts, (w_ref, atom_ref, occ_ref, virt_ref, arrived) = refs[:-5], refs[-5:]
    pieces, z_ref = (parts[:2], parts[2]) if own else (parts[1:], None)
    steps, aux, wide = pieces[0].shape
    copies = wide // BLK
    copy = pltpu.make_async_copy(atom_hbm, atom_ref, arrived.at[0])
    copy.start()
    copy.wait()
    atom = atom_ref[lax.axis_index("pair") * rows // BLK]
    fetch = [
        pltpu.make_async_copy(occ_hbm.at[:, atom], occ_ref, arrived.at[0]),
        pltpu.make_async_copy(virt_hbm.at[:, atom], virt_ref, arrived.at[1]),
    ]
    for copy in fetch:
        copy.start()
    for copy in fetch:
        copy.wait()
    core = lax.rem(lax.axis_index("aux"), 2)
    core = core if own else 1 - core
    place = pl.ds(pl.multiple_of(core * aux, aux), aux)
    same = (
        lax.broadcasted_iota(jnp.int32, (wide, wide), 0) // BLK
        == lax.broadcasted_iota(jnp.int32, (wide, wide), 1) // BLK
    )

    def diagonal(block):
        tall = jnp.concatenate([block.astype(jnp.float32)] * copies, axis=0)
        full = jnp.concatenate([tall] * copies, axis=1)
        return jnp.where(same, full, 0.0).astype(jnp.bfloat16)

    def through(y, first, second):
        half = jnp.dot(y, first, preferred_element_type=jnp.float32).astype(jnp.bfloat16)
        full = lax.dot_general(half, second, NT_DIMS, preferred_element_type=jnp.float32)
        return full.astype(jnp.bfloat16).reshape(steps, aux, wide)

    for t in range(nt):
        occ, virt = diagonal(occ_ref[t]), diagonal(virt_ref[t])
        for half in range(2):
            y = pieces[half][...].reshape(steps * aux, wide)
            if own:
                z_ref[half, :, t * aux:(t + 1) * aux, :] = through(y, occ, virt)
            w_ref[half, t, :, place, :] = through(y, virt, occ)


def transform(atom, green_occ, green_virt, rows, pieces, before=None):
    nt = green_occ.shape[0]
    steps, aux, wide = pieces[0].shape
    own = before is None
    w_shape = jax.ShapeDtypeStruct((2, nt, steps, 2 * aux, wide), jnp.bfloat16)
    z_shape = jax.ShapeDtypeStruct((2, steps, nt * aux, wide), jnp.bfloat16)
    operands = (stay(atom), stay(green_occ), stay(green_virt), *(() if own else (before,)), *pieces)
    return call(
        functools.partial(transform_kernel, nt, rows, own),
        "transform",
        2 << 30,
        out_shape=(z_shape, w_shape) if own else w_shape,
        in_specs=[HBM] * 3 + [VMEM] * (len(operands) - 3),
        out_specs=(VMEM, VMEM) if own else VMEM,
        input_output_aliases={} if own else {3: 0},
        scratch_shapes=[
            pltpu.SMEM(atom.shape, jnp.int32),
            pltpu.VMEM((nt, BLK, BLK), jnp.bfloat16),
            pltpu.VMEM((nt, BLK, BLK), jnp.bfloat16),
            pltpu.SemaphoreType.DMA((2,)),
        ],
    )(*operands)


def matching(chips, step, piece):
    chip = chip_of()
    source = lax.rem(chip + chips - step, chips)
    swap = early(chips, chip) != early(chips, source)
    return jnp.where(swap, 1 - piece, piece)


def near_kernel(chips, step, count, z_ref, *refs):
    mine, other, out_ref = refs[:count], refs[count:2 * count], refs[-1]
    halves = [matching(chips, step, piece) for piece in range(count)]

    def products(low, high):
        total = jnp.zeros(out_ref.shape, jnp.float32)
        for half, first, second in zip(halves, low, high):
            for j in range(z_ref.shape[1]):
                partner = jnp.concatenate([first[j], second[j]], axis=0)
                total += lax.dot_general(z_ref[half, j], partner, NT_DIMS, preferred_element_type=jnp.float32)
        out_ref[...] = total

    core = lax.rem(lax.axis_index("aux"), 2)
    pl.when(core == 0)(lambda: products(mine, other))
    pl.when(core == 1)(lambda: products(other, mine))


def near(z, chips, step, mine, other):
    size = z.shape[2]
    return call(
        functools.partial(near_kernel, chips, step, len(mine)),
        "near",
        1 << 30,
        out_shape=jax.ShapeDtypeStruct((size, 2 * mine[0].shape[-2]), jnp.float32),
        in_specs=[VMEM] * (1 + 2 * len(mine)),
        out_specs=VMEM,
    )(z, *mine, *other)


def fold(x):
    high = x.shape[0] // 2
    past = jnp.concatenate([x[:high, 128:], x[high:, 128:]], axis=1)
    return jnp.concatenate([x[:, :128], past], axis=0)


def unfold(x):
    high = x.shape[0] // 3
    past = x[2 * high:]
    past = jnp.concatenate([past[:, :BLK], past[:, BLK:]], axis=0)
    return jnp.concatenate([x[:2 * high], past], axis=1)


def far_kernel(chips, step, count, w_ref, *refs):
    mine, out_ref = refs[:count], refs[count]
    nt, steps = w_ref.shape[1:3]
    aux = mine[0].shape[1]
    halves = [matching(chips, step, piece) for piece in range(count)]
    shares = []
    for t in range(nt):
        total = jnp.zeros((aux, w_ref.shape[3]), jnp.float32)
        for half, piece in zip(halves, mine):
            for j in range(steps):
                total += lax.dot_general(piece[j], w_ref[half, t, j], NT_DIMS, preferred_element_type=jnp.float32)
        shares.append(total)
    out_ref[...] = fold(jnp.concatenate(shares, axis=0)).astype(out_ref.dtype)


def far(w, chips, step, mine):
    aux = mine[0].shape[1]
    return call(
        functools.partial(far_kernel, chips, step, len(mine)),
        "far",
        1 << 30,
        out_shape=jax.ShapeDtypeStruct((w.shape[1] * aux * 3 // 2, 128), jnp.bfloat16),
        in_specs=[VMEM] * (1 + len(mine)),
        out_specs=VMEM,
    )(w, *mine)


def pack_kernel(chips, pairs, *refs):
    backs, aheads = refs[:chips // 2 + 1], refs[chips // 2 + 1:chips + 1]
    outs, shares = refs[chips + 1:-1], refs[-1]
    chip = chip_of()
    for step in range(chips // 2):
        shares[lax.rem(chip + chips - step, chips)] = fold(backs[step][...])
    for step in range(1, chips // 2):
        shares[lax.rem(chip + step, chips)] = aheads[step - 1][...].astype(jnp.float32)
    opposite = fold(backs[-1][...]) + aheads[-1][...].astype(jnp.float32)
    shares[lax.rem(chip + chips // 2, chips)] = opposite
    if pairs is None:
        for q in range(chips):
            outs[0][q] = unfold(shares[q]).astype(jnp.bfloat16)
    else:
        pair = lax.axis_index("pair")
        for j, out_ref in enumerate(outs):
            out_ref[...] = shares[lax.bitwise_xor(pair, j)].astype(out_ref.dtype)


def pack(chips, pairs, backs, aheads):
    height, width = backs[0].shape
    folded = (height * 3 // 2, 128)
    if pairs is None:
        out_shape = (jax.ShapeDtypeStruct((chips, height, width), jnp.bfloat16),)
    else:
        out_shape = (jax.ShapeDtypeStruct(folded, jnp.float32),)
        out_shape += (jax.ShapeDtypeStruct(folded, jnp.bfloat16),) * (pairs - 1)
    return call(
        functools.partial(pack_kernel, chips, pairs),
        "pack",
        1 << 28,
        out_shape=out_shape,
        in_specs=[VMEM] * (chips + 1),
        out_specs=(VMEM,) * len(out_shape),
        scratch_shapes=[pltpu.VMEM((chips,) + folded, jnp.float32)],
    )(*backs, *aheads)


def finish_kernel(scale, nt, folded, weight_ref, *refs):
    parts, (chi_ref, sum_ref) = refs[:-2], refs[-2:]
    aux = chi_ref.shape[1]
    if folded:
        total = parts[0][...]
        for part in parts[1:]:
            total += part[...].astype(jnp.float32)
        total = unfold(total * scale)
    else:
        total = parts[0][0].astype(jnp.float32)
        for p in range(1, parts[0].shape[0]):
            total += parts[0][p].astype(jnp.float32)
        total *= scale
    local = jnp.zeros((1, 1), jnp.float32)
    for t in range(nt):
        chi = total[t * aux:(t + 1) * aux]
        chi_ref[t] = chi
        local += weight_ref[t] * jnp.sum(chi * chi, keepdims=True)
    sum_ref[...] = jnp.broadcast_to(local, sum_ref.shape)


def finish(scale, time_weights, parts, chi_shape, copies):
    return call(
        functools.partial(finish_kernel, scale, chi_shape[0], len(parts) > 1),
        "finish",
        1 << 28,
        out_shape=(
            jax.ShapeDtypeStruct(chi_shape, jnp.float32),
            jax.ShapeDtypeStruct((copies, 128), jnp.float32),
        ),
        in_specs=[SMEM] + [VMEM] * len(parts),
        out_specs=(VMEM, VMEM),
    )(time_weights, *parts)


def per_device(integrals, block_mask, block_atom, green_occ, green_virt, time_weights):
    rows = integrals.shape[0]
    aux_here = integrals.shape[1] // BLK
    pairs, auxes = lax.axis_size("pair"), lax.axis_size("aux")
    chips = auxes // 2
    aux_total = aux_here * auxes
    columns = aux_total // pairs
    nt = green_occ.shape[0]

    def along(shift):
        return [(i, (i + 2 * shift) % auxes) for i in range(auxes)]

    def to_sibling(array):
        return lax.ppermute(array, "aux", [(i, i ^ 1) for i in range(auxes)])

    own = [arrange(integrals, block_mask, chips, second) for second in (False, True)]
    arriving = [lax.ppermute(a, "aux", along(1)) for a in own]
    z, w = transform(block_atom, green_occ, green_virt, rows, own)
    *later, z = lax.optimization_barrier((*own, z))
    arriving[0], z = lax.optimization_barrier((arriving[0], z))
    sibling = [to_sibling(a) for a in later]
    backs, aheads = [], []
    for step in range(1, chips // 2 + 1):
        held, last = arriving, step == chips // 2
        if not last:
            sent = held if step + 1 < chips // 2 else held[:1]
            arriving = [lax.ppermute(a, "aux", along(1)) for a in sent]
        if step == 1:
            w = transform(block_atom, green_occ, green_virt, rows, sibling, w)
        share = far(w, chips, step, held)
        onward = held
        if last:
            *onward, share = lax.optimization_barrier((*held, share))
        other = [to_sibling(a) for a in onward]
        ahead = lax.ppermute(share, "aux", along(-step))
        if step == 1:
            backs.append(near(z, chips, 0, own, sibling))
        back = near(z, chips, step, held, other)
        if not last:
            arriving[0], _, back, backs[-1] = lax.optimization_barrier((arriving[0], share, back, backs[-1]))
        aheads.append(ahead)
        backs.append(back)
    if columns == 2 * aux_here and pairs & (pairs - 1) == 0:
        mine, *sends = pack(chips, pairs, backs, aheads)
        parts = [mine]
        for j in range(1, pairs):
            parts.append(lax.ppermute(sends[j - 1], "pair", [(i, i ^ j) for i in range(pairs)]))
    else:
        (shares,) = pack(chips, None, backs, aheads)
        shares = shares.transpose(1, 0, 2).reshape(nt * aux_here, pairs, columns).transpose(1, 0, 2)
        parts = [lax.all_to_all(shares, "pair", 0, 0)]
    scale = float((rows * pairs * BLK) ** -0.5)
    doubling = pairs & (pairs - 1) == 0 and auxes & (auxes - 1) == 0
    copies = 8 if doubling else pairs * auxes
    chi, sums = finish(scale, time_weights, parts, (nt, aux_here, columns), copies)
    if doubling:
        for axis, size in (("pair", pairs), ("aux", auxes)):
            for bit in range(size.bit_length() - 1):
                sums += lax.ppermute(sums, axis, [(i, i ^ 1 << bit) for i in range(size)])
        total = sums[0, 0]
    else:
        total = jnp.sum(lax.all_to_all(sums, ("pair", "aux"), 0, 0, tiled=True)[:, 0])
    energy = -total / jnp.float32(aux_total * aux_total)
    return chi, energy


def solution(mesh):
    placed = (P("pair", "aux"), P(None, "aux"), P(), P(), P(), P())
    return jax.shard_map(
        per_device,
        mesh=mesh,
        in_specs=placed,
        out_specs=(P(None, "aux", "pair"), P()),
        check_vma=False,
    )
```

```python
import functools
import jax
import jax.numpy as jnp
from jax import lax
from jax.experimental import pallas as pl
from jax.experimental.pallas import tpu as pltpu
from jax.sharding import PartitionSpec as P

BLK = 64
VMEM = pl.BlockSpec(memory_space=pltpu.VMEM)
SMEM = pl.BlockSpec(memory_space=pltpu.SMEM)
HBM = pl.BlockSpec(memory_space=pltpu.HBM)
NT_DIMS = (((1,), (1,)), ((), ()))


def call(kernel, name, flops, **settings):
    return pl.pallas_call(
        kernel,
        name=name,
        compiler_params=pltpu.CompilerParams(vmem_limit_bytes=40 * 1024 * 1024),
        cost_estimate=pl.CostEstimate(flops=flops, bytes_accessed=1 << 8, transcendentals=0),
        **settings,
    )


def stay(array):
    return pltpu.with_memory_space_constraint(array, pltpu.HBM)


def chip_of():
    return lax.axis_index("aux") // 2


def arrange_kernel(rows, aux, second, x_hbm, mask_hbm, y_ref, x, mask, wide, arrived):
    copies = [
        pltpu.make_async_copy(x_hbm.at[pl.ds(second * (rows // 2), rows // 2)], x, arrived.at[0]),
        pltpu.make_async_copy(mask_hbm, mask, arrived.at[1]),
    ]
    for copy in copies:
        copy.start()
    block = lax.axis_index("pair") * rows // BLK
    low = lax.broadcasted_iota(jnp.int32, (8, 128), 1) < BLK
    for copy in copies:
        copy.wait()
    for i in range(aux // 2):
        tile = x[:, i * 128:(i + 1) * 128].astype(jnp.float32)
        first, last = tile[:8], tile[8:]
        even = jnp.where(low, first, pltpu.roll(last, BLK, 1))
        odd = jnp.where(low, pltpu.roll(first, BLK, 1), last)
        even = jnp.where(mask[block, 2 * i] > 0, even, 0.0)
        odd = jnp.where(mask[block, 2 * i + 1] > 0, odd, 0.0)
        wide[pl.ds(2 * i, 8, stride=aux), :] = even
        wide[pl.ds(2 * i + 1, 8, stride=aux), :] = odd
    for s in range(8):
        lane = s % 2 * 128
        y_ref[s // 2, :, lane:lane + 128] = wide[s * aux:(s + 1) * aux, :].astype(y_ref.dtype)


def arrange(integrals, block_mask, second):
    rows, width = integrals.shape
    aux = width // BLK
    return call(
        functools.partial(arrange_kernel, rows, aux, second),
        "arrange",
        1 << 28,
        out_shape=jax.ShapeDtypeStruct((4, aux, 256), jnp.bfloat16),
        in_specs=[HBM, HBM],
        out_specs=VMEM,
        scratch_shapes=[
            pltpu.VMEM((rows // 2, width), jnp.bfloat16),
            pltpu.SMEM(block_mask.shape, jnp.int32),
            pltpu.VMEM((8 * aux, 128), jnp.float32),
            pltpu.SemaphoreType.DMA((2,)),
        ],
    )(stay(integrals), stay(block_mask))


def transform_kernel(nt, rows, own, atom_hbm, occ_hbm, virt_hbm, *refs):
    parts, (w_ref, atom_ref, occ_ref, virt_ref, arrived) = refs[:-5], refs[-5:]
    pieces, z_ref = (parts[:2], parts[2]) if own else (parts[1:], None)
    steps, aux, wide = pieces[0].shape
    copies = wide // BLK
    copy = pltpu.make_async_copy(atom_hbm, atom_ref, arrived.at[0])
    copy.start()
    copy.wait()
    atom = atom_ref[lax.axis_index("pair") * rows // BLK]
    fetch = [
        pltpu.make_async_copy(occ_hbm.at[:, atom], occ_ref, arrived.at[0]),
        pltpu.make_async_copy(virt_hbm.at[:, atom], virt_ref, arrived.at[1]),
    ]
    for copy in fetch:
        copy.start()
    for copy in fetch:
        copy.wait()
    core = lax.rem(lax.axis_index("aux"), 2)
    core = core if own else 1 - core
    place = pl.ds(pl.multiple_of(core * aux, aux), aux)
    same = (
        lax.broadcasted_iota(jnp.int32, (wide, wide), 0) // BLK
        == lax.broadcasted_iota(jnp.int32, (wide, wide), 1) // BLK
    )

    def diagonal(block):
        tall = jnp.concatenate([block.astype(jnp.float32)] * copies, axis=0)
        full = jnp.concatenate([tall] * copies, axis=1)
        return jnp.where(same, full, 0.0).astype(jnp.bfloat16)

    def through(y, first, second):
        half = jnp.dot(y, first, preferred_element_type=jnp.float32).astype(jnp.bfloat16)
        full = lax.dot_general(half, second, NT_DIMS, preferred_element_type=jnp.float32)
        return full.astype(jnp.bfloat16).reshape(steps, aux, wide)

    for t in range(nt):
        occ, virt = diagonal(occ_ref[t]), diagonal(virt_ref[t])
        for half in range(2):
            y = pieces[half][...].reshape(steps * aux, wide)
            if own:
                z_ref[half, :, t * aux:(t + 1) * aux, :] = through(y, occ, virt)
            w_ref[half, t, :, place, :] = through(y, virt, occ)


def transform(atom, green_occ, green_virt, rows, pieces, before=None):
    nt = green_occ.shape[0]
    steps, aux, wide = pieces[0].shape
    own = before is None
    w_shape = jax.ShapeDtypeStruct((2, nt, steps, 2 * aux, wide), jnp.bfloat16)
    z_shape = jax.ShapeDtypeStruct((2, steps, nt * aux, wide), jnp.bfloat16)
    operands = (stay(atom), stay(green_occ), stay(green_virt), *(() if own else (before,)), *pieces)
    return call(
        functools.partial(transform_kernel, nt, rows, own),
        "transform",
        2 << 30,
        out_shape=(z_shape, w_shape) if own else w_shape,
        in_specs=[HBM] * 3 + [VMEM] * (len(operands) - 3),
        out_specs=(VMEM, VMEM) if own else VMEM,
        input_output_aliases={} if own else {3: 0},
        scratch_shapes=[
            pltpu.SMEM(atom.shape, jnp.int32),
            pltpu.VMEM((nt, BLK, BLK), jnp.bfloat16),
            pltpu.VMEM((nt, BLK, BLK), jnp.bfloat16),
            pltpu.SemaphoreType.DMA((2,)),
        ],
    )(*operands)


def near_kernel(count, start, z_ref, *refs):
    mine, other, out_ref = refs[:count], refs[count:2 * count], refs[-1]

    def products(low, high):
        total = jnp.zeros(out_ref.shape, jnp.float32)
        for half, (first, second) in enumerate(zip(low, high), start):
            for j in range(z_ref.shape[1]):
                partner = jnp.concatenate([first[j], second[j]], axis=0)
                total += lax.dot_general(z_ref[half, j], partner, NT_DIMS, preferred_element_type=jnp.float32)
        out_ref[...] = total

    core = lax.rem(lax.axis_index("aux"), 2)
    pl.when(core == 0)(lambda: products(mine, other))
    pl.when(core == 1)(lambda: products(other, mine))


def near(z, mine, other, start=0):
    size = z.shape[2]
    return call(
        functools.partial(near_kernel, len(mine), start),
        "near",
        1 << 30,
        out_shape=jax.ShapeDtypeStruct((size, 2 * mine[0].shape[-2]), jnp.float32),
        in_specs=[VMEM] * (1 + 2 * len(mine)),
        out_specs=VMEM,
    )(z, *mine, *other)


def fold(x):
    high = x.shape[0] // 2
    past = jnp.concatenate([x[:high, 128:], x[high:, 128:]], axis=1)
    return jnp.concatenate([x[:, :128], past], axis=0)


def unfold(x):
    high = x.shape[0] // 3
    past = x[2 * high:]
    past = jnp.concatenate([past[:, :BLK], past[:, BLK:]], axis=0)
    return jnp.concatenate([x[:2 * high], past], axis=1)


def far_kernel(w_ref, *refs):
    mine, out_ref = refs[:-1], refs[-1]
    nt, steps = w_ref.shape[1:3]
    aux = mine[0].shape[1]
    shares = []
    for t in range(nt):
        total = jnp.zeros((aux, w_ref.shape[3]), jnp.float32)
        for half, piece in enumerate(mine):
            for j in range(steps):
                total += lax.dot_general(piece[j], w_ref[half, t, j], NT_DIMS, preferred_element_type=jnp.float32)
        shares.append(total)
    out_ref[...] = fold(jnp.concatenate(shares, axis=0)).astype(out_ref.dtype)


def far(w, mine):
    aux = mine[0].shape[1]
    return call(
        far_kernel,
        "far",
        1 << 30,
        out_shape=jax.ShapeDtypeStruct((w.shape[1] * aux * 3 // 2, 128), jnp.bfloat16),
        in_specs=[VMEM] * (1 + len(mine)),
        out_specs=VMEM,
    )(w, *mine)


def pack_kernel(chips, pairs, *refs):
    backs, lower, aheads = refs[:chips // 2 + 1], refs[chips // 2 + 1], refs[chips // 2 + 2:chips + 1]
    outs, shares = refs[chips + 1:-1], refs[-1]
    chip = chip_of()
    for step in range(chips // 2 + 1):
        share = backs[step][...] if step < chips // 2 else backs[step][...] + lower[...]
        shares[lax.rem(chip + chips - step, chips)] = fold(share)
    for step in range(1, chips // 2):
        shares[lax.rem(chip + step, chips)] = aheads[step - 1][...].astype(jnp.float32)
    if pairs is None:
        for q in range(chips):
            outs[0][q] = unfold(shares[q]).astype(jnp.bfloat16)
    else:
        pair = lax.axis_index("pair")
        for j, out_ref in enumerate(outs):
            out_ref[...] = shares[lax.bitwise_xor(pair, j)].astype(out_ref.dtype)


def pack(chips, pairs, backs, aheads):
    height, width = backs[0].shape
    folded = (height * 3 // 2, 128)
    if pairs is None:
        out_shape = (jax.ShapeDtypeStruct((chips, height, width), jnp.bfloat16),)
    else:
        out_shape = (jax.ShapeDtypeStruct(folded, jnp.float32),)
        out_shape += (jax.ShapeDtypeStruct(folded, jnp.bfloat16),) * (pairs - 1)
    return call(
        functools.partial(pack_kernel, chips, pairs),
        "pack",
        1 << 28,
        out_shape=out_shape,
        in_specs=[VMEM] * (chips + 1),
        out_specs=(VMEM,) * len(out_shape),
        scratch_shapes=[pltpu.VMEM((chips,) + folded, jnp.float32)],
    )(*backs, *aheads)


def finish_kernel(scale, nt, folded, weight_ref, *refs):
    parts, (chi_ref, sum_ref) = refs[:-2], refs[-2:]
    aux = chi_ref.shape[1]
    if folded:
        total = parts[0][...]
        for part in parts[1:]:
            total += part[...].astype(jnp.float32)
        total = unfold(total * scale)
    else:
        total = parts[0][0].astype(jnp.float32)
        for p in range(1, parts[0].shape[0]):
            total += parts[0][p].astype(jnp.float32)
        total *= scale
    local = jnp.zeros((1, 1), jnp.float32)
    for t in range(nt):
        chi = total[t * aux:(t + 1) * aux]
        chi_ref[t] = chi
        local += weight_ref[t] * jnp.sum(chi * chi, keepdims=True)
    sum_ref[...] = jnp.broadcast_to(local, sum_ref.shape)


def finish(scale, time_weights, parts, chi_shape, copies):
    return call(
        functools.partial(finish_kernel, scale, chi_shape[0], len(parts) > 1),
        "finish",
        1 << 28,
        out_shape=(
            jax.ShapeDtypeStruct(chi_shape, jnp.float32),
            jax.ShapeDtypeStruct((copies, 128), jnp.float32),
        ),
        in_specs=[SMEM] + [VMEM] * len(parts),
        out_specs=(VMEM, VMEM),
    )(time_weights, *parts)


def per_device(integrals, block_mask, block_atom, green_occ, green_virt, time_weights):
    rows = integrals.shape[0]
    aux_here = integrals.shape[1] // BLK
    pairs, auxes = lax.axis_size("pair"), lax.axis_size("aux")
    chips = auxes // 2
    aux_total = aux_here * auxes
    columns = aux_total // pairs
    nt = green_occ.shape[0]

    def along(shift):
        return [(i, (i + 2 * shift) % auxes) for i in range(auxes)]

    def to_sibling(array):
        return lax.ppermute(array, "aux", [(i, i ^ 1) for i in range(auxes)])

    own = [arrange(integrals, block_mask, second) for second in (False, True)]
    arriving = [lax.ppermute(a, "aux", along(1)) for a in own]
    z, w = transform(block_atom, green_occ, green_virt, rows, own)
    *later, z = lax.optimization_barrier((*own, z))
    arriving[0], z = lax.optimization_barrier((arriving[0], z))
    sibling = [to_sibling(a) for a in later]
    backs, aheads = [], []
    for step in range(1, chips // 2 + 1):
        held, last = arriving, step == chips // 2
        if not last:
            arriving = [lax.ppermute(a, "aux", along(1)) for a in held]
        if last:
            upper = near(z, held[:1], [to_sibling(held[0])])
            later, upper = lax.optimization_barrier((held[1], upper))
            backs += [upper, near(z, [later], [to_sibling(later)], 1)]
            continue
        other = [to_sibling(a) for a in held]
        if step == 1:
            w = transform(block_atom, green_occ, green_virt, rows, sibling, w)
        share = far(w, held)
        ahead = lax.ppermute(share, "aux", along(-step))
        if step == 1:
            backs.append(near(z, own, sibling))
        backs.append(near(z, held, other))
        arriving[0], _, backs[-1], backs[-2] = lax.optimization_barrier((arriving[0], share, backs[-1], backs[-2]))
        arriving[1], ahead = lax.optimization_barrier((arriving[1], ahead))
        aheads.append(ahead)
    if columns == 2 * aux_here and pairs & (pairs - 1) == 0:
        mine, *sends = pack(chips, pairs, backs, aheads)
        parts = [mine]
        for j in range(pairs - 1, 0, -1):
            parts.append(lax.ppermute(sends[j - 1], "pair", [(i, i ^ j) for i in range(pairs)]))
    else:
        (shares,) = pack(chips, None, backs, aheads)
        shares = shares.transpose(1, 0, 2).reshape(nt * aux_here, pairs, columns).transpose(1, 0, 2)
        parts = [lax.all_to_all(shares, "pair", 0, 0)]
    scale = float((rows * pairs * BLK) ** -0.5)
    chi, sums = finish(scale, time_weights, parts, (nt, aux_here, columns), pairs * auxes)
    total = jnp.sum(lax.all_to_all(sums, ("pair", "aux"), 0, 0, tiled=True)[:, 0])
    energy = -total / jnp.float32(aux_total * aux_total)
    return chi, energy


def solution(mesh):
    placed = (P("pair", "aux"), P(None, "aux"), P(), P(), P(), P())
    return jax.shard_map(
        per_device,
        mesh=mesh,
        in_specs=placed,
        out_specs=(P(None, "aux", "pair"), P()),
        check_vma=False,
    )
```

```python
import functools
import jax
import jax.numpy as jnp
from jax import lax
from jax.experimental import pallas as pl
from jax.experimental.pallas import tpu as pltpu
from jax.sharding import PartitionSpec as P

BLK = 64
VMEM = pl.BlockSpec(memory_space=pltpu.VMEM)
SMEM = pl.BlockSpec(memory_space=pltpu.SMEM)
HBM = pl.BlockSpec(memory_space=pltpu.HBM)
NT_DIMS = (((1,), (1,)), ((), ()))


def call(kernel, name, flops, **settings):
    return pl.pallas_call(
        kernel,
        name=name,
        compiler_params=pltpu.CompilerParams(vmem_limit_bytes=40 * 1024 * 1024),
        cost_estimate=pl.CostEstimate(flops=flops, bytes_accessed=1 << 8, transcendentals=0),
        **settings,
    )


def stay(array):
    return pltpu.with_memory_space_constraint(array, pltpu.HBM)


def chip_of():
    return lax.axis_index("aux") // 2


def arrange_kernel(rows, aux, second, x_hbm, mask_hbm, y_ref, x, mask, wide, arrived):
    copies = [
        pltpu.make_async_copy(x_hbm.at[pl.ds(second * (rows // 2), rows // 2)], x, arrived.at[0]),
        pltpu.make_async_copy(mask_hbm, mask, arrived.at[1]),
    ]
    for copy in copies:
        copy.start()
    block = lax.axis_index("pair") * rows // BLK
    low = lax.broadcasted_iota(jnp.int32, (8, 128), 1) < BLK
    for copy in copies:
        copy.wait()
    for i in range(aux // 2):
        tile = x[:, i * 128:(i + 1) * 128].astype(jnp.float32)
        first, last = tile[:8], tile[8:]
        even = jnp.where(low, first, pltpu.roll(last, BLK, 1))
        odd = jnp.where(low, pltpu.roll(first, BLK, 1), last)
        even = jnp.where(mask[block, 2 * i] > 0, even, 0.0)
        odd = jnp.where(mask[block, 2 * i + 1] > 0, odd, 0.0)
        wide[pl.ds(2 * i, 8, stride=aux), :] = even
        wide[pl.ds(2 * i + 1, 8, stride=aux), :] = odd
    for s in range(8):
        lane = s % 2 * 128
        y_ref[s // 2, :, lane:lane + 128] = wide[s * aux:(s + 1) * aux, :].astype(y_ref.dtype)


def arrange(integrals, block_mask, second):
    rows, width = integrals.shape
    aux = width // BLK
    return call(
        functools.partial(arrange_kernel, rows, aux, second),
        "arrange",
        1 << 28,
        out_shape=jax.ShapeDtypeStruct((4, aux, 256), jnp.bfloat16),
        in_specs=[HBM, HBM],
        out_specs=VMEM,
        scratch_shapes=[
            pltpu.VMEM((rows // 2, width), jnp.bfloat16),
            pltpu.SMEM(block_mask.shape, jnp.int32),
            pltpu.VMEM((8 * aux, 128), jnp.float32),
            pltpu.SemaphoreType.DMA((2,)),
        ],
    )(stay(integrals), stay(block_mask))


def transform_kernel(nt, rows, atom_hbm, occ_hbm, virt_hbm, y1, y2, o1, o2, z_ref, w_ref, *scratch):
    atom_ref, occ_ref, virt_ref, arrived = scratch
    steps, aux, wide = y1.shape
    copies = wide // BLK
    copy = pltpu.make_async_copy(atom_hbm, atom_ref, arrived.at[0])
    copy.start()
    copy.wait()
    atom = atom_ref[lax.axis_index("pair") * rows // BLK]
    fetch = [
        pltpu.make_async_copy(occ_hbm.at[:, atom], occ_ref, arrived.at[0]),
        pltpu.make_async_copy(virt_hbm.at[:, atom], virt_ref, arrived.at[1]),
    ]
    for copy in fetch:
        copy.start()
    for copy in fetch:
        copy.wait()
    core = lax.rem(lax.axis_index("aux"), 2)
    same = (
        lax.broadcasted_iota(jnp.int32, (wide, wide), 0) // BLK
        == lax.broadcasted_iota(jnp.int32, (wide, wide), 1) // BLK
    )

    def diagonal(block):
        tall = jnp.concatenate([block.astype(jnp.float32)] * copies, axis=0)
        full = jnp.concatenate([tall] * copies, axis=1)
        return jnp.where(same, full, 0.0).astype(jnp.bfloat16)

    def through(y, first, second):
        half = jnp.dot(y, first, preferred_element_type=jnp.float32).astype(jnp.bfloat16)
        full = lax.dot_general(half, second, NT_DIMS, preferred_element_type=jnp.float32)
        return full.astype(jnp.bfloat16).reshape(steps, aux, wide)

    for t in range(nt):
        occ, virt = diagonal(occ_ref[t]), diagonal(virt_ref[t])
        for half, pieces in enumerate(((y1, o1), (y2, o2))):
            for which, piece in enumerate(pieces):
                y = piece[...].reshape(steps * aux, wide)
                if which == 0:
                    z_ref[half, :, t * aux:(t + 1) * aux, :] = through(y, occ, virt)
                place = jnp.bitwise_xor(core, which) * aux
                w_ref[half, t, :, pl.ds(pl.multiple_of(place, aux), aux), :] = through(y, virt, occ)


def transform(atom, green_occ, green_virt, rows, own, sibling):
    nt = green_occ.shape[0]
    steps, aux, wide = own[0].shape
    return call(
        functools.partial(transform_kernel, nt, rows),
        "transform",
        2 << 30,
        out_shape=(
            jax.ShapeDtypeStruct((2, steps, nt * aux, wide), jnp.bfloat16),
            jax.ShapeDtypeStruct((2, nt, steps, 2 * aux, wide), jnp.bfloat16),
        ),
        in_specs=[HBM] * 3 + [VMEM] * 4,
        out_specs=(VMEM, VMEM),
        scratch_shapes=[
            pltpu.SMEM(atom.shape, jnp.int32),
            pltpu.VMEM((nt, BLK, BLK), jnp.bfloat16),
            pltpu.VMEM((nt, BLK, BLK), jnp.bfloat16),
            pltpu.SemaphoreType.DMA((2,)),
        ],
    )(stay(atom), stay(green_occ), stay(green_virt), *own, *sibling)


def near_kernel(count, z_ref, *refs):
    mine, other, out_ref = refs[:count], refs[count:2 * count], refs[-1]

    def products(low, high):
        total = jnp.zeros(out_ref.shape, jnp.float32)
        for half, (first, second) in enumerate(zip(low, high)):
            for j in range(z_ref.shape[1]):
                partner = jnp.concatenate([first[j], second[j]], axis=0)
                total += lax.dot_general(z_ref[half, j], partner, NT_DIMS, preferred_element_type=jnp.float32)
        out_ref[...] = total

    core = lax.rem(lax.axis_index("aux"), 2)
    pl.when(core == 0)(lambda: products(mine, other))
    pl.when(core == 1)(lambda: products(other, mine))


def near(z, mine, other):
    size = z.shape[2]
    return call(
        functools.partial(near_kernel, len(mine)),
        "near",
        1 << 30,
        out_shape=jax.ShapeDtypeStruct((size, 2 * mine[0].shape[-2]), jnp.float32),
        in_specs=[VMEM] * (1 + 2 * len(mine)),
        out_specs=VMEM,
    )(z, *mine, *other)


def fold(x):
    high = x.shape[0] // 2
    past = jnp.concatenate([x[:high, 128:], x[high:, 128:]], axis=1)
    return jnp.concatenate([x[:, :128], past], axis=0)


def unfold(x):
    high = x.shape[0] // 3
    past = x[2 * high:]
    past = jnp.concatenate([past[:, :BLK], past[:, BLK:]], axis=0)
    return jnp.concatenate([x[:2 * high], past], axis=1)


def far_kernel(w_ref, *refs):
    mine, out_ref = refs[:-1], refs[-1]
    nt, steps = w_ref.shape[1:3]
    aux = mine[0].shape[1]
    shares = []
    for t in range(nt):
        total = jnp.zeros((aux, w_ref.shape[3]), jnp.float32)
        for half, piece in enumerate(mine):
            for j in range(steps):
                total += lax.dot_general(piece[j], w_ref[half, t, j], NT_DIMS, preferred_element_type=jnp.float32)
        shares.append(total)
    out_ref[...] = fold(jnp.concatenate(shares, axis=0)).astype(out_ref.dtype)


def far(w, mine):
    aux = mine[0].shape[1]
    return call(
        far_kernel,
        "far",
        1 << 30,
        out_shape=jax.ShapeDtypeStruct((w.shape[1] * aux * 3 // 2, 128), jnp.bfloat16),
        in_specs=[VMEM] * (1 + len(mine)),
        out_specs=VMEM,
    )(w, *mine)


def pack_kernel(chips, pairs, *refs):
    backs, aheads = refs[:chips // 2 + 1], refs[chips // 2 + 1:chips]
    outs, shares = refs[chips:-1], refs[-1]
    chip = chip_of()
    for step in range(chips // 2 + 1):
        shares[lax.rem(chip + chips - step, chips)] = fold(backs[step][...])
    for step in range(1, chips // 2):
        shares[lax.rem(chip + step, chips)] = aheads[step - 1][...].astype(jnp.float32)
    if pairs is None:
        for q in range(chips):
            outs[0][q] = unfold(shares[q]).astype(jnp.bfloat16)
    else:
        pair = lax.axis_index("pair")
        for j, out_ref in enumerate(outs):
            out_ref[...] = shares[lax.bitwise_xor(pair, j)].astype(out_ref.dtype)


def pack(chips, pairs, backs, aheads):
    height, width = backs[0].shape
    folded = (height * 3 // 2, 128)
    if pairs is None:
        out_shape = (jax.ShapeDtypeStruct((chips, height, width), jnp.bfloat16),)
    else:
        out_shape = (jax.ShapeDtypeStruct(folded, jnp.float32),)
        out_shape += (jax.ShapeDtypeStruct(folded, jnp.bfloat16),) * (pairs - 1)
    return call(
        functools.partial(pack_kernel, chips, pairs),
        "pack",
        1 << 28,
        out_shape=out_shape,
        in_specs=[VMEM] * chips,
        out_specs=(VMEM,) * len(out_shape),
        scratch_shapes=[pltpu.VMEM((chips,) + folded, jnp.float32)],
    )(*backs, *aheads)


def finish_kernel(scale, nt, folded, weight_ref, *refs):
    parts, (chi_ref, sum_ref) = refs[:-2], refs[-2:]
    aux = chi_ref.shape[1]
    if folded:
        total = parts[0][...]
        for part in parts[1:]:
            total += part[...].astype(jnp.float32)
        total = unfold(total * scale)
    else:
        total = parts[0][0].astype(jnp.float32)
        for p in range(1, parts[0].shape[0]):
            total += parts[0][p].astype(jnp.float32)
        total *= scale
    local = jnp.zeros((1, 1), jnp.float32)
    for t in range(nt):
        chi = total[t * aux:(t + 1) * aux]
        chi_ref[t] = chi
        local += weight_ref[t] * jnp.sum(chi * chi, keepdims=True)
    sum_ref[...] = jnp.broadcast_to(local, sum_ref.shape)


def finish(scale, time_weights, parts, chi_shape, copies):
    return call(
        functools.partial(finish_kernel, scale, chi_shape[0], len(parts) > 1),
        "finish",
        1 << 28,
        out_shape=(
            jax.ShapeDtypeStruct(chi_shape, jnp.float32),
            jax.ShapeDtypeStruct((copies, 128), jnp.float32),
        ),
        in_specs=[SMEM] + [VMEM] * len(parts),
        out_specs=(VMEM, VMEM),
    )(time_weights, *parts)


def per_device(integrals, block_mask, block_atom, green_occ, green_virt, time_weights):
    rows = integrals.shape[0]
    aux_here = integrals.shape[1] // BLK
    pairs, auxes = lax.axis_size("pair"), lax.axis_size("aux")
    chips = auxes // 2
    aux_total = aux_here * auxes
    columns = aux_total // pairs
    nt = green_occ.shape[0]

    def along(shift):
        return [(i, (i + 2 * shift) % auxes) for i in range(auxes)]

    def to_sibling(array):
        return lax.ppermute(array, "aux", [(i, i ^ 1) for i in range(auxes)])

    own = [arrange(integrals, block_mask, second) for second in (False, True)]
    arriving = [lax.ppermute(a, "aux", along(1)) for a in own]
    *later, arriving[0] = lax.optimization_barrier((*own, arriving[0]))
    sibling = [to_sibling(a) for a in later]
    z, w = transform(block_atom, green_occ, green_virt, rows, own, sibling)
    backs, aheads = [], []
    for step in range(1, chips // 2 + 1):
        held, last = arriving, step == chips // 2
        if not last:
            arriving = [lax.ppermute(a, "aux", along(1)) for a in held]
        if last:
            backs.append(near(z, held, [to_sibling(a) for a in held]))
            continue
        other = [to_sibling(a) for a in held]
        share = far(w, held)
        ahead = lax.ppermute(share, "aux", along(-step))
        if step == 1:
            backs.append(near(z, own, sibling))
        backs.append(near(z, held, other))
        *arriving, ahead, backs[-1], backs[-2] = lax.optimization_barrier((*arriving, ahead, backs[-1], backs[-2]))
        aheads.append(ahead)
    if columns == 2 * aux_here and pairs & (pairs - 1) == 0:
        mine, *sends = pack(chips, pairs, backs, aheads)
        parts = [mine]
        for j in range(pairs - 1, 0, -1):
            parts.append(lax.ppermute(sends[j - 1], "pair", [(i, i ^ j) for i in range(pairs)]))
    else:
        (shares,) = pack(chips, None, backs, aheads)
        shares = shares.transpose(1, 0, 2).reshape(nt * aux_here, pairs, columns).transpose(1, 0, 2)
        parts = [lax.all_to_all(shares, "pair", 0, 0)]
    scale = float((rows * pairs * BLK) ** -0.5)
    chi, sums = finish(scale, time_weights, parts, (nt, aux_here, columns), pairs * auxes)
    total = jnp.sum(lax.all_to_all(sums, ("pair", "aux"), 0, 0, tiled=True)[:, 0])
    energy = -total / jnp.float32(aux_total * aux_total)
    return chi, energy


def solution(mesh):
    placed = (P("pair", "aux"), P(None, "aux"), P(), P(), P(), P())
    return jax.shard_map(
        per_device,
        mesh=mesh,
        in_specs=placed,
        out_specs=(P(None, "aux", "pair"), P()),
        check_vma=False,
    )
```

```python
import functools
import jax
import jax.numpy as jnp
from jax import lax
from jax.experimental import pallas as pl
from jax.experimental.pallas import tpu as pltpu
from jax.sharding import PartitionSpec as P

BLK = 64
VMEM = pl.BlockSpec(memory_space=pltpu.VMEM)
SMEM = pl.BlockSpec(memory_space=pltpu.SMEM)
HBM = pl.BlockSpec(memory_space=pltpu.HBM)
NT_DIMS = (((1,), (1,)), ((), ()))


def call(kernel, name, flops, **settings):
    return pl.pallas_call(
        kernel,
        name=name,
        compiler_params=pltpu.CompilerParams(vmem_limit_bytes=40 * 1024 * 1024),
        cost_estimate=pl.CostEstimate(flops=flops, bytes_accessed=1 << 8, transcendentals=0),
        **settings,
    )


def stay(array):
    return pltpu.with_memory_space_constraint(array, pltpu.HBM)


def chip_of():
    return lax.axis_index("aux") // 2


def arrange_kernel(rows, aux, second, x_hbm, mask_hbm, y_ref, x, mask, wide, arrived):
    copies = [
        pltpu.make_async_copy(x_hbm.at[pl.ds(second * (rows // 2), rows // 2)], x, arrived.at[0]),
        pltpu.make_async_copy(mask_hbm, mask, arrived.at[1]),
    ]
    for copy in copies:
        copy.start()
    block = lax.axis_index("pair") * rows // BLK
    low = lax.broadcasted_iota(jnp.int32, (8, 128), 1) < BLK
    for copy in copies:
        copy.wait()
    for i in range(aux // 2):
        tile = x[:, i * 128:(i + 1) * 128].astype(jnp.float32)
        first, last = tile[:8], tile[8:]
        even = jnp.where(low, first, pltpu.roll(last, BLK, 1))
        odd = jnp.where(low, pltpu.roll(first, BLK, 1), last)
        even = jnp.where(mask[block, 2 * i] > 0, even, 0.0)
        odd = jnp.where(mask[block, 2 * i + 1] > 0, odd, 0.0)
        wide[pl.ds(2 * i, 8, stride=aux), :] = even
        wide[pl.ds(2 * i + 1, 8, stride=aux), :] = odd
    for s in range(8):
        lane = s % 2 * 128
        y_ref[s // 2, :, lane:lane + 128] = wide[s * aux:(s + 1) * aux, :].astype(y_ref.dtype)


def arrange(integrals, block_mask, second):
    rows, width = integrals.shape
    aux = width // BLK
    return call(
        functools.partial(arrange_kernel, rows, aux, second),
        "arrange",
        1 << 28,
        out_shape=jax.ShapeDtypeStruct((4, aux, 256), jnp.bfloat16),
        in_specs=[HBM, HBM],
        out_specs=VMEM,
        scratch_shapes=[
            pltpu.VMEM((rows // 2, width), jnp.bfloat16),
            pltpu.SMEM(block_mask.shape, jnp.int32),
            pltpu.VMEM((8 * aux, 128), jnp.float32),
            pltpu.SemaphoreType.DMA((2,)),
        ],
    )(stay(integrals), stay(block_mask))


def through(y, first, second):
    steps, aux, wide = y.shape
    y = y[...].reshape(steps * aux, wide)
    half = jnp.dot(y, first, preferred_element_type=jnp.float32).astype(jnp.bfloat16)
    full = lax.dot_general(half, second, NT_DIMS, preferred_element_type=jnp.float32)
    return full.astype(jnp.bfloat16).reshape(steps, aux, wide)


def core_rows(aux, other):
    core = jnp.bitwise_xor(lax.rem(lax.axis_index("aux"), 2), other)
    return pl.ds(pl.multiple_of(core * aux, aux), aux)


def transform_kernel(nt, rows, atom_hbm, occ_hbm, virt_hbm, y1, y2, z_ref, w_ref, green_ref, *scratch):
    atom_ref, occ_ref, virt_ref, arrived = scratch
    aux, wide = y1.shape[1:]
    copies = wide // BLK
    copy = pltpu.make_async_copy(atom_hbm, atom_ref, arrived.at[0])
    copy.start()
    copy.wait()
    atom = atom_ref[lax.axis_index("pair") * rows // BLK]
    fetch = [
        pltpu.make_async_copy(occ_hbm.at[:, atom], occ_ref, arrived.at[0]),
        pltpu.make_async_copy(virt_hbm.at[:, atom], virt_ref, arrived.at[1]),
    ]
    for copy in fetch:
        copy.start()
    for copy in fetch:
        copy.wait()
    same = (
        lax.broadcasted_iota(jnp.int32, (wide, wide), 0) // BLK
        == lax.broadcasted_iota(jnp.int32, (wide, wide), 1) // BLK
    )

    def diagonal(block):
        tall = jnp.concatenate([block.astype(jnp.float32)] * copies, axis=0)
        full = jnp.concatenate([tall] * copies, axis=1)
        return jnp.where(same, full, 0.0).astype(jnp.bfloat16)

    for t in range(nt):
        occ, virt = diagonal(occ_ref[t]), diagonal(virt_ref[t])
        green_ref[t, 0], green_ref[t, 1] = occ, virt
        for half, y in enumerate((y1, y2)):
            z_ref[half, :, t * aux:(t + 1) * aux, :] = through(y, occ, virt)
            w_ref[half, t, :, core_rows(aux, 0), :] = through(y, virt, occ)


def transform(atom, green_occ, green_virt, rows, own):
    nt = green_occ.shape[0]
    steps, aux, wide = own[0].shape
    return call(
        functools.partial(transform_kernel, nt, rows),
        "transform",
        2 << 30,
        out_shape=(
            jax.ShapeDtypeStruct((2, steps, nt * aux, wide), jnp.bfloat16),
            jax.ShapeDtypeStruct((2, nt, steps, 2 * aux, wide), jnp.bfloat16),
            jax.ShapeDtypeStruct((nt, 2, wide, wide), jnp.bfloat16),
        ),
        in_specs=[HBM] * 3 + [VMEM] * 2,
        out_specs=(VMEM,) * 3,
        scratch_shapes=[
            pltpu.SMEM(atom.shape, jnp.int32),
            pltpu.VMEM((nt, BLK, BLK), jnp.bfloat16),
            pltpu.VMEM((nt, BLK, BLK), jnp.bfloat16),
            pltpu.SemaphoreType.DMA((2,)),
        ],
    )(stay(atom), stay(green_occ), stay(green_virt), *own)


def complete_kernel(before_ref, green_ref, y1, y2, w_ref):
    aux = y1.shape[1]
    for t in range(green_ref.shape[0]):
        for half, y in enumerate((y1, y2)):
            w_ref[half, t, :, core_rows(aux, 1), :] = through(y, green_ref[t, 1], green_ref[t, 0])


def complete(w, greens, sibling):
    return call(
        complete_kernel,
        "complete",
        1 << 30,
        out_shape=jax.ShapeDtypeStruct(w.shape, w.dtype),
        in_specs=[VMEM] * 4,
        out_specs=VMEM,
        input_output_aliases={0: 0},
    )(w, greens, *sibling)


def near_kernel(count, z_ref, *refs):
    mine, other, out_ref = refs[:count], refs[count:2 * count], refs[-1]

    def products(low, high):
        total = jnp.zeros(out_ref.shape, jnp.float32)
        for half, (first, second) in enumerate(zip(low, high)):
            for j in range(z_ref.shape[1]):
                partner = jnp.concatenate([first[j], second[j]], axis=0)
                total += lax.dot_general(z_ref[half, j], partner, NT_DIMS, preferred_element_type=jnp.float32)
        out_ref[...] = total

    core = lax.rem(lax.axis_index("aux"), 2)
    pl.when(core == 0)(lambda: products(mine, other))
    pl.when(core == 1)(lambda: products(other, mine))


def near(z, mine, other):
    size = z.shape[2]
    return call(
        functools.partial(near_kernel, len(mine)),
        "near",
        1 << 29,
        out_shape=jax.ShapeDtypeStruct((size, 2 * mine[0].shape[-2]), jnp.float32),
        in_specs=[VMEM] * (1 + 2 * len(mine)),
        out_specs=VMEM,
    )(z, *mine, *other)


def fold(x):
    high = x.shape[0] // 2
    past = jnp.concatenate([x[:high, 128:], x[high:, 128:]], axis=1)
    return jnp.concatenate([x[:, :128], past], axis=0)


def unfold(x):
    high = x.shape[0] // 3
    past = x[2 * high:]
    past = jnp.concatenate([past[:, :BLK], past[:, BLK:]], axis=0)
    return jnp.concatenate([x[:2 * high], past], axis=1)


def far_kernel(w_ref, *refs):
    mine, out_ref = refs[:-1], refs[-1]
    nt, steps = w_ref.shape[1:3]
    aux = mine[0].shape[1]
    shares = []
    for t in range(nt):
        total = jnp.zeros((aux, w_ref.shape[3]), jnp.float32)
        for half, piece in enumerate(mine):
            for j in range(steps):
                total += lax.dot_general(piece[j], w_ref[half, t, j], NT_DIMS, preferred_element_type=jnp.float32)
        shares.append(total)
    out_ref[...] = fold(jnp.concatenate(shares, axis=0)).astype(out_ref.dtype)


def far(w, mine):
    aux = mine[0].shape[1]
    return call(
        far_kernel,
        "far",
        1 << 29,
        out_shape=jax.ShapeDtypeStruct((w.shape[1] * aux * 3 // 2, 128), jnp.bfloat16),
        in_specs=[VMEM] * (1 + len(mine)),
        out_specs=VMEM,
    )(w, *mine)


def pack_kernel(chips, pairs, *refs):
    backs, aheads = refs[:chips // 2 + 1], refs[chips // 2 + 1:chips]
    outs, shares = refs[chips:-1], refs[-1]
    chip = chip_of()
    for step in range(chips // 2 + 1):
        shares[lax.rem(chip + chips - step, chips)] = fold(backs[step][...])
    for step in range(1, chips // 2):
        shares[lax.rem(chip + step, chips)] = aheads[step - 1][...].astype(jnp.float32)
    if pairs is None:
        for q in range(chips):
            outs[0][q] = unfold(shares[q]).astype(jnp.bfloat16)
    else:
        pair = lax.axis_index("pair")
        for j, out_ref in enumerate(outs):
            out_ref[...] = shares[lax.bitwise_xor(pair, j)].astype(out_ref.dtype)


def pack(chips, pairs, backs, aheads):
    height, width = backs[0].shape
    folded = (height * 3 // 2, 128)
    if pairs is None:
        out_shape = (jax.ShapeDtypeStruct((chips, height, width), jnp.bfloat16),)
    else:
        out_shape = (jax.ShapeDtypeStruct(folded, jnp.float32),)
        out_shape += (jax.ShapeDtypeStruct(folded, jnp.bfloat16),) * (pairs - 1)
    return call(
        functools.partial(pack_kernel, chips, pairs),
        "pack",
        1 << 28,
        out_shape=out_shape,
        in_specs=[VMEM] * chips,
        out_specs=(VMEM,) * len(out_shape),
        scratch_shapes=[pltpu.VMEM((chips,) + folded, jnp.float32)],
    )(*backs, *aheads)


def finish_kernel(scale, nt, folded, weight_ref, *refs):
    parts, (chi_ref, sum_ref) = refs[:-2], refs[-2:]
    aux = chi_ref.shape[1]
    if folded:
        total = parts[0][...]
        for part in parts[1:]:
            total += part[...].astype(jnp.float32)
        total = unfold(total * scale)
    else:
        total = parts[0][0].astype(jnp.float32)
        for p in range(1, parts[0].shape[0]):
            total += parts[0][p].astype(jnp.float32)
        total *= scale
    local = jnp.zeros((1, 1), jnp.float32)
    for t in range(nt):
        chi = total[t * aux:(t + 1) * aux]
        chi_ref[t] = chi
        local += weight_ref[t] * jnp.sum(chi * chi, keepdims=True)
    sum_ref[...] = jnp.broadcast_to(local, sum_ref.shape)


def finish(scale, time_weights, parts, chi_shape, copies):
    return call(
        functools.partial(finish_kernel, scale, chi_shape[0], len(parts) > 1),
        "finish",
        1 << 28,
        out_shape=(
            jax.ShapeDtypeStruct(chi_shape, jnp.float32),
            jax.ShapeDtypeStruct((copies, 128), jnp.float32),
        ),
        in_specs=[SMEM] + [VMEM] * len(parts),
        out_specs=(VMEM, VMEM),
    )(time_weights, *parts)


def per_device(integrals, block_mask, block_atom, green_occ, green_virt, time_weights):
    rows = integrals.shape[0]
    aux_here = integrals.shape[1] // BLK
    pairs, auxes = lax.axis_size("pair"), lax.axis_size("aux")
    chips = auxes // 2
    aux_total = aux_here * auxes
    columns = aux_total // pairs
    nt = green_occ.shape[0]

    def along(shift):
        return [(i, (i + 2 * shift) % auxes) for i in range(auxes)]

    def to_sibling(array):
        return lax.ppermute(array, "aux", [(i, i ^ 1) for i in range(auxes)])

    own = [arrange(integrals, block_mask, second) for second in (False, True)]
    arriving = [lax.ppermute(a, "aux", along(1)) for a in own]
    z, w, greens = transform(block_atom, green_occ, green_virt, rows, own)
    *later, z = lax.optimization_barrier((*own, z))
    arriving[0], z = lax.optimization_barrier((arriving[0], z))
    sibling = [to_sibling(a) for a in later]
    w = complete(w, greens, sibling)
    backs, aheads = [], []
    for step in range(1, chips // 2 + 1):
        held, last = arriving, step == chips // 2
        if not last:
            arriving = [lax.ppermute(a, "aux", along(1)) for a in held]
        if last:
            backs.append(near(z, held, [to_sibling(a) for a in held]))
            continue
        other = [to_sibling(a) for a in held]
        share = far(w, held)
        ahead = lax.ppermute(share, "aux", along(-step))
        if step == 1:
            backs.append(near(z, own, sibling))
        backs.append(near(z, held, other))
        *arriving, ahead, backs[-1], backs[-2] = lax.optimization_barrier((*arriving, ahead, backs[-1], backs[-2]))
        aheads.append(ahead)
    if columns == 2 * aux_here and pairs & (pairs - 1) == 0:
        mine, *sends = pack(chips, pairs, backs, aheads)
        parts = [mine]
        for j in range(pairs - 1, 0, -1):
            parts.append(lax.ppermute(sends[j - 1], "pair", [(i, i ^ j) for i in range(pairs)]))
    else:
        (shares,) = pack(chips, None, backs, aheads)
        shares = shares.transpose(1, 0, 2).reshape(nt * aux_here, pairs, columns).transpose(1, 0, 2)
        parts = [lax.all_to_all(shares, "pair", 0, 0)]
    scale = float((rows * pairs * BLK) ** -0.5)
    chi, sums = finish(scale, time_weights, parts, (nt, aux_here, columns), pairs * auxes)
    total = jnp.sum(lax.all_to_all(sums, ("pair", "aux"), 0, 0, tiled=True)[:, 0])
    energy = -total / jnp.float32(aux_total * aux_total)
    return chi, energy


def solution(mesh):
    placed = (P("pair", "aux"), P(None, "aux"), P(), P(), P(), P())
    return jax.shard_map(
        per_device,
        mesh=mesh,
        in_specs=placed,
        out_specs=(P(None, "aux", "pair"), P()),
        check_vma=False,
    )
```

```python
import functools
import jax
import jax.numpy as jnp
from jax import lax
from jax.experimental import pallas as pl
from jax.experimental.pallas import tpu as pltpu
from jax.sharding import PartitionSpec as P

BLK = 64
VMEM = pl.BlockSpec(memory_space=pltpu.VMEM)
SMEM = pl.BlockSpec(memory_space=pltpu.SMEM)
HBM = pl.BlockSpec(memory_space=pltpu.HBM)
NT_DIMS = (((1,), (1,)), ((), ()))


def call(kernel, name, flops, **settings):
    return pl.pallas_call(
        kernel,
        name=name,
        compiler_params=pltpu.CompilerParams(vmem_limit_bytes=40 * 1024 * 1024),
        cost_estimate=pl.CostEstimate(flops=flops, bytes_accessed=1 << 8, transcendentals=0),
        **settings,
    )


def stay(array):
    return pltpu.with_memory_space_constraint(array, pltpu.HBM)


def chip_of():
    return lax.axis_index("aux") // 2


def arrange_kernel(rows, aux, second, x_hbm, mask_hbm, y_ref, x, mask, wide, arrived):
    copies = [
        pltpu.make_async_copy(x_hbm.at[pl.ds(second * (rows // 2), rows // 2)], x, arrived.at[0]),
        pltpu.make_async_copy(mask_hbm, mask, arrived.at[1]),
    ]
    for copy in copies:
        copy.start()
    block = lax.axis_index("pair") * rows // BLK
    low = lax.broadcasted_iota(jnp.int32, (8, 128), 1) < BLK
    for copy in copies:
        copy.wait()
    for i in range(aux // 2):
        tile = x[:, i * 128:(i + 1) * 128].astype(jnp.float32)
        first, last = tile[:8], tile[8:]
        even = jnp.where(low, first, pltpu.roll(last, BLK, 1))
        odd = jnp.where(low, pltpu.roll(first, BLK, 1), last)
        even = jnp.where(mask[block, 2 * i] > 0, even, 0.0)
        odd = jnp.where(mask[block, 2 * i + 1] > 0, odd, 0.0)
        wide[pl.ds(2 * i, 8, stride=aux + 1), :] = even
        wide[pl.ds(2 * i + 1, 8, stride=aux + 1), :] = odd
    for s in range(8):
        lane = s % 2 * 128
        y_ref[s // 2, :, lane:lane + 128] = wide[s * (aux + 1):s * (aux + 1) + aux, :].astype(y_ref.dtype)


def arrange(integrals, block_mask, second):
    rows, width = integrals.shape
    aux = width // BLK
    return call(
        functools.partial(arrange_kernel, rows, aux, second),
        "arrange",
        1 << 28,
        out_shape=jax.ShapeDtypeStruct((4, aux, 256), jnp.bfloat16),
        in_specs=[HBM, HBM],
        out_specs=VMEM,
        scratch_shapes=[
            pltpu.VMEM((rows // 2, width), jnp.bfloat16),
            pltpu.SMEM(block_mask.shape, jnp.int32),
            pltpu.VMEM((8 * (aux + 1), 128), jnp.float32),
            pltpu.SemaphoreType.DMA((2,)),
        ],
    )(stay(integrals), stay(block_mask))


def through(y, first, second):
    steps, aux, wide = y.shape
    y = y[...].reshape(steps * aux, wide)
    half = jnp.dot(y, first, preferred_element_type=jnp.float32).astype(jnp.bfloat16)
    full = lax.dot_general(half, second, NT_DIMS, preferred_element_type=jnp.float32)
    return full.astype(jnp.bfloat16).reshape(steps, aux, wide)


def core_rows(aux, other):
    core = jnp.bitwise_xor(lax.rem(lax.axis_index("aux"), 2), other)
    return pl.ds(pl.multiple_of(core * aux, aux), aux)


def transform_kernel(nt, rows, atom_hbm, occ_hbm, virt_hbm, y1, y2, z_ref, w_ref, green_ref, *scratch):
    atom_ref, occ_ref, virt_ref, arrived = scratch
    aux, wide = y1.shape[1:]
    copies = wide // BLK
    copy = pltpu.make_async_copy(atom_hbm, atom_ref, arrived.at[0])
    copy.start()
    copy.wait()
    atom = atom_ref[lax.axis_index("pair") * rows // BLK]
    fetch = [
        pltpu.make_async_copy(occ_hbm.at[:, atom], occ_ref, arrived.at[0]),
        pltpu.make_async_copy(virt_hbm.at[:, atom], virt_ref, arrived.at[1]),
    ]
    for copy in fetch:
        copy.start()
    for copy in fetch:
        copy.wait()
    same = (
        lax.broadcasted_iota(jnp.int32, (wide, wide), 0) // BLK
        == lax.broadcasted_iota(jnp.int32, (wide, wide), 1) // BLK
    )

    def diagonal(block):
        tall = jnp.concatenate([block.astype(jnp.float32)] * copies, axis=0)
        full = jnp.concatenate([tall] * copies, axis=1)
        return jnp.where(same, full, 0.0).astype(jnp.bfloat16)

    for t in range(nt):
        occ, virt = diagonal(occ_ref[t]), diagonal(virt_ref[t])
        green_ref[t, 0], green_ref[t, 1] = occ, virt
        for half, y in enumerate((y1, y2)):
            z_ref[half, :, t * aux:(t + 1) * aux, :] = through(y, occ, virt)
            w_ref[half, t, :, core_rows(aux, 0), :] = through(y, virt, occ)


def transform(atom, green_occ, green_virt, rows, own):
    nt = green_occ.shape[0]
    steps, aux, wide = own[0].shape
    return call(
        functools.partial(transform_kernel, nt, rows),
        "transform",
        2 << 30,
        out_shape=(
            jax.ShapeDtypeStruct((2, steps, nt * aux, wide), jnp.bfloat16),
            jax.ShapeDtypeStruct((2, nt, steps, 2 * aux, wide), jnp.bfloat16),
            jax.ShapeDtypeStruct((nt, 2, wide, wide), jnp.bfloat16),
        ),
        in_specs=[HBM] * 3 + [VMEM] * 2,
        out_specs=(VMEM,) * 3,
        scratch_shapes=[
            pltpu.SMEM(atom.shape, jnp.int32),
            pltpu.VMEM((nt, BLK, BLK), jnp.bfloat16),
            pltpu.VMEM((nt, BLK, BLK), jnp.bfloat16),
            pltpu.SemaphoreType.DMA((2,)),
        ],
    )(stay(atom), stay(green_occ), stay(green_virt), *own)


def complete_kernel(before_ref, green_ref, y1, y2, w_ref):
    aux = y1.shape[1]
    for t in range(green_ref.shape[0]):
        for half, y in enumerate((y1, y2)):
            w_ref[half, t, :, core_rows(aux, 1), :] = through(y, green_ref[t, 1], green_ref[t, 0])


def complete(w, greens, sibling):
    return call(
        complete_kernel,
        "complete",
        1 << 30,
        out_shape=jax.ShapeDtypeStruct(w.shape, w.dtype),
        in_specs=[VMEM] * 4,
        out_specs=VMEM,
        input_output_aliases={0: 0},
    )(w, greens, *sibling)


def near_kernel(count, z_ref, *refs):
    mine, other, out_ref = refs[:count], refs[count:2 * count], refs[-1]

    def products(low, high):
        total = jnp.zeros(out_ref.shape, jnp.float32)
        for half, (first, second) in enumerate(zip(low, high)):
            for j in range(z_ref.shape[1]):
                partner = jnp.concatenate([first[j], second[j]], axis=0)
                total += lax.dot_general(z_ref[half, j], partner, NT_DIMS, preferred_element_type=jnp.float32)
        out_ref[...] = total

    core = lax.rem(lax.axis_index("aux"), 2)
    pl.when(core == 0)(lambda: products(mine, other))
    pl.when(core == 1)(lambda: products(other, mine))


def near(z, mine, other):
    size = z.shape[2]
    return call(
        functools.partial(near_kernel, len(mine)),
        "near",
        1 << 29,
        out_shape=jax.ShapeDtypeStruct((size, 2 * mine[0].shape[-2]), jnp.float32),
        in_specs=[VMEM] * (1 + 2 * len(mine)),
        out_specs=VMEM,
    )(z, *mine, *other)


def fold(x):
    high = x.shape[0] // 2
    past = jnp.concatenate([x[:high, 128:], x[high:, 128:]], axis=1)
    return jnp.concatenate([x[:, :128], past], axis=0)


def unfold(x):
    high = x.shape[0] // 3
    past = x[2 * high:]
    past = jnp.concatenate([past[:, :BLK], past[:, BLK:]], axis=0)
    return jnp.concatenate([x[:2 * high], past], axis=1)


def far_kernel(w_ref, *refs):
    mine, out_ref = refs[:-1], refs[-1]
    nt, steps = w_ref.shape[1:3]
    aux = mine[0].shape[1]
    shares = []
    for t in range(nt):
        total = jnp.zeros((aux, w_ref.shape[3]), jnp.float32)
        for half, piece in enumerate(mine):
            for j in range(steps):
                total += lax.dot_general(piece[j], w_ref[half, t, j], NT_DIMS, preferred_element_type=jnp.float32)
        shares.append(total)
    out_ref[...] = fold(jnp.concatenate(shares, axis=0)).astype(out_ref.dtype)


def far(w, mine):
    aux = mine[0].shape[1]
    return call(
        far_kernel,
        "far",
        1 << 29,
        out_shape=jax.ShapeDtypeStruct((w.shape[1] * aux * 3 // 2, 128), jnp.bfloat16),
        in_specs=[VMEM] * (1 + len(mine)),
        out_specs=VMEM,
    )(w, *mine)


def pack_kernel(chips, pairs, *refs):
    backs, aheads = refs[:chips // 2 + 1], refs[chips // 2 + 1:chips]
    outs, shares = refs[chips:-1], refs[-1]
    chip = chip_of()
    for step in range(chips // 2 + 1):
        shares[lax.rem(chip + chips - step, chips)] = fold(backs[step][...])
    for step in range(1, chips // 2):
        shares[lax.rem(chip + step, chips)] = aheads[step - 1][...].astype(jnp.float32)
    if pairs is None:
        for q in range(chips):
            outs[0][q] = unfold(shares[q]).astype(jnp.bfloat16)
    else:
        pair = lax.axis_index("pair")
        for j, out_ref in enumerate(outs):
            out_ref[...] = shares[lax.bitwise_xor(pair, j)].astype(out_ref.dtype)


def pack(chips, pairs, backs, aheads):
    height, width = backs[0].shape
    folded = (height * 3 // 2, 128)
    if pairs is None:
        out_shape = (jax.ShapeDtypeStruct((chips, height, width), jnp.bfloat16),)
    else:
        out_shape = (jax.ShapeDtypeStruct(folded, jnp.float32),)
        out_shape += (jax.ShapeDtypeStruct(folded, jnp.bfloat16),) * (pairs - 1)
    return call(
        functools.partial(pack_kernel, chips, pairs),
        "pack",
        1 << 28,
        out_shape=out_shape,
        in_specs=[VMEM] * chips,
        out_specs=(VMEM,) * len(out_shape),
        scratch_shapes=[pltpu.VMEM((chips,) + folded, jnp.float32)],
    )(*backs, *aheads)


def finish_kernel(scale, nt, folded, weight_ref, *refs):
    parts, (chi_hbm, sum_ref, chi_ref, leaving) = refs[:-4], refs[-4:]
    aux = chi_ref.shape[1]
    if folded:
        total = parts[0][...]
        for part in parts[1:]:
            total += part[...].astype(jnp.float32)
        total = unfold(total * scale)
    else:
        total = parts[0][0].astype(jnp.float32)
        for p in range(1, parts[0].shape[0]):
            total += parts[0][p].astype(jnp.float32)
        total *= scale
    for t in range(nt):
        chi_ref[t] = total[t * aux:(t + 1) * aux]
    copy = pltpu.make_async_copy(chi_ref, chi_hbm, leaving)
    copy.start()
    local = jnp.zeros((1, 1), jnp.float32)
    for t in range(nt):
        chi = total[t * aux:(t + 1) * aux]
        local += weight_ref[:, t:t + 1] * jnp.sum(chi * chi, keepdims=True)
    sum_ref[...] = jnp.broadcast_to(local, sum_ref.shape)
    copy.wait()


def finish(scale, time_weights, parts, chi_shape, copies):
    return call(
        functools.partial(finish_kernel, scale, chi_shape[0], len(parts) > 1),
        "finish",
        1 << 28,
        out_shape=(
            jax.ShapeDtypeStruct(chi_shape, jnp.float32),
            jax.ShapeDtypeStruct((copies, 128), jnp.float32),
        ),
        in_specs=[VMEM] * (1 + len(parts)),
        out_specs=(HBM, VMEM),
        scratch_shapes=[pltpu.VMEM(chi_shape, jnp.float32), pltpu.SemaphoreType.DMA],
    )(time_weights[None], *parts)


def per_device(integrals, block_mask, block_atom, green_occ, green_virt, time_weights):
    rows = integrals.shape[0]
    aux_here = integrals.shape[1] // BLK
    pairs, auxes = lax.axis_size("pair"), lax.axis_size("aux")
    chips = auxes // 2
    aux_total = aux_here * auxes
    columns = aux_total // pairs
    nt = green_occ.shape[0]

    def along(shift):
        return [(i, (i + 2 * shift) % auxes) for i in range(auxes)]

    def to_sibling(array):
        return lax.ppermute(array, "aux", [(i, i ^ 1) for i in range(auxes)])

    own = [arrange(integrals, block_mask, second) for second in (False, True)]
    arriving = [lax.ppermute(a, "aux", along(1)) for a in own]
    z, w, greens = transform(block_atom, green_occ, green_virt, rows, own)
    *later, z = lax.optimization_barrier((*own, z))
    arriving[0], z = lax.optimization_barrier((arriving[0], z))
    sibling = [to_sibling(a) for a in later]
    w = complete(w, greens, sibling)
    backs, aheads = [], []
    for step in range(1, chips // 2 + 1):
        held, last = arriving, step == chips // 2
        if not last:
            arriving = [lax.ppermute(a, "aux", along(1)) for a in held]
        if last:
            backs.append(near(z, held, [to_sibling(a) for a in held]))
            continue
        other = [to_sibling(a) for a in held]
        share = far(w, held)
        ahead = lax.ppermute(share, "aux", along(-step))
        if step == 1:
            backs.append(near(z, own, sibling))
        backs.append(near(z, held, other))
        *arriving, ahead, backs[-1], backs[-2] = lax.optimization_barrier((*arriving, ahead, backs[-1], backs[-2]))
        aheads.append(ahead)
    if columns == 2 * aux_here and pairs & (pairs - 1) == 0:
        mine, *sends = pack(chips, pairs, backs, aheads)
        parts = [mine]
        for j in range(pairs - 1, 0, -1):
            parts.append(lax.ppermute(sends[j - 1], "pair", [(i, i ^ j) for i in range(pairs)]))
    else:
        (shares,) = pack(chips, None, backs, aheads)
        shares = shares.transpose(1, 0, 2).reshape(nt * aux_here, pairs, columns).transpose(1, 0, 2)
        parts = [lax.all_to_all(shares, "pair", 0, 0)]
    scale = float((rows * pairs * BLK) ** -0.5)
    chi, sums = finish(scale, time_weights, parts, (nt, aux_here, columns), pairs * auxes)
    total = jnp.sum(lax.all_to_all(sums, ("pair", "aux"), 0, 0, tiled=True)[:, 0])
    energy = -total / jnp.float32(aux_total * aux_total)
    return chi, energy


def solution(mesh):
    placed = (P("pair", "aux"), P(None, "aux"), P(), P(), P(), P())
    return jax.shard_map(
        per_device,
        mesh=mesh,
        in_specs=placed,
        out_specs=(P(None, "aux", "pair"), P()),
        check_vma=False,
    )
```

```python
import functools
import jax
import jax.numpy as jnp
from jax import lax
from jax.experimental import pallas as pl
from jax.experimental.pallas import tpu as pltpu
from jax.sharding import PartitionSpec as P

BLK = 64
VMEM = pl.BlockSpec(memory_space=pltpu.VMEM)
SMEM = pl.BlockSpec(memory_space=pltpu.SMEM)
HBM = pl.BlockSpec(memory_space=pltpu.HBM)
NT_DIMS = (((1,), (1,)), ((), ()))


def call(kernel, name, flops, **settings):
    return pl.pallas_call(
        kernel,
        name=name,
        compiler_params=pltpu.CompilerParams(vmem_limit_bytes=40 * 1024 * 1024),
        cost_estimate=pl.CostEstimate(flops=flops, bytes_accessed=1 << 8, transcendentals=0),
        **settings,
    )


def stay(array):
    return pltpu.with_memory_space_constraint(array, pltpu.HBM)


def chip_of():
    return lax.axis_index("aux") // 2


def arrange_kernel(rows, aux, second, x_hbm, mask_hbm, y_ref, x, mask, wide, arrived):
    copies = [
        pltpu.make_async_copy(x_hbm.at[pl.ds(second * (rows // 2), rows // 2)], x, arrived.at[0]),
        pltpu.make_async_copy(mask_hbm, mask, arrived.at[1]),
    ]
    for copy in copies:
        copy.start()
    block = lax.axis_index("pair") * rows // BLK
    low = lax.broadcasted_iota(jnp.int32, (8, 128), 1) < BLK
    for copy in copies:
        copy.wait()
    for i in range(aux // 2):
        tile = x[:, i * 128:(i + 1) * 128].astype(jnp.float32)
        first, last = tile[:8], tile[8:]
        even = jnp.where(low, first, pltpu.roll(last, BLK, 1))
        odd = jnp.where(low, pltpu.roll(first, BLK, 1), last)
        even = jnp.where(mask[block, 2 * i] > 0, even, 0.0)
        odd = jnp.where(mask[block, 2 * i + 1] > 0, odd, 0.0)
        wide[pl.ds(2 * i, 8, stride=aux + 1), :] = even
        wide[pl.ds(2 * i + 1, 8, stride=aux + 1), :] = odd
    for s in range(8):
        lane = s % 2 * 128
        y_ref[s // 2, :, lane:lane + 128] = wide[s * (aux + 1):s * (aux + 1) + aux, :].astype(y_ref.dtype)


def arrange(integrals, block_mask, second):
    rows, width = integrals.shape
    aux = width // BLK
    return call(
        functools.partial(arrange_kernel, rows, aux, second),
        "arrange",
        1 << 28,
        out_shape=jax.ShapeDtypeStruct((4, aux, 256), jnp.bfloat16),
        in_specs=[HBM, HBM],
        out_specs=VMEM,
        scratch_shapes=[
            pltpu.VMEM((rows // 2, width), jnp.bfloat16),
            pltpu.SMEM(block_mask.shape, jnp.int32),
            pltpu.VMEM((8 * (aux + 1), 128), jnp.float32),
            pltpu.SemaphoreType.DMA((2,)),
        ],
    )(stay(integrals), stay(block_mask))


def through(y, first, second):
    steps, aux, wide = y.shape
    y = y[...].reshape(steps * aux, wide)
    half = jnp.dot(y, first, preferred_element_type=jnp.float32).astype(jnp.bfloat16)
    full = lax.dot_general(half, second, NT_DIMS, preferred_element_type=jnp.float32)
    return full.astype(jnp.bfloat16).reshape(steps, aux, wide)


def core_rows(aux, other):
    core = jnp.bitwise_xor(lax.rem(lax.axis_index("aux"), 2), other)
    return pl.ds(pl.multiple_of(core * aux, aux), aux)


def transform_kernel(nt, rows, atom_hbm, occ_hbm, virt_hbm, y1, y2, z_ref, w_ref, green_ref, *scratch):
    atom_ref, occ_ref, virt_ref, arrived = scratch
    aux, wide = y1.shape[1:]
    copies = wide // BLK
    copy = pltpu.make_async_copy(atom_hbm, atom_ref, arrived.at[0])
    copy.start()
    copy.wait()
    atom = atom_ref[lax.axis_index("pair") * rows // BLK]
    fetch = [
        pltpu.make_async_copy(occ_hbm.at[:, atom], occ_ref, arrived.at[0]),
        pltpu.make_async_copy(virt_hbm.at[:, atom], virt_ref, arrived.at[1]),
    ]
    for copy in fetch:
        copy.start()
    for copy in fetch:
        copy.wait()
    same = (
        lax.broadcasted_iota(jnp.int32, (wide, wide), 0) // BLK
        == lax.broadcasted_iota(jnp.int32, (wide, wide), 1) // BLK
    )

    def diagonal(block):
        tall = jnp.concatenate([block.astype(jnp.float32)] * copies, axis=0)
        full = jnp.concatenate([tall] * copies, axis=1)
        return jnp.where(same, full, 0.0).astype(jnp.bfloat16)

    for t in range(nt):
        occ, virt = diagonal(occ_ref[t]), diagonal(virt_ref[t])
        green_ref[t, 0], green_ref[t, 1] = occ, virt
        for half, y in enumerate((y1, y2)):
            z_ref[half, :, t * aux:(t + 1) * aux, :] = through(y, occ, virt)
            w_ref[half, t, :, core_rows(aux, 0), :] = through(y, virt, occ)


def transform(atom, green_occ, green_virt, rows, own):
    nt = green_occ.shape[0]
    steps, aux, wide = own[0].shape
    return call(
        functools.partial(transform_kernel, nt, rows),
        "transform",
        2 << 30,
        out_shape=(
            jax.ShapeDtypeStruct((2, steps, nt * aux, wide), jnp.bfloat16),
            jax.ShapeDtypeStruct((2, nt, steps, 2 * aux, wide), jnp.bfloat16),
            jax.ShapeDtypeStruct((nt, 2, wide, wide), jnp.bfloat16),
        ),
        in_specs=[HBM] * 3 + [VMEM] * 2,
        out_specs=(VMEM,) * 3,
        scratch_shapes=[
            pltpu.SMEM(atom.shape, jnp.int32),
            pltpu.VMEM((nt, BLK, BLK), jnp.bfloat16),
            pltpu.VMEM((nt, BLK, BLK), jnp.bfloat16),
            pltpu.SemaphoreType.DMA((2,)),
        ],
    )(stay(atom), stay(green_occ), stay(green_virt), *own)


def complete_kernel(before_ref, green_ref, y1, y2, w_ref):
    aux = y1.shape[1]
    for t in range(green_ref.shape[0]):
        for half, y in enumerate((y1, y2)):
            w_ref[half, t, :, core_rows(aux, 1), :] = through(y, green_ref[t, 1], green_ref[t, 0])


def complete(w, greens, sibling):
    return call(
        complete_kernel,
        "complete",
        1 << 30,
        out_shape=jax.ShapeDtypeStruct(w.shape, w.dtype),
        in_specs=[VMEM] * 4,
        out_specs=VMEM,
        input_output_aliases={0: 0},
    )(w, greens, *sibling)


def mirror_kernel(green_ref, y1, y2, z_ref):
    aux = y1.shape[1]
    for t in range(green_ref.shape[0]):
        for half, y in enumerate((y1, y2)):
            z_ref[half, :, t * aux:(t + 1) * aux, :] = through(y, green_ref[t, 0], green_ref[t, 1])


def mirror(greens, sibling):
    steps, aux, wide = sibling[0].shape
    return call(
        mirror_kernel,
        "mirror",
        1 << 29,
        out_shape=jax.ShapeDtypeStruct((2, steps, greens.shape[0] * aux, wide), jnp.bfloat16),
        in_specs=[VMEM] * 3,
        out_specs=VMEM,
    )(greens, *sibling)


def both_kernel(z_ref, sibling_ref, y1, y2, mine_ref, theirs_ref):
    for operand, out_ref in ((sibling_ref, theirs_ref), (z_ref, mine_ref)):
        total = jnp.zeros(out_ref.shape, jnp.float32)
        for half, y in enumerate((y1, y2)):
            for j in range(y.shape[0]):
                total += lax.dot_general(operand[half, j], y[j], NT_DIMS, preferred_element_type=jnp.float32)
        out_ref[...] = total


def both(z, z_sibling, pieces):
    share = jax.ShapeDtypeStruct((z.shape[2], pieces[0].shape[1]), jnp.float32)
    return call(
        both_kernel,
        "both",
        1 << 29,
        out_shape=(share, share),
        in_specs=[VMEM] * 4,
        out_specs=(VMEM, VMEM),
    )(z, z_sibling, *pieces)


def near_kernel(count, z_ref, *refs):
    mine, other, out_ref = refs[:count], refs[count:2 * count], refs[-1]

    def products(low, high):
        total = jnp.zeros(out_ref.shape, jnp.float32)
        for half, (first, second) in enumerate(zip(low, high)):
            for j in range(z_ref.shape[1]):
                partner = jnp.concatenate([first[j], second[j]], axis=0)
                total += lax.dot_general(z_ref[half, j], partner, NT_DIMS, preferred_element_type=jnp.float32)
        out_ref[...] = total

    core = lax.rem(lax.axis_index("aux"), 2)
    pl.when(core == 0)(lambda: products(mine, other))
    pl.when(core == 1)(lambda: products(other, mine))


def near(z, mine, other):
    size = z.shape[2]
    return call(
        functools.partial(near_kernel, len(mine)),
        "near",
        1 << 29,
        out_shape=jax.ShapeDtypeStruct((size, 2 * mine[0].shape[-2]), jnp.float32),
        in_specs=[VMEM] * (1 + 2 * len(mine)),
        out_specs=VMEM,
    )(z, *mine, *other)


def fold(x):
    high = x.shape[0] // 2
    past = jnp.concatenate([x[:high, 128:], x[high:, 128:]], axis=1)
    return jnp.concatenate([x[:, :128], past], axis=0)


def unfold(x):
    high = x.shape[0] // 3
    past = x[2 * high:]
    past = jnp.concatenate([past[:, :BLK], past[:, BLK:]], axis=0)
    return jnp.concatenate([x[:2 * high], past], axis=1)


def far_kernel(w_ref, *refs):
    mine, out_ref = refs[:-1], refs[-1]
    nt, steps = w_ref.shape[1:3]
    aux = mine[0].shape[1]
    shares = []
    for t in range(nt):
        total = jnp.zeros((aux, w_ref.shape[3]), jnp.float32)
        for half, piece in enumerate(mine):
            for j in range(steps):
                total += lax.dot_general(piece[j], w_ref[half, t, j], NT_DIMS, preferred_element_type=jnp.float32)
        shares.append(total)
    out_ref[...] = fold(jnp.concatenate(shares, axis=0)).astype(out_ref.dtype)


def far(w, mine):
    aux = mine[0].shape[1]
    return call(
        far_kernel,
        "far",
        1 << 29,
        out_shape=jax.ShapeDtypeStruct((w.shape[1] * aux * 3 // 2, 128), jnp.bfloat16),
        in_specs=[VMEM] * (1 + len(mine)),
        out_specs=VMEM,
    )(w, *mine)


def pack_kernel(chips, pairs, *refs):
    backs, aheads = refs[:chips // 2], refs[chips // 2 + 2:chips + 1]
    mine, other = refs[chips // 2][...], refs[chips // 2 + 1][...]
    outs, shares = refs[chips + 1:-1], refs[-1]
    chip = chip_of()
    for step in range(chips // 2):
        shares[lax.rem(chip + chips - step, chips)] = fold(backs[step][...])
    first = lax.rem(lax.axis_index("aux"), 2) == 0
    pieces = [jnp.where(first, mine, other), jnp.where(first, other, mine)]
    shares[lax.rem(chip + chips // 2, chips)] = fold(jnp.concatenate(pieces, axis=1))
    for step in range(1, chips // 2):
        shares[lax.rem(chip + step, chips)] = aheads[step - 1][...].astype(jnp.float32)
    if pairs is None:
        for q in range(chips):
            outs[0][q] = unfold(shares[q]).astype(jnp.bfloat16)
    else:
        pair = lax.axis_index("pair")
        for j, out_ref in enumerate(outs):
            out_ref[...] = shares[lax.bitwise_xor(pair, j)].astype(out_ref.dtype)


def pack(chips, pairs, backs, aheads):
    height, width = backs[0].shape
    folded = (height * 3 // 2, 128)
    if pairs is None:
        out_shape = (jax.ShapeDtypeStruct((chips, height, width), jnp.bfloat16),)
    else:
        out_shape = (jax.ShapeDtypeStruct(folded, jnp.float32),)
        out_shape += (jax.ShapeDtypeStruct(folded, jnp.bfloat16),) * (pairs - 1)
    return call(
        functools.partial(pack_kernel, chips, pairs),
        "pack",
        1 << 28,
        out_shape=out_shape,
        in_specs=[VMEM] * (chips + 1),
        out_specs=(VMEM,) * len(out_shape),
        scratch_shapes=[pltpu.VMEM((chips,) + folded, jnp.float32)],
    )(*backs, *aheads)


def finish_kernel(scale, nt, folded, weight_ref, *refs):
    parts, (chi_hbm, sum_ref, chi_ref, leaving) = refs[:-4], refs[-4:]
    aux = chi_ref.shape[1]
    if folded:
        total = parts[0][...]
        for part in parts[1:]:
            total += part[...].astype(jnp.float32)
        total = unfold(total * scale)
    else:
        total = parts[0][0].astype(jnp.float32)
        for p in range(1, parts[0].shape[0]):
            total += parts[0][p].astype(jnp.float32)
        total *= scale
    for t in range(nt):
        chi_ref[t] = total[t * aux:(t + 1) * aux]
    copy = pltpu.make_async_copy(chi_ref, chi_hbm, leaving)
    copy.start()
    local = jnp.zeros((1, 1), jnp.float32)
    for t in range(nt):
        chi = total[t * aux:(t + 1) * aux]
        local += weight_ref[:, t:t + 1] * jnp.sum(chi * chi, keepdims=True)
    sum_ref[...] = jnp.broadcast_to(local, sum_ref.shape)
    copy.wait()


def finish(scale, time_weights, parts, chi_shape, copies):
    return call(
        functools.partial(finish_kernel, scale, chi_shape[0], len(parts) > 1),
        "finish",
        1 << 28,
        out_shape=(
            jax.ShapeDtypeStruct(chi_shape, jnp.float32),
            jax.ShapeDtypeStruct((copies, 128), jnp.float32),
        ),
        in_specs=[VMEM] * (1 + len(parts)),
        out_specs=(HBM, VMEM),
        scratch_shapes=[pltpu.VMEM(chi_shape, jnp.float32), pltpu.SemaphoreType.DMA],
    )(time_weights[None], *parts)


def per_device(integrals, block_mask, block_atom, green_occ, green_virt, time_weights):
    rows = integrals.shape[0]
    aux_here = integrals.shape[1] // BLK
    pairs, auxes = lax.axis_size("pair"), lax.axis_size("aux")
    chips = auxes // 2
    aux_total = aux_here * auxes
    columns = aux_total // pairs
    nt = green_occ.shape[0]

    def along(shift):
        return [(i, (i + 2 * shift) % auxes) for i in range(auxes)]

    def to_sibling(array):
        return lax.ppermute(array, "aux", [(i, i ^ 1) for i in range(auxes)])

    own = [arrange(integrals, block_mask, second) for second in (False, True)]
    arriving = [lax.ppermute(a, "aux", along(1)) for a in own]
    z, w, greens = transform(block_atom, green_occ, green_virt, rows, own)
    *later, z = lax.optimization_barrier((*own, z))
    arriving[0], z = lax.optimization_barrier((arriving[0], z))
    sibling = [to_sibling(a) for a in later]
    w = complete(w, greens, sibling)
    backs, aheads = [], []
    for step in range(1, chips // 2 + 1):
        held, last = arriving, step == chips // 2
        if not last:
            arriving = [lax.ppermute(a, "aux", along(1)) for a in held]
        if last:
            mine, theirs = both(z, z_sibling, held)
            backs += [mine, to_sibling(theirs)]
            continue
        other = [to_sibling(a) for a in held]
        share = far(w, held)
        ahead = lax.ppermute(share, "aux", along(-step))
        if step == 1:
            backs.append(near(z, own, sibling))
        backs.append(near(z, held, other))
        if step == 1:
            *sibling, _ = lax.optimization_barrier((*sibling, share))
            z_sibling = mirror(greens, sibling)
        *arriving, ahead, backs[-1], backs[-2], z_sibling = lax.optimization_barrier(
            (*arriving, ahead, backs[-1], backs[-2], z_sibling)
        )
        aheads.append(ahead)
    if columns == 2 * aux_here and pairs & (pairs - 1) == 0:
        mine, *sends = pack(chips, pairs, backs, aheads)
        parts = [mine]
        for j in range(pairs - 1, 0, -1):
            parts.append(lax.ppermute(sends[j - 1], "pair", [(i, i ^ j) for i in range(pairs)]))
    else:
        (shares,) = pack(chips, None, backs, aheads)
        shares = shares.transpose(1, 0, 2).reshape(nt * aux_here, pairs, columns).transpose(1, 0, 2)
        parts = [lax.all_to_all(shares, "pair", 0, 0)]
    scale = float((rows * pairs * BLK) ** -0.5)
    chi, sums = finish(scale, time_weights, parts, (nt, aux_here, columns), pairs * auxes)
    total = jnp.sum(lax.all_to_all(sums, ("pair", "aux"), 0, 0, tiled=True)[:, 0])
    energy = -total / jnp.float32(aux_total * aux_total)
    return chi, energy


def solution(mesh):
    placed = (P("pair", "aux"), P(None, "aux"), P(), P(), P(), P())
    return jax.shard_map(
        per_device,
        mesh=mesh,
        in_specs=placed,
        out_specs=(P(None, "aux", "pair"), P()),
        check_vma=False,
    )
```

```python
import functools
import jax
import jax.numpy as jnp
from jax import lax
from jax.experimental import pallas as pl
from jax.experimental.pallas import tpu as pltpu
from jax.sharding import PartitionSpec as P

BLK = 64
VMEM = pl.BlockSpec(memory_space=pltpu.VMEM)
SMEM = pl.BlockSpec(memory_space=pltpu.SMEM)
HBM = pl.BlockSpec(memory_space=pltpu.HBM)
NT_DIMS = (((1,), (1,)), ((), ()))


def call(kernel, name, flops, **settings):
    return pl.pallas_call(
        kernel,
        name=name,
        compiler_params=pltpu.CompilerParams(vmem_limit_bytes=40 * 1024 * 1024),
        cost_estimate=pl.CostEstimate(flops=flops, bytes_accessed=1 << 8, transcendentals=0),
        **settings,
    )


def stay(array):
    return pltpu.with_memory_space_constraint(array, pltpu.HBM)


def chip_of():
    return lax.axis_index("aux") // 2


def arrange_kernel(rows, aux, second, x_hbm, mask_hbm, y_ref, x, mask, wide, arrived):
    copies = [
        pltpu.make_async_copy(x_hbm.at[pl.ds(second * (rows // 2), rows // 2)], x, arrived.at[0]),
        pltpu.make_async_copy(mask_hbm, mask, arrived.at[1]),
    ]
    for copy in copies:
        copy.start()
    block = lax.axis_index("pair") * rows // BLK
    low = lax.broadcasted_iota(jnp.int32, (8, 128), 1) < BLK
    for copy in copies:
        copy.wait()
    for i in range(aux // 2):
        tile = x[:, i * 128:(i + 1) * 128].astype(jnp.float32)
        first, last = tile[:8], tile[8:]
        even = jnp.where(low, first, pltpu.roll(last, BLK, 1))
        odd = jnp.where(low, pltpu.roll(first, BLK, 1), last)
        even = jnp.where(mask[block, 2 * i] > 0, even, 0.0)
        odd = jnp.where(mask[block, 2 * i + 1] > 0, odd, 0.0)
        wide[pl.ds(2 * i, 8, stride=aux + 1), :] = even
        wide[pl.ds(2 * i + 1, 8, stride=aux + 1), :] = odd
    for s in range(8):
        lane = s % 2 * 128
        y_ref[s // 2, :, lane:lane + 128] = wide[s * (aux + 1):s * (aux + 1) + aux, :].astype(y_ref.dtype)


def arrange(integrals, block_mask, second):
    rows, width = integrals.shape
    aux = width // BLK
    return call(
        functools.partial(arrange_kernel, rows, aux, second),
        "arrange",
        1 << 28,
        out_shape=jax.ShapeDtypeStruct((4, aux, 256), jnp.bfloat16),
        in_specs=[HBM, HBM],
        out_specs=VMEM,
        scratch_shapes=[
            pltpu.VMEM((rows // 2, width), jnp.bfloat16),
            pltpu.SMEM(block_mask.shape, jnp.int32),
            pltpu.VMEM((8 * (aux + 1), 128), jnp.float32),
            pltpu.SemaphoreType.DMA((2,)),
        ],
    )(stay(integrals), stay(block_mask))


def through(y, first, second):
    steps, aux, wide = y.shape
    y = y[...].reshape(steps * aux, wide)
    half = jnp.dot(y, first, preferred_element_type=jnp.float32).astype(jnp.bfloat16)
    full = lax.dot_general(half, second, NT_DIMS, preferred_element_type=jnp.float32)
    return full.astype(jnp.bfloat16).reshape(steps, aux, wide)


def core_rows(aux, other):
    core = jnp.bitwise_xor(lax.rem(lax.axis_index("aux"), 2), other)
    return pl.ds(pl.multiple_of(core * aux, aux), aux)


def transform_kernel(nt, rows, atom_hbm, occ_hbm, virt_hbm, y1, y2, z_ref, w_ref, green_ref, *scratch):
    atom_ref, occ_ref, virt_ref, arrived = scratch
    aux, wide = y1.shape[1:]
    copies = wide // BLK
    copy = pltpu.make_async_copy(atom_hbm, atom_ref, arrived.at[0])
    copy.start()
    copy.wait()
    atom = atom_ref[lax.axis_index("pair") * rows // BLK]
    fetch = [
        pltpu.make_async_copy(occ_hbm.at[:, atom], occ_ref, arrived.at[0]),
        pltpu.make_async_copy(virt_hbm.at[:, atom], virt_ref, arrived.at[1]),
    ]
    for copy in fetch:
        copy.start()
    for copy in fetch:
        copy.wait()
    same = (
        lax.broadcasted_iota(jnp.int32, (wide, wide), 0) // BLK
        == lax.broadcasted_iota(jnp.int32, (wide, wide), 1) // BLK
    )

    def diagonal(block):
        tall = jnp.concatenate([block.astype(jnp.float32)] * copies, axis=0)
        full = jnp.concatenate([tall] * copies, axis=1)
        return jnp.where(same, full, 0.0).astype(jnp.bfloat16)

    for t in range(nt):
        occ, virt = diagonal(occ_ref[t]), diagonal(virt_ref[t])
        green_ref[t, 0], green_ref[t, 1] = occ, virt
        for half, y in enumerate((y1, y2)):
            z_ref[half, :, t * aux:(t + 1) * aux, :] = through(y, occ, virt)
            w_ref[half, t, :, core_rows(aux, 0), :] = through(y, virt, occ)


def transform(atom, green_occ, green_virt, rows, own):
    nt = green_occ.shape[0]
    steps, aux, wide = own[0].shape
    return call(
        functools.partial(transform_kernel, nt, rows),
        "transform",
        2 << 30,
        out_shape=(
            jax.ShapeDtypeStruct((2, steps, nt * aux, wide), jnp.bfloat16),
            jax.ShapeDtypeStruct((2, nt, steps, 2 * aux, wide), jnp.bfloat16),
            jax.ShapeDtypeStruct((nt, 2, wide, wide), jnp.bfloat16),
        ),
        in_specs=[HBM] * 3 + [VMEM] * 2,
        out_specs=(VMEM,) * 3,
        scratch_shapes=[
            pltpu.SMEM(atom.shape, jnp.int32),
            pltpu.VMEM((nt, BLK, BLK), jnp.bfloat16),
            pltpu.VMEM((nt, BLK, BLK), jnp.bfloat16),
            pltpu.SemaphoreType.DMA((2,)),
        ],
    )(stay(atom), stay(green_occ), stay(green_virt), *own)


def complete_kernel(before_ref, green_ref, y1, y2, w_ref):
    aux = y1.shape[1]
    for t in range(green_ref.shape[0]):
        for half, y in enumerate((y1, y2)):
            w_ref[half, t, :, core_rows(aux, 1), :] = through(y, green_ref[t, 1], green_ref[t, 0])


def complete(w, greens, sibling):
    return call(
        complete_kernel,
        "complete",
        1 << 30,
        out_shape=jax.ShapeDtypeStruct(w.shape, w.dtype),
        in_specs=[VMEM] * 4,
        out_specs=VMEM,
        input_output_aliases={0: 0},
    )(w, greens, *sibling)


def mirror_kernel(green_ref, y1, y2, z_ref):
    aux = y1.shape[1]
    for t in range(green_ref.shape[0]):
        for half, y in enumerate((y1, y2)):
            z_ref[half, :, t * aux:(t + 1) * aux, :] = through(y, green_ref[t, 0], green_ref[t, 1])


def mirror(greens, sibling):
    steps, aux, wide = sibling[0].shape
    return call(
        mirror_kernel,
        "mirror",
        1 << 29,
        out_shape=jax.ShapeDtypeStruct((2, steps, greens.shape[0] * aux, wide), jnp.bfloat16),
        in_specs=[VMEM] * 3,
        out_specs=VMEM,
    )(greens, *sibling)


def both_kernel(z_ref, sibling_ref, y1, y2, mine_ref, theirs_ref):
    for operand, out_ref in ((sibling_ref, theirs_ref), (z_ref, mine_ref)):
        total = jnp.zeros(out_ref.shape, jnp.float32)
        for half, y in enumerate((y1, y2)):
            for j in range(y.shape[0]):
                total += lax.dot_general(operand[half, j], y[j], NT_DIMS, preferred_element_type=jnp.float32)
        out_ref[...] = total


def both(z, z_sibling, pieces):
    share = jax.ShapeDtypeStruct((z.shape[2], pieces[0].shape[1]), jnp.float32)
    return call(
        both_kernel,
        "both",
        1 << 29,
        out_shape=(share, share),
        in_specs=[VMEM] * 4,
        out_specs=(VMEM, VMEM),
    )(z, z_sibling, *pieces)


def near_kernel(count, z_ref, *refs):
    mine, other, out_ref = refs[:count], refs[count:2 * count], refs[-1]

    def products(low, high):
        total = jnp.zeros(out_ref.shape, jnp.float32)
        for half, (first, second) in enumerate(zip(low, high)):
            for j in range(z_ref.shape[1]):
                partner = jnp.concatenate([first[j], second[j]], axis=0)
                total += lax.dot_general(z_ref[half, j], partner, NT_DIMS, preferred_element_type=jnp.float32)
        out_ref[...] = total

    core = lax.rem(lax.axis_index("aux"), 2)
    pl.when(core == 0)(lambda: products(mine, other))
    pl.when(core == 1)(lambda: products(other, mine))


def near(z, mine, other):
    size = z.shape[2]
    return call(
        functools.partial(near_kernel, len(mine)),
        "near",
        1 << 29,
        out_shape=jax.ShapeDtypeStruct((size, 2 * mine[0].shape[-2]), jnp.float32),
        in_specs=[VMEM] * (1 + 2 * len(mine)),
        out_specs=VMEM,
    )(z, *mine, *other)


def fold(x):
    high = x.shape[0] // 2
    past = jnp.concatenate([x[:high, 128:], x[high:, 128:]], axis=1)
    return jnp.concatenate([x[:, :128], past], axis=0)


def unfold(x):
    high = x.shape[0] // 3
    past = x[2 * high:]
    past = jnp.concatenate([past[:, :BLK], past[:, BLK:]], axis=0)
    return jnp.concatenate([x[:2 * high], past], axis=1)


def far_kernel(w_ref, *refs):
    mine, out_ref = refs[:-1], refs[-1]
    nt, steps = w_ref.shape[1:3]
    aux = mine[0].shape[1]
    shares = []
    for t in range(nt):
        total = jnp.zeros((aux, w_ref.shape[3]), jnp.float32)
        for half, piece in enumerate(mine):
            for j in range(steps):
                total += lax.dot_general(piece[j], w_ref[half, t, j], NT_DIMS, preferred_element_type=jnp.float32)
        shares.append(total)
    out_ref[...] = fold(jnp.concatenate(shares, axis=0)).astype(out_ref.dtype)


def far(w, mine):
    aux = mine[0].shape[1]
    return call(
        far_kernel,
        "far",
        1 << 29,
        out_shape=jax.ShapeDtypeStruct((w.shape[1] * aux * 3 // 2, 128), jnp.bfloat16),
        in_specs=[VMEM] * (1 + len(mine)),
        out_specs=VMEM,
    )(w, *mine)


def pack_kernel(chips, folded, *refs):
    backs, aheads = refs[:chips // 2], refs[chips // 2 + 2:chips + 1]
    mine, other = refs[chips // 2][...], refs[chips // 2 + 1][...]
    out_ref, shares = refs[-2:]
    chip = chip_of()
    for step in range(chips // 2):
        shares[lax.rem(chip + chips - step, chips)] = fold(backs[step][...])
    first = lax.rem(lax.axis_index("aux"), 2) == 0
    pieces = [jnp.where(first, mine, other), jnp.where(first, other, mine)]
    shares[lax.rem(chip + chips // 2, chips)] = fold(jnp.concatenate(pieces, axis=1))
    for step in range(1, chips // 2):
        shares[lax.rem(chip + step, chips)] = aheads[step - 1][...].astype(jnp.float32)
    for q in range(chips):
        out_ref[q] = (shares[q] if folded else unfold(shares[q])).astype(out_ref.dtype)


def pack(chips, folded, backs, aheads):
    height, width = backs[0].shape
    narrow = (chips, height * 3 // 2, 128)
    return call(
        functools.partial(pack_kernel, chips, folded),
        "pack",
        1 << 28,
        out_shape=jax.ShapeDtypeStruct(narrow if folded else (chips, height, width), jnp.bfloat16),
        in_specs=[VMEM] * (chips + 1),
        out_specs=VMEM,
        scratch_shapes=[pltpu.VMEM(narrow, jnp.float32)],
    )(*backs, *aheads)


def finish_kernel(scale, nt, folded, weight_ref, part_ref, chi_hbm, sum_ref, chi_ref, leaving):
    aux = chi_ref.shape[1]
    total = part_ref[0].astype(jnp.float32)
    for p in range(1, part_ref.shape[0]):
        total += part_ref[p].astype(jnp.float32)
    total *= scale
    if folded:
        total = unfold(total)
    for t in range(nt):
        chi_ref[t] = total[t * aux:(t + 1) * aux]
    copy = pltpu.make_async_copy(chi_ref, chi_hbm, leaving)
    copy.start()
    local = jnp.zeros((1, 1), jnp.float32)
    for t in range(nt):
        chi = total[t * aux:(t + 1) * aux]
        local += weight_ref[:, t:t + 1] * jnp.sum(chi * chi, keepdims=True)
    sum_ref[...] = jnp.broadcast_to(local, sum_ref.shape)
    copy.wait()


def finish(scale, folded, time_weights, parts, chi_shape, copies):
    return call(
        functools.partial(finish_kernel, scale, chi_shape[0], folded),
        "finish",
        1 << 28,
        out_shape=(
            jax.ShapeDtypeStruct(chi_shape, jnp.float32),
            jax.ShapeDtypeStruct((copies, 128), jnp.float32),
        ),
        in_specs=[VMEM] * 2,
        out_specs=(HBM, VMEM),
        scratch_shapes=[pltpu.VMEM(chi_shape, jnp.float32), pltpu.SemaphoreType.DMA],
    )(time_weights[None], parts)


def per_device(integrals, block_mask, block_atom, green_occ, green_virt, time_weights):
    rows = integrals.shape[0]
    aux_here = integrals.shape[1] // BLK
    pairs, auxes = lax.axis_size("pair"), lax.axis_size("aux")
    chips = auxes // 2
    aux_total = aux_here * auxes
    columns = aux_total // pairs
    nt = green_occ.shape[0]

    def along(shift):
        return [(i, (i + 2 * shift) % auxes) for i in range(auxes)]

    def to_sibling(array):
        return lax.ppermute(array, "aux", [(i, i ^ 1) for i in range(auxes)])

    own = [arrange(integrals, block_mask, second) for second in (False, True)]
    arriving = [lax.ppermute(a, "aux", along(1)) for a in own]
    z, w, greens = transform(block_atom, green_occ, green_virt, rows, own)
    *later, z = lax.optimization_barrier((*own, z))
    arriving[0], z = lax.optimization_barrier((arriving[0], z))
    sibling = [to_sibling(a) for a in later]
    w = complete(w, greens, sibling)
    backs, aheads = [], []
    for step in range(1, chips // 2 + 1):
        held, last = arriving, step == chips // 2
        if not last:
            arriving = [lax.ppermute(a, "aux", along(1)) for a in held]
        if last:
            mine, theirs = both(z, z_sibling, held)
            backs += [mine, to_sibling(theirs)]
            continue
        other = [to_sibling(a) for a in held]
        share = far(w, held)
        ahead = lax.ppermute(share, "aux", along(-step))
        if step == 1:
            backs.append(near(z, own, sibling))
        backs.append(near(z, held, other))
        if step == 1:
            *sibling, _ = lax.optimization_barrier((*sibling, share))
            z_sibling = mirror(greens, sibling)
        *arriving, ahead, backs[-1], backs[-2], z_sibling = lax.optimization_barrier(
            (*arriving, ahead, backs[-1], backs[-2], z_sibling)
        )
        aheads.append(ahead)
    folded = columns == 2 * aux_here
    shares = pack(chips, folded, backs, aheads)
    if not folded:
        shares = shares.transpose(1, 0, 2).reshape(nt * aux_here, pairs, columns).transpose(1, 0, 2)
    parts = lax.all_to_all(shares, "pair", 0, 0)
    scale = float((rows * pairs * BLK) ** -0.5)
    chi, sums = finish(scale, folded, time_weights, parts, (nt, aux_here, columns), pairs * auxes)
    total = jnp.sum(lax.all_to_all(sums, ("pair", "aux"), 0, 0, tiled=True)[:, 0])
    energy = -total / jnp.float32(aux_total * aux_total)
    return chi, energy


def solution(mesh):
    placed = (P("pair", "aux"), P(None, "aux"), P(), P(), P(), P())
    return jax.shard_map(
        per_device,
        mesh=mesh,
        in_specs=placed,
        out_specs=(P(None, "aux", "pair"), P()),
        check_vma=False,
    )
```

```python
import functools
import jax
import jax.numpy as jnp
from jax import lax
from jax.experimental import pallas as pl
from jax.experimental.pallas import tpu as pltpu
from jax.sharding import PartitionSpec as P

BLK = 64
VMEM = pl.BlockSpec(memory_space=pltpu.VMEM)
SMEM = pl.BlockSpec(memory_space=pltpu.SMEM)
HBM = pl.BlockSpec(memory_space=pltpu.HBM)
NT_DIMS = (((1,), (1,)), ((), ()))


def call(kernel, name, flops, **settings):
    return pl.pallas_call(
        kernel,
        name=name,
        compiler_params=pltpu.CompilerParams(vmem_limit_bytes=40 * 1024 * 1024),
        cost_estimate=pl.CostEstimate(flops=flops, bytes_accessed=1 << 8, transcendentals=0),
        **settings,
    )


def stay(array):
    return pltpu.with_memory_space_constraint(array, pltpu.HBM)


def chip_of():
    return lax.axis_index("aux") // 2


def arrange_kernel(rows, aux, second, x_hbm, mask_hbm, y_ref, x, mask, wide, arrived):
    copies = [
        pltpu.make_async_copy(x_hbm.at[pl.ds(second * (rows // 2), rows // 2)], x, arrived.at[0]),
        pltpu.make_async_copy(mask_hbm, mask, arrived.at[1]),
    ]
    for copy in copies:
        copy.start()
    block = lax.axis_index("pair") * rows // BLK
    low = lax.broadcasted_iota(jnp.int32, (8, 128), 1) < BLK
    for copy in copies:
        copy.wait()
    for i in range(aux // 2):
        tile = x[:, i * 128:(i + 1) * 128].astype(jnp.float32)
        first, last = tile[:8], tile[8:]
        even = jnp.where(low, first, pltpu.roll(last, BLK, 1))
        odd = jnp.where(low, pltpu.roll(first, BLK, 1), last)
        even = jnp.where(mask[block, 2 * i] > 0, even, 0.0)
        odd = jnp.where(mask[block, 2 * i + 1] > 0, odd, 0.0)
        wide[pl.ds(2 * i, 8, stride=aux + 1), :] = even
        wide[pl.ds(2 * i + 1, 8, stride=aux + 1), :] = odd
    for s in range(8):
        lane = s % 2 * 128
        y_ref[s // 2, :, lane:lane + 128] = wide[s * (aux + 1):s * (aux + 1) + aux, :].astype(y_ref.dtype)


def arrange(integrals, block_mask, second):
    rows, width = integrals.shape
    aux = width // BLK
    return call(
        functools.partial(arrange_kernel, rows, aux, second),
        "arrange",
        1 << 28,
        out_shape=jax.ShapeDtypeStruct((4, aux, 256), jnp.bfloat16),
        in_specs=[HBM, HBM],
        out_specs=VMEM,
        scratch_shapes=[
            pltpu.VMEM((rows // 2, width), jnp.bfloat16),
            pltpu.SMEM(block_mask.shape, jnp.int32),
            pltpu.VMEM((8 * (aux + 1), 128), jnp.float32),
            pltpu.SemaphoreType.DMA((2,)),
        ],
    )(stay(integrals), stay(block_mask))


def through(y, first, second):
    steps, aux, wide = y.shape
    y = y[...].reshape(steps * aux, wide)
    half = jnp.dot(y, first, preferred_element_type=jnp.float32).astype(jnp.bfloat16)
    full = lax.dot_general(half, second, NT_DIMS, preferred_element_type=jnp.float32)
    return full.astype(jnp.bfloat16).reshape(steps, aux, wide)


def core_rows(aux, other):
    core = jnp.bitwise_xor(lax.rem(lax.axis_index("aux"), 2), other)
    return pl.ds(pl.multiple_of(core * aux, aux), aux)


def transform_kernel(nt, rows, atom_hbm, occ_hbm, virt_hbm, y1, y2, z_ref, w_ref, green_ref, *scratch):
    atom_ref, occ_ref, virt_ref, arrived = scratch
    aux, wide = y1.shape[1:]
    copies = wide // BLK
    copy = pltpu.make_async_copy(atom_hbm, atom_ref, arrived.at[0])
    copy.start()
    copy.wait()
    atom = atom_ref[lax.axis_index("pair") * rows // BLK]
    fetch = [
        pltpu.make_async_copy(occ_hbm.at[:, atom], occ_ref, arrived.at[0]),
        pltpu.make_async_copy(virt_hbm.at[:, atom], virt_ref, arrived.at[1]),
    ]
    for copy in fetch:
        copy.start()
    for copy in fetch:
        copy.wait()
    same = (
        lax.broadcasted_iota(jnp.int32, (wide, wide), 0) // BLK
        == lax.broadcasted_iota(jnp.int32, (wide, wide), 1) // BLK
    )

    def diagonal(block):
        tall = jnp.concatenate([block.astype(jnp.float32)] * copies, axis=0)
        full = jnp.concatenate([tall] * copies, axis=1)
        return jnp.where(same, full, 0.0).astype(jnp.bfloat16)

    for t in range(nt):
        occ, virt = diagonal(occ_ref[t]), diagonal(virt_ref[t])
        green_ref[t, 0], green_ref[t, 1] = occ, virt
        for half, y in enumerate((y1, y2)):
            z_ref[half, :, t * aux:(t + 1) * aux, :] = through(y, occ, virt)
            w_ref[half, t, :, core_rows(aux, 0), :] = through(y, virt, occ)


def transform(atom, green_occ, green_virt, rows, own):
    nt = green_occ.shape[0]
    steps, aux, wide = own[0].shape
    return call(
        functools.partial(transform_kernel, nt, rows),
        "transform",
        2 << 30,
        out_shape=(
            jax.ShapeDtypeStruct((2, steps, nt * aux, wide), jnp.bfloat16),
            jax.ShapeDtypeStruct((2, nt, steps, 2 * aux, wide), jnp.bfloat16),
            jax.ShapeDtypeStruct((nt, 2, wide, wide), jnp.bfloat16),
        ),
        in_specs=[HBM] * 3 + [VMEM] * 2,
        out_specs=(VMEM,) * 3,
        scratch_shapes=[
            pltpu.SMEM(atom.shape, jnp.int32),
            pltpu.VMEM((nt, BLK, BLK), jnp.bfloat16),
            pltpu.VMEM((nt, BLK, BLK), jnp.bfloat16),
            pltpu.SemaphoreType.DMA((2,)),
        ],
    )(stay(atom), stay(green_occ), stay(green_virt), *own)


def complete_kernel(before_ref, green_ref, y1, y2, w_ref):
    aux = y1.shape[1]
    for t in range(green_ref.shape[0]):
        for half, y in enumerate((y1, y2)):
            w_ref[half, t, :, core_rows(aux, 1), :] = through(y, green_ref[t, 1], green_ref[t, 0])


def complete(w, greens, sibling):
    return call(
        complete_kernel,
        "complete",
        1 << 30,
        out_shape=jax.ShapeDtypeStruct(w.shape, w.dtype),
        in_specs=[VMEM] * 4,
        out_specs=VMEM,
        input_output_aliases={0: 0},
    )(w, greens, *sibling)


def mirror_kernel(green_ref, y1, y2, z_ref):
    aux = y1.shape[1]
    for t in range(green_ref.shape[0]):
        for half, y in enumerate((y1, y2)):
            z_ref[half, :, t * aux:(t + 1) * aux, :] = through(y, green_ref[t, 0], green_ref[t, 1])


def mirror(greens, sibling):
    steps, aux, wide = sibling[0].shape
    return call(
        mirror_kernel,
        "mirror",
        1 << 29,
        out_shape=jax.ShapeDtypeStruct((2, steps, greens.shape[0] * aux, wide), jnp.bfloat16),
        in_specs=[VMEM] * 3,
        out_specs=VMEM,
    )(greens, *sibling)


def both_kernel(z_ref, sibling_ref, y1, y2, mine_ref, theirs_ref):
    for operand, out_ref in ((sibling_ref, theirs_ref), (z_ref, mine_ref)):
        total = jnp.zeros(out_ref.shape, jnp.float32)
        for half, y in enumerate((y1, y2)):
            for j in range(y.shape[0]):
                total += lax.dot_general(operand[half, j], y[j], NT_DIMS, preferred_element_type=jnp.float32)
        out_ref[...] = total


def both(z, z_sibling, pieces):
    share = jax.ShapeDtypeStruct((z.shape[2], pieces[0].shape[1]), jnp.float32)
    return call(
        both_kernel,
        "both",
        1 << 29,
        out_shape=(share, share),
        in_specs=[VMEM] * 4,
        out_specs=(VMEM, VMEM),
    )(z, z_sibling, *pieces)


def near_kernel(count, z_ref, *refs):
    mine, other, out_ref = refs[:count], refs[count:2 * count], refs[-1]

    def products(low, high):
        total = jnp.zeros(out_ref.shape, jnp.float32)
        for half, (first, second) in enumerate(zip(low, high)):
            for j in range(z_ref.shape[1]):
                partner = jnp.concatenate([first[j], second[j]], axis=0)
                total += lax.dot_general(z_ref[half, j], partner, NT_DIMS, preferred_element_type=jnp.float32)
        out_ref[...] = total

    core = lax.rem(lax.axis_index("aux"), 2)
    pl.when(core == 0)(lambda: products(mine, other))
    pl.when(core == 1)(lambda: products(other, mine))


def near(z, mine, other):
    size = z.shape[2]
    return call(
        functools.partial(near_kernel, len(mine)),
        "near",
        1 << 29,
        out_shape=jax.ShapeDtypeStruct((size, 2 * mine[0].shape[-2]), jnp.float32),
        in_specs=[VMEM] * (1 + 2 * len(mine)),
        out_specs=VMEM,
    )(z, *mine, *other)


def fold(x):
    high = x.shape[0] // 2
    past = jnp.concatenate([x[:high, 128:], x[high:, 128:]], axis=1)
    return jnp.concatenate([x[:, :128], past], axis=0)


def unfold(x):
    high = x.shape[0] // 3
    past = x[2 * high:]
    past = jnp.concatenate([past[:, :BLK], past[:, BLK:]], axis=0)
    return jnp.concatenate([x[:2 * high], past], axis=1)


def far_kernel(w_ref, *refs):
    mine, out_ref = refs[:-1], refs[-1]
    nt, steps = w_ref.shape[1:3]
    aux = mine[0].shape[1]
    shares = []
    for t in range(nt):
        total = jnp.zeros((aux, w_ref.shape[3]), jnp.float32)
        for half, piece in enumerate(mine):
            for j in range(steps):
                total += lax.dot_general(piece[j], w_ref[half, t, j], NT_DIMS, preferred_element_type=jnp.float32)
        shares.append(total)
    out_ref[...] = fold(jnp.concatenate(shares, axis=0)).astype(out_ref.dtype)


def far(w, mine):
    aux = mine[0].shape[1]
    return call(
        far_kernel,
        "far",
        1 << 29,
        out_shape=jax.ShapeDtypeStruct((w.shape[1] * aux * 3 // 2, 128), jnp.bfloat16),
        in_specs=[VMEM] * (1 + len(mine)),
        out_specs=VMEM,
    )(w, *mine)


def pack_kernel(chips, pairs, *refs):
    backs, aheads = refs[:chips // 2], refs[chips // 2 + 2:chips + 1]
    mine, other = refs[chips // 2][...], refs[chips // 2 + 1][...]
    outs, shares = refs[chips + 1:-1], refs[-1]
    chip = chip_of()
    for step in range(chips // 2):
        shares[lax.rem(chip + chips - step, chips)] = fold(backs[step][...])
    first = lax.rem(lax.axis_index("aux"), 2) == 0
    pieces = [jnp.where(first, mine, other), jnp.where(first, other, mine)]
    shares[lax.rem(chip + chips // 2, chips)] = fold(jnp.concatenate(pieces, axis=1))
    for step in range(1, chips // 2):
        shares[lax.rem(chip + step, chips)] = aheads[step - 1][...].astype(jnp.float32)
    if pairs is None:
        for q in range(chips):
            outs[0][q] = unfold(shares[q]).astype(jnp.bfloat16)
    else:
        pair = lax.axis_index("pair")
        for j, out_ref in enumerate(outs):
            out_ref[...] = shares[lax.bitwise_xor(pair, j)].astype(out_ref.dtype)


def pack(chips, pairs, backs, aheads):
    height, width = backs[0].shape
    folded = (height * 3 // 2, 128)
    if pairs is None:
        out_shape = (jax.ShapeDtypeStruct((chips, height, width), jnp.bfloat16),)
    else:
        out_shape = (jax.ShapeDtypeStruct(folded, jnp.float32),)
        out_shape += (jax.ShapeDtypeStruct(folded, jnp.bfloat16),) * (pairs - 1)
    return call(
        functools.partial(pack_kernel, chips, pairs),
        "pack",
        1 << 28,
        out_shape=out_shape,
        in_specs=[VMEM] * (chips + 1),
        out_specs=(VMEM,) * len(out_shape),
        scratch_shapes=[pltpu.VMEM((chips,) + folded, jnp.float32)],
    )(*backs, *aheads)


def combine_kernel(scale, nt, folded, weight_ref, *refs):
    parts, (chi_ref, sum_ref) = refs[:-2], refs[-2:]
    aux = chi_ref.shape[1]
    if folded:
        total = parts[0][...]
        for part in parts[1:]:
            total += part[...].astype(jnp.float32)
        total = unfold(total * scale)
    else:
        total = parts[0][0].astype(jnp.float32)
        for p in range(1, parts[0].shape[0]):
            total += parts[0][p].astype(jnp.float32)
        total *= scale
    local = jnp.zeros((1, 1), jnp.float32)
    for t in range(nt):
        chi = total[t * aux:(t + 1) * aux]
        chi_ref[t] = chi
        local += weight_ref[:, t:t + 1] * jnp.sum(chi * chi, keepdims=True)
    sum_ref[...] = jnp.broadcast_to(local, sum_ref.shape)


def combine(scale, time_weights, parts, chi_shape, copies):
    return call(
        functools.partial(combine_kernel, scale, chi_shape[0], len(parts) > 1),
        "combine",
        1 << 28,
        out_shape=(
            jax.ShapeDtypeStruct(chi_shape, jnp.float32),
            jax.ShapeDtypeStruct((copies, 128), jnp.float32),
        ),
        in_specs=[VMEM] * (1 + len(parts)),
        out_specs=(VMEM, VMEM),
    )(time_weights[None], *parts)


def close_kernel(norm, tile_ref, sums_ref, chi_hbm, energy_ref, leaving):
    copy = pltpu.make_async_copy(tile_ref, chi_hbm, leaving)
    copy.start()
    total = jnp.sum(sums_ref[...], axis=0, keepdims=True)
    energy_ref[...] = -total[:, :1] / norm
    copy.wait()


def close(norm, tile, sums):
    return call(
        functools.partial(close_kernel, norm),
        "close",
        1 << 28,
        out_shape=(
            jax.ShapeDtypeStruct(tile.shape, jnp.float32),
            jax.ShapeDtypeStruct((1, 1), jnp.float32),
        ),
        in_specs=[VMEM, VMEM],
        out_specs=(HBM, VMEM),
        scratch_shapes=[pltpu.SemaphoreType.DMA],
    )(tile, sums)


def per_device(integrals, block_mask, block_atom, green_occ, green_virt, time_weights):
    rows = integrals.shape[0]
    aux_here = integrals.shape[1] // BLK
    pairs, auxes = lax.axis_size("pair"), lax.axis_size("aux")
    chips = auxes // 2
    aux_total = aux_here * auxes
    columns = aux_total // pairs
    nt = green_occ.shape[0]

    def along(shift):
        return [(i, (i + 2 * shift) % auxes) for i in range(auxes)]

    def to_sibling(array):
        return lax.ppermute(array, "aux", [(i, i ^ 1) for i in range(auxes)])

    own = [arrange(integrals, block_mask, second) for second in (False, True)]
    arriving = [lax.ppermute(a, "aux", along(1)) for a in own]
    z, w, greens = transform(block_atom, green_occ, green_virt, rows, own)
    *later, z = lax.optimization_barrier((*own, z))
    arriving[0], z = lax.optimization_barrier((arriving[0], z))
    sibling = [to_sibling(a) for a in later]
    w = complete(w, greens, sibling)
    backs, aheads = [], []
    for step in range(1, chips // 2 + 1):
        held, last = arriving, step == chips // 2
        if not last:
            arriving = [lax.ppermute(a, "aux", along(1)) for a in held]
        if last:
            mine, theirs = both(z, z_sibling, held)
            backs += [mine, to_sibling(theirs)]
            continue
        other = [to_sibling(a) for a in held]
        share = far(w, held)
        ahead = lax.ppermute(share, "aux", along(-step))
        if step == 1:
            backs.append(near(z, own, sibling))
        backs.append(near(z, held, other))
        if step == 1:
            *sibling, _ = lax.optimization_barrier((*sibling, share))
            z_sibling = mirror(greens, sibling)
        *arriving, ahead, backs[-1], backs[-2], z_sibling = lax.optimization_barrier(
            (*arriving, ahead, backs[-1], backs[-2], z_sibling)
        )
        aheads.append(ahead)
    if columns == 2 * aux_here and pairs & (pairs - 1) == 0:
        mine, *sends = pack(chips, pairs, backs, aheads)
        parts = [mine]
        for j in range(pairs - 1, 0, -1):
            parts.append(lax.ppermute(sends[j - 1], "pair", [(i, i ^ j) for i in range(pairs)]))
    else:
        (shares,) = pack(chips, None, backs, aheads)
        shares = shares.transpose(1, 0, 2).reshape(nt * aux_here, pairs, columns).transpose(1, 0, 2)
        parts = [lax.all_to_all(shares, "pair", 0, 0)]
    scale = float((rows * pairs * BLK) ** -0.5)
    tile, sums = combine(scale, time_weights, parts, (nt, aux_here, columns), pairs * auxes)
    everyone = lax.all_to_all(sums, ("pair", "aux"), 0, 0, tiled=True)
    chi, energy = close(float(aux_total * aux_total), tile, everyone)
    return chi, energy[0, 0]


def solution(mesh):
    placed = (P("pair", "aux"), P(None, "aux"), P(), P(), P(), P())
    return jax.shard_map(
        per_device,
        mesh=mesh,
        in_specs=placed,
        out_specs=(P(None, "aux", "pair"), P()),
        check_vma=False,
    )
```

```python
import functools
import jax
import jax.numpy as jnp
from jax import lax
from jax.experimental import pallas as pl
from jax.experimental.pallas import tpu as pltpu
from jax.sharding import PartitionSpec as P

BLK = 64
VMEM = pl.BlockSpec(memory_space=pltpu.VMEM)
SMEM = pl.BlockSpec(memory_space=pltpu.SMEM)
HBM = pl.BlockSpec(memory_space=pltpu.HBM)
NT_DIMS = (((1,), (1,)), ((), ()))


def call(kernel, name, flops, **settings):
    return pl.pallas_call(
        kernel,
        name=name,
        compiler_params=pltpu.CompilerParams(vmem_limit_bytes=40 * 1024 * 1024),
        cost_estimate=pl.CostEstimate(flops=flops, bytes_accessed=1 << 8, transcendentals=0),
        **settings,
    )


def stay(array):
    return pltpu.with_memory_space_constraint(array, pltpu.HBM)


def chip_of():
    return lax.axis_index("aux") // 2


def arrange_kernel(rows, aux, second, x_hbm, mask_hbm, y_ref, x, mask, wide, arrived):
    copies = [
        pltpu.make_async_copy(x_hbm.at[pl.ds(second * (rows // 2), rows // 2)], x, arrived.at[0]),
        pltpu.make_async_copy(mask_hbm, mask, arrived.at[1]),
    ]
    for copy in copies:
        copy.start()
    block = lax.axis_index("pair") * rows // BLK
    low = lax.broadcasted_iota(jnp.int32, (8, 128), 1) < BLK
    for copy in copies:
        copy.wait()
    for i in range(aux // 2):
        tile = x[:, i * 128:(i + 1) * 128].astype(jnp.float32)
        first, last = tile[:8], tile[8:]
        even = jnp.where(low, first, pltpu.roll(last, BLK, 1))
        odd = jnp.where(low, pltpu.roll(first, BLK, 1), last)
        even = jnp.where(mask[block, 2 * i] > 0, even, 0.0)
        odd = jnp.where(mask[block, 2 * i + 1] > 0, odd, 0.0)
        wide[pl.ds(2 * i, 8, stride=aux + 1), :] = even
        wide[pl.ds(2 * i + 1, 8, stride=aux + 1), :] = odd
    for s in range(8):
        lane = s % 2 * 128
        y_ref[s // 2, :, lane:lane + 128] = wide[s * (aux + 1):s * (aux + 1) + aux, :].astype(y_ref.dtype)


def arrange(integrals, block_mask, second):
    rows, width = integrals.shape
    aux = width // BLK
    return call(
        functools.partial(arrange_kernel, rows, aux, second),
        "arrange",
        1 << 28,
        out_shape=jax.ShapeDtypeStruct((4, aux, 256), jnp.bfloat16),
        in_specs=[HBM, HBM],
        out_specs=VMEM,
        scratch_shapes=[
            pltpu.VMEM((rows // 2, width), jnp.bfloat16),
            pltpu.SMEM(block_mask.shape, jnp.int32),
            pltpu.VMEM((8 * (aux + 1), 128), jnp.float32),
            pltpu.SemaphoreType.DMA((2,)),
        ],
    )(stay(integrals), stay(block_mask))


def through(y, first, second):
    steps, aux, wide = y.shape
    y = y[...].reshape(steps * aux, wide)
    half = jnp.dot(y, first, preferred_element_type=jnp.float32).astype(jnp.bfloat16)
    full = lax.dot_general(half, second, NT_DIMS, preferred_element_type=jnp.float32)
    return full.astype(jnp.bfloat16).reshape(steps, aux, wide)


def core_rows(aux, other):
    core = jnp.bitwise_xor(lax.rem(lax.axis_index("aux"), 2), other)
    return pl.ds(pl.multiple_of(core * aux, aux), aux)


def transform_kernel(nt, rows, atom_hbm, occ_hbm, virt_hbm, y1, y2, z_ref, w_ref, green_ref, *scratch):
    atom_ref, occ_ref, virt_ref, arrived = scratch
    aux, wide = y1.shape[1:]
    copies = wide // BLK
    copy = pltpu.make_async_copy(atom_hbm, atom_ref, arrived.at[0])
    copy.start()
    copy.wait()
    atom = atom_ref[lax.axis_index("pair") * rows // BLK]
    fetch = [
        pltpu.make_async_copy(occ_hbm.at[:, atom], occ_ref, arrived.at[0]),
        pltpu.make_async_copy(virt_hbm.at[:, atom], virt_ref, arrived.at[1]),
    ]
    for copy in fetch:
        copy.start()
    for copy in fetch:
        copy.wait()
    same = (
        lax.broadcasted_iota(jnp.int32, (wide, wide), 0) // BLK
        == lax.broadcasted_iota(jnp.int32, (wide, wide), 1) // BLK
    )

    def diagonal(block):
        tall = jnp.concatenate([block.astype(jnp.float32)] * copies, axis=0)
        full = jnp.concatenate([tall] * copies, axis=1)
        return jnp.where(same, full, 0.0).astype(jnp.bfloat16)

    for t in range(nt):
        occ, virt = diagonal(occ_ref[t]), diagonal(virt_ref[t])
        green_ref[t, 0], green_ref[t, 1] = occ, virt
        for half, y in enumerate((y1, y2)):
            z_ref[half, :, t * aux:(t + 1) * aux, :] = through(y, occ, virt)
            w_ref[half, t, :, core_rows(aux, 0), :] = through(y, virt, occ)


def transform(atom, green_occ, green_virt, rows, own):
    nt = green_occ.shape[0]
    steps, aux, wide = own[0].shape
    return call(
        functools.partial(transform_kernel, nt, rows),
        "transform",
        2 << 30,
        out_shape=(
            jax.ShapeDtypeStruct((2, steps, nt * aux, wide), jnp.bfloat16),
            jax.ShapeDtypeStruct((2, nt, steps, 2 * aux, wide), jnp.bfloat16),
            jax.ShapeDtypeStruct((nt, 2, wide, wide), jnp.bfloat16),
        ),
        in_specs=[HBM] * 3 + [VMEM] * 2,
        out_specs=(VMEM,) * 3,
        scratch_shapes=[
            pltpu.SMEM(atom.shape, jnp.int32),
            pltpu.VMEM((nt, BLK, BLK), jnp.bfloat16),
            pltpu.VMEM((nt, BLK, BLK), jnp.bfloat16),
            pltpu.SemaphoreType.DMA((2,)),
        ],
    )(stay(atom), stay(green_occ), stay(green_virt), *own)


def complete_kernel(before_ref, green_ref, y1, y2, w_ref):
    aux = y1.shape[1]
    for t in range(green_ref.shape[0]):
        for half, y in enumerate((y1, y2)):
            w_ref[half, t, :, core_rows(aux, 1), :] = through(y, green_ref[t, 1], green_ref[t, 0])


def complete(w, greens, sibling):
    return call(
        complete_kernel,
        "complete",
        1 << 30,
        out_shape=jax.ShapeDtypeStruct(w.shape, w.dtype),
        in_specs=[VMEM] * 4,
        out_specs=VMEM,
        input_output_aliases={0: 0},
    )(w, greens, *sibling)


def mirror_kernel(green_ref, y1, y2, z_ref):
    aux = y1.shape[1]
    for t in range(green_ref.shape[0]):
        for half, y in enumerate((y1, y2)):
            z_ref[half, :, t * aux:(t + 1) * aux, :] = through(y, green_ref[t, 0], green_ref[t, 1])


def mirror(greens, sibling):
    steps, aux, wide = sibling[0].shape
    return call(
        mirror_kernel,
        "mirror",
        1 << 29,
        out_shape=jax.ShapeDtypeStruct((2, steps, greens.shape[0] * aux, wide), jnp.bfloat16),
        in_specs=[VMEM] * 3,
        out_specs=VMEM,
    )(greens, *sibling)


def both_kernel(z_ref, sibling_ref, y1, y2, mine_ref, theirs_ref):
    for operand, out_ref in ((sibling_ref, theirs_ref), (z_ref, mine_ref)):
        total = jnp.zeros(out_ref.shape, jnp.float32)
        for half, y in enumerate((y1, y2)):
            for j in range(y.shape[0]):
                total += lax.dot_general(operand[half, j], y[j], NT_DIMS, preferred_element_type=jnp.float32)
        out_ref[...] = total


def both(z, z_sibling, pieces):
    share = jax.ShapeDtypeStruct((z.shape[2], pieces[0].shape[1]), jnp.float32)
    return call(
        both_kernel,
        "both",
        1 << 29,
        out_shape=(share, share),
        in_specs=[VMEM] * 4,
        out_specs=(VMEM, VMEM),
    )(z, z_sibling, *pieces)


def near_kernel(count, z_ref, *refs):
    mine, other, out_ref = refs[:count], refs[count:2 * count], refs[-1]

    def products(low, high):
        total = jnp.zeros(out_ref.shape, jnp.float32)
        for half, (first, second) in enumerate(zip(low, high)):
            for j in range(z_ref.shape[1]):
                partner = jnp.concatenate([first[j], second[j]], axis=0)
                total += lax.dot_general(z_ref[half, j], partner, NT_DIMS, preferred_element_type=jnp.float32)
        out_ref[...] = total

    core = lax.rem(lax.axis_index("aux"), 2)
    pl.when(core == 0)(lambda: products(mine, other))
    pl.when(core == 1)(lambda: products(other, mine))


def near(z, mine, other):
    size = z.shape[2]
    return call(
        functools.partial(near_kernel, len(mine)),
        "near",
        1 << 29,
        out_shape=jax.ShapeDtypeStruct((size, 2 * mine[0].shape[-2]), jnp.float32),
        in_specs=[VMEM] * (1 + 2 * len(mine)),
        out_specs=VMEM,
    )(z, *mine, *other)


def fold(x):
    high = x.shape[0] // 2
    past = jnp.concatenate([x[:high, 128:], x[high:, 128:]], axis=1)
    return jnp.concatenate([x[:, :128], past], axis=0)


def unfold(x):
    high = x.shape[0] // 3
    past = x[2 * high:]
    past = jnp.concatenate([past[:, :BLK], past[:, BLK:]], axis=0)
    return jnp.concatenate([x[:2 * high], past], axis=1)


def far_kernel(w_ref, *refs):
    mine, out_ref = refs[:-1], refs[-1]
    nt, steps = w_ref.shape[1:3]
    aux = mine[0].shape[1]
    shares = []
    for t in range(nt):
        total = jnp.zeros((aux, w_ref.shape[3]), jnp.float32)
        for half, piece in enumerate(mine):
            for j in range(steps):
                total += lax.dot_general(piece[j], w_ref[half, t, j], NT_DIMS, preferred_element_type=jnp.float32)
        shares.append(total)
    out_ref[...] = fold(jnp.concatenate(shares, axis=0)).astype(out_ref.dtype)


def far(w, mine):
    aux = mine[0].shape[1]
    return call(
        far_kernel,
        "far",
        1 << 29,
        out_shape=jax.ShapeDtypeStruct((w.shape[1] * aux * 3 // 2, 128), jnp.bfloat16),
        in_specs=[VMEM] * (1 + len(mine)),
        out_specs=VMEM,
    )(w, *mine)


def pack_kernel(chips, pairs, *refs):
    backs, aheads = refs[:chips // 2], refs[chips // 2 + 2:chips + 1]
    mine, other = refs[chips // 2][...], refs[chips // 2 + 1][...]
    outs, shares = refs[chips + 1:-1], refs[-1]
    chip = chip_of()
    for step in range(chips // 2):
        shares[lax.rem(chip + chips - step, chips)] = fold(backs[step][...])
    first = lax.rem(lax.axis_index("aux"), 2) == 0
    pieces = [jnp.where(first, mine, other), jnp.where(first, other, mine)]
    shares[lax.rem(chip + chips // 2, chips)] = fold(jnp.concatenate(pieces, axis=1))
    for step in range(1, chips // 2):
        shares[lax.rem(chip + step, chips)] = aheads[step - 1][...].astype(jnp.float32)
    if pairs is None:
        for q in range(chips):
            outs[0][q] = unfold(shares[q]).astype(jnp.bfloat16)
    else:
        pair = lax.axis_index("pair")
        for j, out_ref in enumerate(outs):
            out_ref[...] = shares[lax.bitwise_xor(pair, j)].astype(out_ref.dtype)


def pack(chips, pairs, backs, aheads):
    height, width = backs[0].shape
    folded = (height * 3 // 2, 128)
    if pairs is None:
        out_shape = (jax.ShapeDtypeStruct((chips, height, width), jnp.bfloat16),)
    else:
        out_shape = (jax.ShapeDtypeStruct(folded, jnp.float32),)
        out_shape += (jax.ShapeDtypeStruct(folded, jnp.bfloat16),) * (pairs - 1)
    return call(
        functools.partial(pack_kernel, chips, pairs),
        "pack",
        1 << 28,
        out_shape=out_shape,
        in_specs=[VMEM] * (chips + 1),
        out_specs=(VMEM,) * len(out_shape),
        scratch_shapes=[pltpu.VMEM((chips,) + folded, jnp.float32)],
    )(*backs, *aheads)


def combine_kernel(scale, nt, folded, weight_ref, *refs):
    parts, (chi_ref, sum_ref) = refs[:-2], refs[-2:]
    aux = chi_ref.shape[1]
    if folded:
        total = parts[0][...]
        for part in parts[1:]:
            total += part[...].astype(jnp.float32)
        total = unfold(total * scale)
    else:
        total = parts[0][0].astype(jnp.float32)
        for p in range(1, parts[0].shape[0]):
            total += parts[0][p].astype(jnp.float32)
        total *= scale
    local = jnp.zeros((1, 1), jnp.float32)
    for t in range(nt):
        chi = total[t * aux:(t + 1) * aux]
        chi_ref[t] = chi
        local += weight_ref[:, t:t + 1] * jnp.sum(chi * chi, keepdims=True)
    sum_ref[...] = jnp.broadcast_to(local, sum_ref.shape)


def combine(scale, time_weights, parts, chi_shape, copies):
    return call(
        functools.partial(combine_kernel, scale, chi_shape[0], len(parts) > 1),
        "combine",
        1 << 28,
        out_shape=(
            jax.ShapeDtypeStruct(chi_shape, jnp.float32),
            jax.ShapeDtypeStruct((copies, 128), jnp.float32),
        ),
        in_specs=[VMEM] * (1 + len(parts)),
        out_specs=(VMEM, VMEM),
    )(time_weights[None], *parts)


def close_kernel(norm, tile_ref, sums_ref, chi_hbm, energy_hbm, energy_ref, leaving):
    tile = pltpu.make_async_copy(tile_ref, chi_hbm, leaving.at[0])
    tile.start()
    total = jnp.sum(sums_ref[...], axis=0, keepdims=True)
    energy_ref[...] = -total[:, :1] / norm
    energy = pltpu.make_async_copy(energy_ref, energy_hbm, leaving.at[1])
    energy.start()
    tile.wait()
    energy.wait()


def close(norm, tile, sums):
    return call(
        functools.partial(close_kernel, norm),
        "close",
        1 << 28,
        out_shape=(
            jax.ShapeDtypeStruct(tile.shape, jnp.float32),
            jax.ShapeDtypeStruct((1, 1), jnp.float32),
        ),
        in_specs=[VMEM, VMEM],
        out_specs=(HBM, HBM),
        scratch_shapes=[pltpu.VMEM((1, 1), jnp.float32), pltpu.SemaphoreType.DMA((2,))],
    )(tile, sums)


def per_device(integrals, block_mask, block_atom, green_occ, green_virt, time_weights):
    rows = integrals.shape[0]
    aux_here = integrals.shape[1] // BLK
    pairs, auxes = lax.axis_size("pair"), lax.axis_size("aux")
    chips = auxes // 2
    aux_total = aux_here * auxes
    columns = aux_total // pairs
    nt = green_occ.shape[0]

    def along(shift):
        return [(i, (i + 2 * shift) % auxes) for i in range(auxes)]

    def to_sibling(array):
        return lax.ppermute(array, "aux", [(i, i ^ 1) for i in range(auxes)])

    own = [arrange(integrals, block_mask, second) for second in (False, True)]
    arriving = [lax.ppermute(a, "aux", along(1)) for a in own]
    z, w, greens = transform(block_atom, green_occ, green_virt, rows, own)
    *later, z = lax.optimization_barrier((*own, z))
    arriving[0], z = lax.optimization_barrier((arriving[0], z))
    sibling = [to_sibling(a) for a in later]
    w = complete(w, greens, sibling)
    backs, aheads = [], []
    for step in range(1, chips // 2 + 1):
        held, last = arriving, step == chips // 2
        if not last:
            arriving = [lax.ppermute(a, "aux", along(1)) for a in held]
        if last:
            mine, theirs = both(z, z_sibling, held)
            backs += [mine, to_sibling(theirs)]
            continue
        other = [to_sibling(a) for a in held]
        share = far(w, held)
        ahead = lax.ppermute(share, "aux", along(-step))
        if step == 1:
            backs.append(near(z, own, sibling))
        backs.append(near(z, held, other))
        if step == 1:
            *sibling, _ = lax.optimization_barrier((*sibling, share))
            z_sibling = mirror(greens, sibling)
        *arriving, ahead, backs[-1], backs[-2], z_sibling = lax.optimization_barrier(
            (*arriving, ahead, backs[-1], backs[-2], z_sibling)
        )
        aheads.append(ahead)
    if columns == 2 * aux_here and pairs & (pairs - 1) == 0:
        mine, *sends = pack(chips, pairs, backs, aheads)
        parts = [mine]
        for j in range(pairs - 1, 0, -1):
            parts.append(lax.ppermute(sends[j - 1], "pair", [(i, i ^ j) for i in range(pairs)]))
    else:
        (shares,) = pack(chips, None, backs, aheads)
        shares = shares.transpose(1, 0, 2).reshape(nt * aux_here, pairs, columns).transpose(1, 0, 2)
        parts = [lax.all_to_all(shares, "pair", 0, 0)]
    scale = float((rows * pairs * BLK) ** -0.5)
    tile, sums = combine(scale, time_weights, parts, (nt, aux_here, columns), pairs * auxes)
    everyone = lax.all_to_all(sums, ("pair", "aux"), 0, 0, tiled=True)
    chi, energy = close(float(aux_total * aux_total), tile, everyone)
    return chi, energy[0, 0]


def solution(mesh):
    placed = (P("pair", "aux"), P(None, "aux"), P(), P(), P(), P())
    return jax.shard_map(
        per_device,
        mesh=mesh,
        in_specs=placed,
        out_specs=(P(None, "aux", "pair"), P()),
        check_vma=False,
    )
```

```python
import functools
import jax
import jax.numpy as jnp
from jax import lax
from jax.experimental import pallas as pl
from jax.experimental.pallas import tpu as pltpu
from jax.sharding import PartitionSpec as P

BLK = 64
VMEM = pl.BlockSpec(memory_space=pltpu.VMEM)
SMEM = pl.BlockSpec(memory_space=pltpu.SMEM)
HBM = pl.BlockSpec(memory_space=pltpu.HBM)
NT_DIMS = (((1,), (1,)), ((), ()))


def call(kernel, name, flops, **settings):
    return pl.pallas_call(
        kernel,
        name=name,
        compiler_params=pltpu.CompilerParams(vmem_limit_bytes=40 * 1024 * 1024),
        cost_estimate=pl.CostEstimate(flops=flops, bytes_accessed=1 << 8, transcendentals=0),
        **settings,
    )


def stay(array):
    return pltpu.with_memory_space_constraint(array, pltpu.HBM)


def chip_of():
    return lax.axis_index("aux") // 2


def arrange_kernel(rows, aux, second, x_hbm, mask_hbm, y_ref, x, mask, wide, arrived):
    copies = [
        pltpu.make_async_copy(x_hbm.at[pl.ds(second * (rows // 2), rows // 2)], x, arrived.at[0]),
        pltpu.make_async_copy(mask_hbm, mask, arrived.at[1]),
    ]
    for copy in copies:
        copy.start()
    block = lax.axis_index("pair") * rows // BLK
    low = lax.broadcasted_iota(jnp.int32, (8, 128), 1) < BLK
    for copy in copies:
        copy.wait()
    for i in range(aux // 2):
        tile = x[:, i * 128:(i + 1) * 128].astype(jnp.float32)
        first, last = tile[:8], tile[8:]
        even = jnp.where(low, first, pltpu.roll(last, BLK, 1))
        odd = jnp.where(low, pltpu.roll(first, BLK, 1), last)
        even = jnp.where(mask[block, 2 * i] > 0, even, 0.0)
        odd = jnp.where(mask[block, 2 * i + 1] > 0, odd, 0.0)
        wide[pl.ds(2 * i, 8, stride=aux + 1), :] = even
        wide[pl.ds(2 * i + 1, 8, stride=aux + 1), :] = odd
    for s in range(8):
        lane = s % 2 * 128
        y_ref[s // 2, :, lane:lane + 128] = wide[s * (aux + 1):s * (aux + 1) + aux, :].astype(y_ref.dtype)


def arrange(integrals, block_mask, second):
    rows, width = integrals.shape
    aux = width // BLK
    return call(
        functools.partial(arrange_kernel, rows, aux, second),
        "arrange",
        1 << 28,
        out_shape=jax.ShapeDtypeStruct((4, aux, 256), jnp.bfloat16),
        in_specs=[HBM, HBM],
        out_specs=VMEM,
        scratch_shapes=[
            pltpu.VMEM((rows // 2, width), jnp.bfloat16),
            pltpu.SMEM(block_mask.shape, jnp.int32),
            pltpu.VMEM((8 * (aux + 1), 128), jnp.float32),
            pltpu.SemaphoreType.DMA((2,)),
        ],
    )(stay(integrals), stay(block_mask))


def through(y, first, second):
    steps, aux, wide = y.shape
    y = y[...].reshape(steps * aux, wide)
    half = jnp.dot(y, first, preferred_element_type=jnp.float32).astype(jnp.bfloat16)
    full = lax.dot_general(half, second, NT_DIMS, preferred_element_type=jnp.float32)
    return full.astype(jnp.bfloat16).reshape(steps, aux, wide)


def core_rows(aux, other):
    core = jnp.bitwise_xor(lax.rem(lax.axis_index("aux"), 2), other)
    return pl.ds(pl.multiple_of(core * aux, aux), aux)


def transform_kernel(nt, rows, atom_hbm, occ_hbm, virt_hbm, y1, y2, z_ref, w_ref, green_ref, *scratch):
    atom_ref, occ_ref, virt_ref, arrived = scratch
    aux, wide = y1.shape[1:]
    copies = wide // BLK
    copy = pltpu.make_async_copy(atom_hbm, atom_ref, arrived.at[0])
    copy.start()
    copy.wait()
    atom = atom_ref[lax.axis_index("pair") * rows // BLK]
    fetch = [
        pltpu.make_async_copy(occ_hbm.at[:, atom], occ_ref, arrived.at[0]),
        pltpu.make_async_copy(virt_hbm.at[:, atom], virt_ref, arrived.at[1]),
    ]
    for copy in fetch:
        copy.start()
    for copy in fetch:
        copy.wait()
    same = (
        lax.broadcasted_iota(jnp.int32, (wide, wide), 0) // BLK
        == lax.broadcasted_iota(jnp.int32, (wide, wide), 1) // BLK
    )

    def diagonal(block):
        tall = jnp.concatenate([block.astype(jnp.float32)] * copies, axis=0)
        full = jnp.concatenate([tall] * copies, axis=1)
        return jnp.where(same, full, 0.0).astype(jnp.bfloat16)

    for t in range(nt):
        occ, virt = diagonal(occ_ref[t]), diagonal(virt_ref[t])
        green_ref[t, 0], green_ref[t, 1] = occ, virt
        for half, y in enumerate((y1, y2)):
            z_ref[half, :, t * aux:(t + 1) * aux, :] = through(y, occ, virt)
            w_ref[half, t, :, core_rows(aux, 0), :] = through(y, virt, occ)


def transform(atom, green_occ, green_virt, rows, own):
    nt = green_occ.shape[0]
    steps, aux, wide = own[0].shape
    return call(
        functools.partial(transform_kernel, nt, rows),
        "transform",
        2 << 30,
        out_shape=(
            jax.ShapeDtypeStruct((2, steps, nt * aux, wide), jnp.bfloat16),
            jax.ShapeDtypeStruct((2, nt, steps, 2 * aux, wide), jnp.bfloat16),
            jax.ShapeDtypeStruct((nt, 2, wide, wide), jnp.bfloat16),
        ),
        in_specs=[HBM] * 3 + [VMEM] * 2,
        out_specs=(VMEM,) * 3,
        scratch_shapes=[
            pltpu.SMEM(atom.shape, jnp.int32),
            pltpu.VMEM((nt, BLK, BLK), jnp.bfloat16),
            pltpu.VMEM((nt, BLK, BLK), jnp.bfloat16),
            pltpu.SemaphoreType.DMA((2,)),
        ],
    )(stay(atom), stay(green_occ), stay(green_virt), *own)


def complete_kernel(before_ref, green_ref, y1, y2, w_ref):
    aux = y1.shape[1]
    for t in range(green_ref.shape[0]):
        for half, y in enumerate((y1, y2)):
            w_ref[half, t, :, core_rows(aux, 1), :] = through(y, green_ref[t, 1], green_ref[t, 0])


def complete(w, greens, sibling):
    return call(
        complete_kernel,
        "complete",
        1 << 30,
        out_shape=jax.ShapeDtypeStruct(w.shape, w.dtype),
        in_specs=[VMEM] * 4,
        out_specs=VMEM,
        input_output_aliases={0: 0},
    )(w, greens, *sibling)


def mirror_kernel(green_ref, y1, y2, z_ref):
    aux = y1.shape[1]
    for t in range(green_ref.shape[0]):
        for half, y in enumerate((y1, y2)):
            z_ref[half, :, t * aux:(t + 1) * aux, :] = through(y, green_ref[t, 0], green_ref[t, 1])


def mirror(greens, sibling):
    steps, aux, wide = sibling[0].shape
    return call(
        mirror_kernel,
        "mirror",
        1 << 29,
        out_shape=jax.ShapeDtypeStruct((2, steps, greens.shape[0] * aux, wide), jnp.bfloat16),
        in_specs=[VMEM] * 3,
        out_specs=VMEM,
    )(greens, *sibling)


def last_kernel(z_ref, y1, y2, out_ref):
    total = jnp.zeros(out_ref.shape, jnp.float32)
    for half, y in enumerate((y1, y2)):
        for j in range(y.shape[0]):
            total += lax.dot_general(z_ref[half, j], y[j], NT_DIMS, preferred_element_type=jnp.float32)
    out_ref[...] = total


def last_share(z, pieces):
    return call(
        last_kernel,
        "last_share",
        1 << 29,
        out_shape=jax.ShapeDtypeStruct((z.shape[2], pieces[0].shape[1]), jnp.float32),
        in_specs=[VMEM] * 3,
        out_specs=VMEM,
    )(z, *pieces)


def near_kernel(count, z_ref, *refs):
    mine, other, out_ref = refs[:count], refs[count:2 * count], refs[-1]

    def products(low, high):
        total = jnp.zeros(out_ref.shape, jnp.float32)
        for half, (first, second) in enumerate(zip(low, high)):
            for j in range(z_ref.shape[1]):
                partner = jnp.concatenate([first[j], second[j]], axis=0)
                total += lax.dot_general(z_ref[half, j], partner, NT_DIMS, preferred_element_type=jnp.float32)
        out_ref[...] = total

    core = lax.rem(lax.axis_index("aux"), 2)
    pl.when(core == 0)(lambda: products(mine, other))
    pl.when(core == 1)(lambda: products(other, mine))


def near(z, mine, other):
    size = z.shape[2]
    return call(
        functools.partial(near_kernel, len(mine)),
        "near",
        1 << 29,
        out_shape=jax.ShapeDtypeStruct((size, 2 * mine[0].shape[-2]), jnp.float32),
        in_specs=[VMEM] * (1 + 2 * len(mine)),
        out_specs=VMEM,
    )(z, *mine, *other)


def fold(x):
    high = x.shape[0] // 2
    past = jnp.concatenate([x[:high, 128:], x[high:, 128:]], axis=1)
    return jnp.concatenate([x[:, :128], past], axis=0)


def unfold(x):
    high = x.shape[0] // 3
    past = x[2 * high:]
    past = jnp.concatenate([past[:, :BLK], past[:, BLK:]], axis=0)
    return jnp.concatenate([x[:2 * high], past], axis=1)


def far_kernel(w_ref, *refs):
    mine, out_ref = refs[:-1], refs[-1]
    nt, steps = w_ref.shape[1:3]
    aux = mine[0].shape[1]
    shares = []
    for t in range(nt):
        total = jnp.zeros((aux, w_ref.shape[3]), jnp.float32)
        for half, piece in enumerate(mine):
            for j in range(steps):
                total += lax.dot_general(piece[j], w_ref[half, t, j], NT_DIMS, preferred_element_type=jnp.float32)
        shares.append(total)
    out_ref[...] = fold(jnp.concatenate(shares, axis=0)).astype(out_ref.dtype)


def far(w, mine):
    aux = mine[0].shape[1]
    return call(
        far_kernel,
        "far",
        1 << 29,
        out_shape=jax.ShapeDtypeStruct((w.shape[1] * aux * 3 // 2, 128), jnp.bfloat16),
        in_specs=[VMEM] * (1 + len(mine)),
        out_specs=VMEM,
    )(w, *mine)


def pack_kernel(chips, pairs, *refs):
    backs, aheads = refs[:chips // 2], refs[chips // 2 + 2:chips + 1]
    mine, other = refs[chips // 2][...], refs[chips // 2 + 1][...]
    outs, shares = refs[chips + 1:-1], refs[-1]
    chip = chip_of()
    for step in range(chips // 2):
        shares[lax.rem(chip + chips - step, chips)] = fold(backs[step][...])
    first = lax.rem(lax.axis_index("aux"), 2) == 0
    pieces = [jnp.where(first, mine, other), jnp.where(first, other, mine)]
    shares[lax.rem(chip + chips // 2, chips)] = fold(jnp.concatenate(pieces, axis=1))
    for step in range(1, chips // 2):
        shares[lax.rem(chip + step, chips)] = aheads[step - 1][...].astype(jnp.float32)
    if pairs is None:
        for q in range(chips):
            outs[0][q] = unfold(shares[q]).astype(jnp.bfloat16)
    else:
        pair = lax.axis_index("pair")
        for j, out_ref in enumerate(outs):
            out_ref[...] = shares[lax.bitwise_xor(pair, j)].astype(out_ref.dtype)


def pack(chips, pairs, backs, aheads):
    height, width = backs[0].shape
    folded = (height * 3 // 2, 128)
    if pairs is None:
        out_shape = (jax.ShapeDtypeStruct((chips, height, width), jnp.bfloat16),)
    else:
        out_shape = (jax.ShapeDtypeStruct(folded, jnp.float32),)
        out_shape += (jax.ShapeDtypeStruct(folded, jnp.bfloat16),) * (pairs - 1)
    return call(
        functools.partial(pack_kernel, chips, pairs),
        "pack",
        1 << 28,
        out_shape=out_shape,
        in_specs=[VMEM] * (chips + 1),
        out_specs=(VMEM,) * len(out_shape),
        scratch_shapes=[pltpu.VMEM((chips,) + folded, jnp.float32)],
    )(*backs, *aheads)


def combine_kernel(scale, nt, folded, weight_ref, *refs):
    parts, (chi_ref, sum_ref) = refs[:-2], refs[-2:]
    aux = chi_ref.shape[1]
    if folded:
        total = parts[0][...]
        for part in parts[1:]:
            total += part[...].astype(jnp.float32)
        total = unfold(total * scale)
    else:
        total = parts[0][0].astype(jnp.float32)
        for p in range(1, parts[0].shape[0]):
            total += parts[0][p].astype(jnp.float32)
        total *= scale
    local = jnp.zeros((1, 1), jnp.float32)
    for t in range(nt):
        chi = total[t * aux:(t + 1) * aux]
        chi_ref[t] = chi
        local += weight_ref[:, t:t + 1] * jnp.sum(chi * chi, keepdims=True)
    sum_ref[...] = jnp.broadcast_to(local, sum_ref.shape)


def combine(scale, time_weights, parts, chi_shape, copies):
    return call(
        functools.partial(combine_kernel, scale, chi_shape[0], len(parts) > 1),
        "combine",
        1 << 28,
        out_shape=(
            jax.ShapeDtypeStruct(chi_shape, jnp.float32),
            jax.ShapeDtypeStruct((copies, 128), jnp.float32),
        ),
        in_specs=[VMEM] * (1 + len(parts)),
        out_specs=(VMEM, VMEM),
    )(time_weights[None], *parts)


def close_kernel(norm, tile_ref, sums_ref, chi_hbm, energy_hbm, energy_ref, leaving):
    tile = pltpu.make_async_copy(tile_ref, chi_hbm, leaving.at[0])
    tile.start()
    total = jnp.sum(sums_ref[...], axis=0, keepdims=True)
    energy_ref[...] = -total[:, :1] / norm
    energy = pltpu.make_async_copy(energy_ref, energy_hbm, leaving.at[1])
    energy.start()
    tile.wait()
    energy.wait()


def close(norm, tile, sums):
    return call(
        functools.partial(close_kernel, norm),
        "close",
        1 << 28,
        out_shape=(
            jax.ShapeDtypeStruct(tile.shape, jnp.float32),
            jax.ShapeDtypeStruct((1, 1), jnp.float32),
        ),
        in_specs=[VMEM, VMEM],
        out_specs=(HBM, HBM),
        scratch_shapes=[pltpu.VMEM((1, 1), jnp.float32), pltpu.SemaphoreType.DMA((2,))],
    )(tile, sums)


def per_device(integrals, block_mask, block_atom, green_occ, green_virt, time_weights):
    rows = integrals.shape[0]
    aux_here = integrals.shape[1] // BLK
    pairs, auxes = lax.axis_size("pair"), lax.axis_size("aux")
    chips = auxes // 2
    aux_total = aux_here * auxes
    columns = aux_total // pairs
    nt = green_occ.shape[0]

    def along(shift):
        return [(i, (i + 2 * shift) % auxes) for i in range(auxes)]

    def to_sibling(array):
        return lax.ppermute(array, "aux", [(i, i ^ 1) for i in range(auxes)])

    own = [arrange(integrals, block_mask, second) for second in (False, True)]
    arriving = [lax.ppermute(a, "aux", along(1)) for a in own]
    z, w, greens = transform(block_atom, green_occ, green_virt, rows, own)
    *later, z = lax.optimization_barrier((*own, z))
    arriving[0], z = lax.optimization_barrier((arriving[0], z))
    sibling = [to_sibling(a) for a in later]
    w = complete(w, greens, sibling)
    backs, aheads = [], []
    for step in range(1, chips // 2 + 1):
        held, last = arriving, step == chips // 2
        if not last:
            arriving = [lax.ppermute(a, "aux", along(1)) for a in held]
        if last:
            theirs = last_share(z_sibling, held)
            *pieces, theirs = lax.optimization_barrier((*held, theirs))
            backs += [last_share(z, pieces), to_sibling(theirs)]
            continue
        other = [to_sibling(a) for a in held]
        share = far(w, held)
        ahead = lax.ppermute(share, "aux", along(-step))
        if step == 1:
            backs.append(near(z, own, sibling))
        backs.append(near(z, held, other))
        if step == 1:
            *sibling, _ = lax.optimization_barrier((*sibling, share))
            z_sibling = mirror(greens, sibling)
        *arriving, ahead, backs[-1], backs[-2], z_sibling = lax.optimization_barrier(
            (*arriving, ahead, backs[-1], backs[-2], z_sibling)
        )
        aheads.append(ahead)
    if columns == 2 * aux_here and pairs & (pairs - 1) == 0:
        mine, *sends = pack(chips, pairs, backs, aheads)
        parts = [mine]
        for j in range(pairs - 1, 0, -1):
            parts.append(lax.ppermute(sends[j - 1], "pair", [(i, i ^ j) for i in range(pairs)]))
    else:
        (shares,) = pack(chips, None, backs, aheads)
        shares = shares.transpose(1, 0, 2).reshape(nt * aux_here, pairs, columns).transpose(1, 0, 2)
        parts = [lax.all_to_all(shares, "pair", 0, 0)]
    scale = float((rows * pairs * BLK) ** -0.5)
    tile, sums = combine(scale, time_weights, parts, (nt, aux_here, columns), pairs * auxes)
    everyone = lax.all_to_all(sums, ("pair", "aux"), 0, 0, tiled=True)
    chi, energy = close(float(aux_total * aux_total), tile, everyone)
    return chi, energy[0, 0]


def solution(mesh):
    placed = (P("pair", "aux"), P(None, "aux"), P(), P(), P(), P())
    return jax.shard_map(
        per_device,
        mesh=mesh,
        in_specs=placed,
        out_specs=(P(None, "aux", "pair"), P()),
        check_vma=False,
    )
```

```python
import functools
import jax
import jax.numpy as jnp
from jax import lax
from jax.experimental import pallas as pl
from jax.experimental.pallas import tpu as pltpu
from jax.sharding import PartitionSpec as P

BLK = 64
VMEM = pl.BlockSpec(memory_space=pltpu.VMEM)
SMEM = pl.BlockSpec(memory_space=pltpu.SMEM)
HBM = pl.BlockSpec(memory_space=pltpu.HBM)
NT_DIMS = (((1,), (1,)), ((), ()))


def call(kernel, name, flops, **settings):
    return pl.pallas_call(
        kernel,
        name=name,
        compiler_params=pltpu.CompilerParams(vmem_limit_bytes=40 * 1024 * 1024),
        cost_estimate=pl.CostEstimate(flops=flops, bytes_accessed=1 << 8, transcendentals=0),
        **settings,
    )


def stay(array):
    return pltpu.with_memory_space_constraint(array, pltpu.HBM)


def chip_of():
    return lax.axis_index("aux") // 2


def arrange_kernel(rows, aux, second, x_hbm, mask_hbm, y_ref, x, mask, wide, arrived):
    copies = [
        pltpu.make_async_copy(x_hbm.at[pl.ds(second * (rows // 2), rows // 2)], x, arrived.at[0]),
        pltpu.make_async_copy(mask_hbm, mask, arrived.at[1]),
    ]
    for copy in copies:
        copy.start()
    block = lax.axis_index("pair") * rows // BLK
    low = lax.broadcasted_iota(jnp.int32, (8, 128), 1) < BLK
    for copy in copies:
        copy.wait()
    for i in range(aux // 2):
        tile = x[:, i * 128:(i + 1) * 128].astype(jnp.float32)
        first, last = tile[:8], tile[8:]
        even = jnp.where(low, first, pltpu.roll(last, BLK, 1))
        odd = jnp.where(low, pltpu.roll(first, BLK, 1), last)
        even = jnp.where(mask[block, 2 * i] > 0, even, 0.0)
        odd = jnp.where(mask[block, 2 * i + 1] > 0, odd, 0.0)
        wide[pl.ds(2 * i, 8, stride=aux + 1), :] = even
        wide[pl.ds(2 * i + 1, 8, stride=aux + 1), :] = odd
    for s in range(8):
        lane = s % 2 * 128
        y_ref[s // 2, :, lane:lane + 128] = wide[s * (aux + 1):s * (aux + 1) + aux, :].astype(y_ref.dtype)


def arrange(integrals, block_mask, second):
    rows, width = integrals.shape
    aux = width // BLK
    return call(
        functools.partial(arrange_kernel, rows, aux, second),
        "arrange",
        1 << 28,
        out_shape=jax.ShapeDtypeStruct((4, aux, 256), jnp.bfloat16),
        in_specs=[HBM, HBM],
        out_specs=VMEM,
        scratch_shapes=[
            pltpu.VMEM((rows // 2, width), jnp.bfloat16),
            pltpu.SMEM(block_mask.shape, jnp.int32),
            pltpu.VMEM((8 * (aux + 1), 128), jnp.float32),
            pltpu.SemaphoreType.DMA((2,)),
        ],
    )(stay(integrals), stay(block_mask))


def through(y, first, second):
    steps, aux, wide = y.shape
    y = y[...].reshape(steps * aux, wide)
    half = jnp.dot(y, first, preferred_element_type=jnp.float32).astype(jnp.bfloat16)
    full = lax.dot_general(half, second, NT_DIMS, preferred_element_type=jnp.float32)
    return full.astype(jnp.bfloat16).reshape(steps, aux, wide)


def core_rows(aux, other):
    core = jnp.bitwise_xor(lax.rem(lax.axis_index("aux"), 2), other)
    return pl.ds(pl.multiple_of(core * aux, aux), aux)


def transform_kernel(nt, rows, atom_hbm, occ_hbm, virt_hbm, y1, y2, z_ref, w_ref, green_ref, *scratch):
    atom_ref, occ_ref, virt_ref, arrived = scratch
    aux, wide = y1.shape[1:]
    copies = wide // BLK
    copy = pltpu.make_async_copy(atom_hbm, atom_ref, arrived.at[0])
    copy.start()
    copy.wait()
    atom = atom_ref[lax.axis_index("pair") * rows // BLK]
    fetch = [
        pltpu.make_async_copy(occ_hbm.at[:, atom], occ_ref, arrived.at[0]),
        pltpu.make_async_copy(virt_hbm.at[:, atom], virt_ref, arrived.at[1]),
    ]
    for copy in fetch:
        copy.start()
    for copy in fetch:
        copy.wait()
    same = (
        lax.broadcasted_iota(jnp.int32, (wide, wide), 0) // BLK
        == lax.broadcasted_iota(jnp.int32, (wide, wide), 1) // BLK
    )

    def diagonal(block):
        tall = jnp.concatenate([block.astype(jnp.float32)] * copies, axis=0)
        full = jnp.concatenate([tall] * copies, axis=1)
        return jnp.where(same, full, 0.0).astype(jnp.bfloat16)

    for t in range(nt):
        occ, virt = diagonal(occ_ref[t]), diagonal(virt_ref[t])
        green_ref[t, 0], green_ref[t, 1] = occ, virt
        for half, y in enumerate((y1, y2)):
            z_ref[half, :, t * aux:(t + 1) * aux, :] = through(y, occ, virt)
            w_ref[half, t, :, core_rows(aux, 0), :] = through(y, virt, occ)


def transform(atom, green_occ, green_virt, rows, own):
    nt = green_occ.shape[0]
    steps, aux, wide = own[0].shape
    return call(
        functools.partial(transform_kernel, nt, rows),
        "transform",
        2 << 30,
        out_shape=(
            jax.ShapeDtypeStruct((2, steps, nt * aux, wide), jnp.bfloat16),
            jax.ShapeDtypeStruct((2, nt, steps, 2 * aux, wide), jnp.bfloat16),
            jax.ShapeDtypeStruct((nt, 2, wide, wide), jnp.bfloat16),
        ),
        in_specs=[HBM] * 3 + [VMEM] * 2,
        out_specs=(VMEM,) * 3,
        scratch_shapes=[
            pltpu.SMEM(atom.shape, jnp.int32),
            pltpu.VMEM((nt, BLK, BLK), jnp.bfloat16),
            pltpu.VMEM((nt, BLK, BLK), jnp.bfloat16),
            pltpu.SemaphoreType.DMA((2,)),
        ],
    )(stay(atom), stay(green_occ), stay(green_virt), *own)


def complete_kernel(before_ref, green_ref, y1, y2, w_ref):
    aux = y1.shape[1]
    for t in range(green_ref.shape[0]):
        for half, y in enumerate((y1, y2)):
            w_ref[half, t, :, core_rows(aux, 1), :] = through(y, green_ref[t, 1], green_ref[t, 0])


def complete(w, greens, sibling):
    return call(
        complete_kernel,
        "complete",
        1 << 30,
        out_shape=jax.ShapeDtypeStruct(w.shape, w.dtype),
        in_specs=[VMEM] * 4,
        out_specs=VMEM,
        input_output_aliases={0: 0},
    )(w, greens, *sibling)


def mirror_kernel(green_ref, y1, y2, z_ref):
    aux = y1.shape[1]
    for t in range(green_ref.shape[0]):
        for half, y in enumerate((y1, y2)):
            z_ref[half, :, t * aux:(t + 1) * aux, :] = through(y, green_ref[t, 0], green_ref[t, 1])


def mirror(greens, sibling):
    steps, aux, wide = sibling[0].shape
    return call(
        mirror_kernel,
        "mirror",
        1 << 29,
        out_shape=jax.ShapeDtypeStruct((2, steps, greens.shape[0] * aux, wide), jnp.bfloat16),
        in_specs=[VMEM] * 3,
        out_specs=VMEM,
    )(greens, *sibling)


def last_kernel(z_ref, y1, y2, out_ref):
    total = jnp.zeros(out_ref.shape, jnp.float32)
    for half, y in enumerate((y1, y2)):
        for j in range(y.shape[0]):
            total += lax.dot_general(z_ref[half, j], y[j], NT_DIMS, preferred_element_type=jnp.float32)
    out_ref[...] = total


def last_share(z, pieces):
    return call(
        last_kernel,
        "last_share",
        1 << 29,
        out_shape=jax.ShapeDtypeStruct((z.shape[2], pieces[0].shape[1]), jnp.float32),
        in_specs=[VMEM] * 3,
        out_specs=VMEM,
    )(z, *pieces)


def near_kernel(count, z_ref, *refs):
    mine, other, out_ref = refs[:count], refs[count:2 * count], refs[-1]

    def products(low, high):
        total = jnp.zeros(out_ref.shape, jnp.float32)
        for half, (first, second) in enumerate(zip(low, high)):
            for j in range(z_ref.shape[1]):
                partner = jnp.concatenate([first[j], second[j]], axis=0)
                total += lax.dot_general(z_ref[half, j], partner, NT_DIMS, preferred_element_type=jnp.float32)
        out_ref[...] = total

    core = lax.rem(lax.axis_index("aux"), 2)
    pl.when(core == 0)(lambda: products(mine, other))
    pl.when(core == 1)(lambda: products(other, mine))


def near(z, mine, other):
    size = z.shape[2]
    return call(
        functools.partial(near_kernel, len(mine)),
        "near",
        1 << 29,
        out_shape=jax.ShapeDtypeStruct((size, 2 * mine[0].shape[-2]), jnp.float32),
        in_specs=[VMEM] * (1 + 2 * len(mine)),
        out_specs=VMEM,
    )(z, *mine, *other)


def fold(x):
    high = x.shape[0] // 2
    past = jnp.concatenate([x[:high, 128:], x[high:, 128:]], axis=1)
    return jnp.concatenate([x[:, :128], past], axis=0)


def unfold(x):
    high = x.shape[0] // 3
    past = x[2 * high:]
    past = jnp.concatenate([past[:, :BLK], past[:, BLK:]], axis=0)
    return jnp.concatenate([x[:2 * high], past], axis=1)


def far_kernel(w_ref, *refs):
    mine, out_ref = refs[:-1], refs[-1]
    nt, steps = w_ref.shape[1:3]
    aux = mine[0].shape[1]
    shares = []
    for t in range(nt):
        total = jnp.zeros((aux, w_ref.shape[3]), jnp.float32)
        for half, piece in enumerate(mine):
            for j in range(steps):
                total += lax.dot_general(piece[j], w_ref[half, t, j], NT_DIMS, preferred_element_type=jnp.float32)
        shares.append(total)
    out_ref[...] = fold(jnp.concatenate(shares, axis=0)).astype(out_ref.dtype)


def far(w, mine):
    aux = mine[0].shape[1]
    return call(
        far_kernel,
        "far",
        1 << 29,
        out_shape=jax.ShapeDtypeStruct((w.shape[1] * aux * 3 // 2, 128), jnp.bfloat16),
        in_specs=[VMEM] * (1 + len(mine)),
        out_specs=VMEM,
    )(w, *mine)


def pack_kernel(chips, pairs, *refs):
    backs, aheads = refs[:chips // 2], refs[chips // 2 + 2:chips + 1]
    mine, other = refs[chips // 2][...], refs[chips // 2 + 1][...]
    outs, shares = refs[chips + 1:-1], refs[-1]
    chip = chip_of()
    for step in range(chips // 2):
        shares[lax.rem(chip + chips - step, chips)] = fold(backs[step][...])
    first = lax.rem(lax.axis_index("aux"), 2) == 0
    pieces = [jnp.where(first, mine, other), jnp.where(first, other, mine)]
    shares[lax.rem(chip + chips // 2, chips)] = fold(jnp.concatenate(pieces, axis=1))
    for step in range(1, chips // 2):
        shares[lax.rem(chip + step, chips)] = aheads[step - 1][...].astype(jnp.float32)
    if pairs is None:
        for q in range(chips):
            outs[0][q] = unfold(shares[q]).astype(jnp.bfloat16)
    else:
        pair = lax.axis_index("pair")
        for j, out_ref in enumerate(outs):
            out_ref[...] = shares[lax.bitwise_xor(pair, j)].astype(out_ref.dtype)


def pack(chips, pairs, backs, aheads):
    height, width = backs[0].shape
    folded = (height * 3 // 2, 128)
    if pairs is None:
        out_shape = (jax.ShapeDtypeStruct((chips, height, width), jnp.bfloat16),)
    else:
        out_shape = (jax.ShapeDtypeStruct(folded, jnp.float32),)
        out_shape += (jax.ShapeDtypeStruct(folded, jnp.bfloat16),) * (pairs - 1)
    return call(
        functools.partial(pack_kernel, chips, pairs),
        "pack",
        1 << 28,
        out_shape=out_shape,
        in_specs=[VMEM] * (chips + 1),
        out_specs=(VMEM,) * len(out_shape),
        scratch_shapes=[pltpu.VMEM((chips,) + folded, jnp.float32)],
    )(*backs, *aheads)


def combine_kernel(scale, nt, folded, weight_ref, *refs):
    parts, (chi_ref, sum_ref) = refs[:-2], refs[-2:]
    aux = chi_ref.shape[1]
    if folded:
        total = parts[0][...]
        for part in parts[1:]:
            total += part[...].astype(jnp.float32)
        total = unfold(total * scale)
    else:
        total = parts[0][0].astype(jnp.float32)
        for p in range(1, parts[0].shape[0]):
            total += parts[0][p].astype(jnp.float32)
        total *= scale
    local = jnp.zeros((1, 1), jnp.float32)
    for t in range(nt):
        chi = total[t * aux:(t + 1) * aux]
        chi_ref[t] = chi
        local += weight_ref[:, t:t + 1] * jnp.sum(chi * chi, keepdims=True)
    sum_ref[...] = jnp.broadcast_to(local, sum_ref.shape)


def combine(scale, time_weights, parts, chi_shape, copies):
    return call(
        functools.partial(combine_kernel, scale, chi_shape[0], len(parts) > 1),
        "combine",
        1 << 28,
        out_shape=(
            jax.ShapeDtypeStruct(chi_shape, jnp.float32),
            jax.ShapeDtypeStruct((copies, 128), jnp.float32),
        ),
        in_specs=[VMEM] * (1 + len(parts)),
        out_specs=(VMEM, VMEM),
    )(time_weights[None], *parts)


def close_kernel(norm, tile_ref, sums_ref, chi_hbm, energy_hbm, energy_ref, leaving):
    tile = pltpu.make_async_copy(tile_ref, chi_hbm, leaving.at[0])
    tile.start()
    total = jnp.sum(sums_ref[...], axis=0, keepdims=True)
    energy_ref[...] = -total[:, :1] / norm
    energy = pltpu.make_async_copy(energy_ref, energy_hbm, leaving.at[1])
    energy.start()
    tile.wait()
    energy.wait()


def close(norm, tile, sums):
    return call(
        functools.partial(close_kernel, norm),
        "close",
        1 << 28,
        out_shape=(
            jax.ShapeDtypeStruct(tile.shape, jnp.float32),
            jax.ShapeDtypeStruct((1, 1), jnp.float32),
        ),
        in_specs=[VMEM, VMEM],
        out_specs=(HBM, HBM),
        scratch_shapes=[pltpu.VMEM((1, 1), jnp.float32), pltpu.SemaphoreType.DMA((2,))],
    )(tile, sums)


def per_device(integrals, block_mask, block_atom, green_occ, green_virt, time_weights):
    rows = integrals.shape[0]
    aux_here = integrals.shape[1] // BLK
    pairs, auxes = lax.axis_size("pair"), lax.axis_size("aux")
    chips = auxes // 2
    aux_total = aux_here * auxes
    columns = aux_total // pairs
    nt = green_occ.shape[0]

    def along(shift):
        return [(i, (i + 2 * shift) % auxes) for i in range(auxes)]

    def to_sibling(array):
        return lax.ppermute(array, "aux", [(i, i ^ 1) for i in range(auxes)])

    own = [arrange(integrals, block_mask, second) for second in (False, True)]
    arriving = [lax.ppermute(a, "aux", along(1)) for a in own]
    z, w, greens = transform(block_atom, green_occ, green_virt, rows, own)
    *later, z = lax.optimization_barrier((*own, z))
    arriving[0], z = lax.optimization_barrier((arriving[0], z))
    sibling = [to_sibling(a) for a in later]
    w = complete(w, greens, sibling)
    backs, aheads = [], []
    for step in range(1, chips // 2 + 1):
        held, last = arriving, step == chips // 2
        if not last:
            arriving = [lax.ppermute(a, "aux", along(1)) for a in held]
        if last:
            theirs = last_share(z_sibling, held)
            *pieces, theirs = lax.optimization_barrier((*held, theirs))
            backs += [last_share(z, pieces), to_sibling(theirs)]
            continue
        other = [to_sibling(a) for a in held]
        share = far(w, held)
        ahead = lax.ppermute(share, "aux", along(-step))
        if step == 1:
            backs.append(near(z, own, sibling))
        backs.append(near(z, held, other))
        if step == 1:
            *sibling, _ = lax.optimization_barrier((*sibling, share))
            z_sibling = mirror(greens, sibling)
        *arriving, ahead, backs[-1], backs[-2], z_sibling = lax.optimization_barrier(
            (*arriving, ahead, backs[-1], backs[-2], z_sibling)
        )
        aheads.append(ahead)
    if columns == 2 * aux_here and pairs & (pairs - 1) == 0:
        mine, *sends = pack(chips, pairs, backs, aheads)
        parts = [mine]
        half = pairs // 2
        for j in [half, *range(pairs - 1, half, -1), *range(half - 1, 0, -1)]:
            parts.append(lax.ppermute(sends[j - 1], "pair", [(i, i ^ j) for i in range(pairs)]))
    else:
        (shares,) = pack(chips, None, backs, aheads)
        shares = shares.transpose(1, 0, 2).reshape(nt * aux_here, pairs, columns).transpose(1, 0, 2)
        parts = [lax.all_to_all(shares, "pair", 0, 0)]
    scale = float((rows * pairs * BLK) ** -0.5)
    tile, sums = combine(scale, time_weights, parts, (nt, aux_here, columns), pairs * auxes)
    everyone = lax.all_to_all(sums, ("pair", "aux"), 0, 0, tiled=True)
    chi, energy = close(float(aux_total * aux_total), tile, everyone)
    return chi, energy[0, 0]


def solution(mesh):
    placed = (P("pair", "aux"), P(None, "aux"), P(), P(), P(), P())
    return jax.shard_map(
        per_device,
        mesh=mesh,
        in_specs=placed,
        out_specs=(P(None, "aux", "pair"), P()),
        check_vma=False,
    )
```
